32 devices in a mesh: groups: 2 (over x), clus: 8 (over z, y), blk: 2 (over core).
Axes of the slice: x: 2, y: 2, z: 4, core: 2. Of those that a mesh axis runs over, the one named last changes fastest.
Arguments:
- embeddings: bfloat16 [32768, 1024], P(('groups', 'clus', 'blk')), parts along dimension 0, may hold values from -120 to 120
- cluster_ids: int32 [32, 1024], P(('groups', 'clus', 'blk')), parts along dimension 0, may hold values from 0 to 15, as said below
Outputs:
- best_match: float32 [32, 2048], P(('groups', 'clus'), 'blk'), parts along dimension 0
The draws below stay inside these ranges and needn't reach their ends.
There are 2 independent parts, one for each index of `groups`. The reference program is written for one: setup_inputs(seed, part) draws one part's arguments, and reference() takes and returns one part's arrays. A program takes and returns all parts, laid end to end along the dimension named above; each array names one. Nothing has to cross between parts.
Inputs may be any that keep to these rules, and one draw needn't show every extreme that they name: `cluster_ids`: each loader shard holds at most 128 rows of any one cluster, and in every draw some cluster has exactly 128 rows on every loader shard.
All inputs are finite; a program needn't handle non-finite values.
Results may differ from the reference program's by a relative error of at most 0.0005.
Values may be sent and summed in bfloat16 or wider, within the bound.
No kernel may reach another device: no remote copies, remote signals or barrier semaphores. Data moves between devices by JAX's collectives and lax.ppermute only.
A program may use at most 64 MiB of HBM per device.

```python
import math
import jax
import jax.numpy as jnp
from jax import lax

D = 1024
LOAD_DEV = 1024
CLUSTERS = 16
LOADERS = 16
PAIR_MAX = 128
BLOCK = 1024
CAP = 2048
N_BLK = 2


def cluster_layout(key):
    anchor = jax.random.fold_in(key, 901)
    total = CLUSTERS * PAIR_MAX
    heat = jax.random.randint(jax.random.fold_in(anchor, 1), (CLUSTERS,), 0, 4)
    hottest = jax.random.randint(jax.random.fold_in(anchor, 2), (), 0, CLUSTERS)
    heat = jnp.where(jnp.arange(CLUSTERS) == hottest, 8, heat)
    cells = jnp.arange(total, dtype=jnp.int32)
    cell_heat = heat[cells // PAIR_MAX]

    def per_loader(loader_key):
        ranking = jax.random.permutation(jax.random.fold_in(loader_key, 1), total)
        scores = (cell_heat * (total // 2) + ranking) * total + cells
        top_scores, chosen = lax.top_k(scores, LOAD_DEV)
        shuffle = jax.random.permutation(jax.random.fold_in(loader_key, 2), LOAD_DEV)
        return chosen[shuffle].astype(jnp.int32)
    loader_keys = jax.random.split(jax.random.fold_in(anchor, 3), LOADERS)
    return jax.vmap(per_loader)(loader_keys)


def draw_cluster_ids(key, part):
    cells = cluster_layout(key)
    return (cells // PAIR_MAX).astype(jnp.int32)


def draw_embeddings(key, part):
    cells = cluster_layout(key)
    key = jax.random.fold_in(key, 7)
    cluster = (cells // PAIR_MAX).reshape(-1)
    count_rows = LOADERS * LOAD_DEV
    centers = jax.random.normal(jax.random.fold_in(key, 1), (CLUSTERS, D), jnp.float32)
    shared_tag = jax.random.randint(jax.random.fold_in(key, 2), (count_rows,), 0, 4 * LOAD_DEV)
    noise_key = jax.random.fold_in(key, 3)

    def shared_row(tag):
        return jax.random.normal(jax.random.fold_in(noise_key, tag), (D,), jnp.float32)
    shared = jax.vmap(shared_row)(cluster * (4 * LOAD_DEV) + shared_tag)
    fresh = jax.random.normal(jax.random.fold_in(key, 4), (count_rows, D), jnp.float32)
    scale = jnp.exp(jax.random.uniform(jax.random.fold_in(key, 5), (count_rows, 1), jnp.float32, 0.0, math.log(10.0)))
    values = (centers[cluster] + 0.9 * (shared + 0.3 * fresh)) * scale
    return jnp.clip(values, -120.0, 120.0).astype(jnp.bfloat16)


def setup_inputs(seed: int = 0, part: int = 0) -> dict:
    key_of = jax.random.split(jax.random.key(seed), 3)
    part_keys = jax.random.split(jax.random.fold_in(key_of[2], part), 3)
    embeddings = draw_embeddings(jax.random.fold_in(jax.random.fold_in(key_of[2], part), 71), part)
    cluster_ids = draw_cluster_ids(jax.random.fold_in(jax.random.fold_in(key_of[2], part), 71), part)
    return {"embeddings": embeddings, "cluster_ids": cluster_ids}


def reference(embeddings, cluster_ids):
    values = embeddings.astype(jnp.float32)
    unit = (values * lax.rsqrt(lax.optimization_barrier(jnp.sum(values * values, axis=1, keepdims=True)) + 1e-06)).astype(jnp.bfloat16)
    loaders = cluster_ids.shape[0]
    onehot = (cluster_ids[:, :, None] == jnp.arange(CLUSTERS, dtype=jnp.int32)[None, None, :]).astype(jnp.int32)
    before = jnp.cumsum(onehot, axis=1) - onehot
    slot = lax.optimization_barrier(jnp.sum(before * onehot, axis=2)).astype(jnp.int32)
    loader = jnp.arange(loaders, dtype=jnp.int32)[:, None]
    position = loader % N_BLK * BLOCK + loader // N_BLK * PAIR_MAX + slot
    flat = (cluster_ids * CAP + position).reshape(-1).astype(jnp.int32)
    placed = jnp.zeros((CLUSTERS * CAP, D), jnp.bfloat16).at[flat].set(unit).reshape(CLUSTERS, CAP, D)
    filled = jnp.zeros((CLUSTERS * CAP,), jnp.bool_).at[flat].set(True).reshape(CLUSTERS, CAP)
    later = jnp.arange(CAP, dtype=jnp.int32)[:, None] > jnp.arange(CAP, dtype=jnp.int32)[None, :]

    def per_cluster(parts):
        matrix, usable = parts
        similarity = jnp.dot(matrix, matrix.T, preferred_element_type=jnp.float32)
        allowed = later & usable[None, :]
        largest = lax.optimization_barrier(jnp.max(jnp.where(allowed, similarity, jnp.float32(-1.0)), axis=1))
        return jnp.where(usable, largest, jnp.float32(0.0))
    return lax.map(per_cluster, (placed, filled))
```

```python
import functools

import jax
import jax.numpy as jnp
from jax import lax
from jax.experimental import pallas as pl
from jax.experimental.pallas import tpu as pltpu
from jax.sharding import PartitionSpec as P

CLUS_DEV = 2
LANES = 128
MARK = 2.0
BF = jnp.bfloat16
F32 = jnp.float32


def iota(shape, dim):
    return lax.broadcasted_iota(jnp.int32, shape, dim)


def matmul(a, b, contract):
    return lax.dot_general(a, b, (contract, ((), ())), preferred_element_type=F32)


def targets(ids, clusters, per_source):
    groups = ids.shape[1] // LANES
    parts = [ids[:, g * LANES : (g + 1) * LANES] for g in range(groups)]
    hot = jnp.concatenate(
        [(iota((clusters, LANES), 0) == part).astype(F32) for part in parts], axis=0
    )
    stacked = groups * clusters
    earlier = (iota((LANES, LANES), 0) < iota((LANES, LANES), 1)).astype(F32).astype(BF)
    within = matmul(hot.astype(BF), earlier, ((1,), (0,)))
    totals = jnp.broadcast_to(jnp.sum(hot, axis=1, keepdims=True), (stacked, LANES))
    a, b = iota((stacked, stacked), 0), iota((stacked, stacked), 1)
    chunks_before = ((a % clusters == b % clusters) & (b < a)).astype(F32).astype(BF)
    before = within + matmul(chunks_before, totals.astype(BF), ((1,), (0,)))
    picked = hot * before
    out = [
        jnp.sum(picked[g * clusters : (g + 1) * clusters], axis=0, keepdims=True).astype(jnp.int32)
        + parts[g] * per_source
        for g in range(groups)
    ]
    return jnp.concatenate(out, axis=1)


def pack_block(unit, tgt, dest, width):
    hit = (tgt - dest * width) == iota((width, tgt.shape[1]), 0)
    hot = hit.astype(F32)
    rows = matmul(hot.astype(BF), unit, ((1,), (0,)))
    empty = jnp.max(hot, axis=1, keepdims=True) < 0.5
    head = jnp.where(empty, F32(MARK), rows[:, :LANES])
    return head.astype(BF), rows[:, LANES:].astype(BF)


def store_blocks(unit, tgt, steps, width, outs):
    me = lax.axis_index("clus")
    for step, out in zip(steps, outs):
        head, tail = pack_block(unit, tgt, me ^ step, width)
        out[:, :LANES] = head
        out[:, LANES:] = tail


def pack_first(steps, clusters, per_source, emb, ids, unit, tgt, *outs):
    values = emb[...].astype(F32)
    scale = lax.rsqrt(jnp.sum(values * values, axis=1, keepdims=True) + 1e-6)
    unit[...] = (values * scale).astype(BF)
    tgt[...] = targets(ids[...], clusters, per_source)
    store_blocks(unit[...], tgt[...], steps, CLUS_DEV * per_source, outs)


def pack_rest(steps, per_source, unit, tgt, *outs):
    store_blocks(unit[...], tgt[...], steps, CLUS_DEV * per_source, outs)


VMEM = pl.BlockSpec(memory_space=pltpu.VMEM)


def call_pack_first(emb, ids, steps, clusters, per_source):
    block = jax.ShapeDtypeStruct((CLUS_DEV * per_source, emb.shape[1]), BF)
    n = len(steps)
    return pl.pallas_call(
        functools.partial(pack_first, steps, clusters, per_source),
        out_shape=[
            jax.ShapeDtypeStruct(emb.shape, BF),
            jax.ShapeDtypeStruct(ids.shape, jnp.int32),
        ]
        + [block] * n,
        in_specs=[VMEM] * 2,
        out_specs=[VMEM] * (n + 2),
        compiler_params=pltpu.CompilerParams(vmem_limit_bytes=48 * 2**20),
        cost_estimate=pl.CostEstimate(
            flops=2 * n * block.shape[0] * emb.size, bytes_accessed=8 * 2**20, transcendentals=0
        ),
        name="pack_first",
    )(emb, ids)


def call_pack_rest(unit, tgt, steps, per_source):
    block = jax.ShapeDtypeStruct((CLUS_DEV * per_source, unit.shape[1]), BF)
    n = len(steps)
    return pl.pallas_call(
        functools.partial(pack_rest, steps, per_source),
        out_shape=[block] * n,
        in_specs=[VMEM] * 2,
        out_specs=[VMEM] * n,
        compiler_params=pltpu.CompilerParams(vmem_limit_bytes=48 * 2**20),
        cost_estimate=pl.CostEstimate(
            flops=2 * n * block.shape[0] * unit.size, bytes_accessed=8 * 2**20, transcendentals=0
        ),
        name="pack_rest",
    )(unit, tgt)


def load_half(blocks, scratch, me, half):
    per = blocks[0].shape[1]
    for step, block in enumerate(blocks):
        place = (me ^ step) & (half - 1)
        scratch[pl.ds(pl.multiple_of(place * per, per), per), :] = block[0]


CHUNK = 256


def best_over(keys, queries, start, triangular):
    chunk = queries[start : start + CHUNK, :]
    count = start + CHUNK if triangular else keys.shape[0]
    sims = matmul(keys[:count, :], chunk, ((1,), (1,)))
    filled = keys[:count, :LANES].astype(F32) < 1.5
    out = []
    for first in range(0, CHUNK, LANES):
        tile = sims[:, first : first + LANES]
        allowed = filled
        if triangular:
            allowed = filled & (
                iota((count, LANES), 0) < iota((count, LANES), 1) + (start + first)
            )
        out.append(jnp.max(jnp.where(allowed, tile, F32(-1.0)), axis=0, keepdims=True))
    return jnp.concatenate(out, axis=1)


def raise_best(best, keys, queries, triangular=False):
    for start in range(0, queries.shape[0], CHUNK):
        part = best_over(keys, queries, start, triangular)
        window = slice(start, start + CHUNK)
        best[:, window] = jnp.maximum(best[:, window], part)


def filled_queries(rows):
    ones = jnp.ones((8, LANES), BF)
    return matmul(ones, rows[:, :LANES], ((1,), (1,)))[:1] < 100.0


def near_kernel(half, *refs):
    own, other = refs[:half], refs[half : 2 * half]
    out, keys, others = refs[2 * half :]
    me = lax.axis_index("clus")
    load_half(own, keys, me, half)
    out[0] = jnp.full(out.shape[1:], -1.0, F32)
    raise_best(out.at[0], keys, keys, True)

    @pl.when(lax.axis_index("blk") == 1)
    def _():
        load_half(other, others, me, half)
        raise_best(out.at[0], others, keys)


def far_kernel(half, *refs):
    own, other = refs[: 2 * half], refs[2 * half : 4 * half]
    near_best, out, near, far, near_other, far_other, best_n, best_f = refs[4 * half :]
    me = lax.axis_index("clus")
    upper = me >= half
    load_half(own[:half], near, me, half)
    load_half(own[half:], far, me, half)
    best_n[...] = near_best[0]
    best_f[...] = jnp.full(best_f.shape, -1.0, F32)
    raise_best(best_f, far, far, True)

    @pl.when(upper)
    def _():
        raise_best(best_n, far, near)

    @pl.when(jnp.logical_not(upper))
    def _():
        raise_best(best_f, near, far)

    @pl.when(lax.axis_index("blk") == 1)
    def _():
        load_half(other[:half], near_other, me, half)
        load_half(other[half:], far_other, me, half)
        raise_best(best_f, near_other, far)
        raise_best(best_f, far_other, far)
        raise_best(best_n, far_other, near)

    rows = near.shape[0]
    at_near = pl.ds(pl.multiple_of(jnp.where(upper, rows, 0), rows), rows)
    at_far = pl.ds(pl.multiple_of(jnp.where(upper, 0, rows), rows), rows)
    out[0, :, at_near] = jnp.where(filled_queries(near), best_n[...], F32(0.0))
    out[0, :, at_far] = jnp.where(filled_queries(far), best_f[...], F32(0.0))


def call_near(own, other, half):
    _, per, width = own[0].shape
    rows = half * per
    spec = pl.BlockSpec((1, per, width), lambda c: (c, 0, 0))
    return pl.pallas_call(
        functools.partial(near_kernel, half),
        grid=(CLUS_DEV,),
        out_shape=jax.ShapeDtypeStruct((CLUS_DEV, 1, rows), F32),
        in_specs=[spec] * (2 * half),
        out_specs=pl.BlockSpec((1, 1, rows), lambda c: (c, 0, 0)),
        scratch_shapes=[pltpu.VMEM((rows, width), BF)] * 2,
        compiler_params=pltpu.CompilerParams(vmem_limit_bytes=48 * 2**20),
        cost_estimate=pl.CostEstimate(
            flops=2 * CLUS_DEV * 2 * rows * rows * width,
            bytes_accessed=8 * CLUS_DEV * rows * width,
            transcendentals=0,
        ),
        name="near",
    )(*own, *other)


def call_far(own, other, near_best, half):
    _, per, width = own[0].shape
    rows = half * per
    spec = pl.BlockSpec((1, per, width), lambda c: (c, 0, 0))
    return pl.pallas_call(
        functools.partial(far_kernel, half),
        grid=(CLUS_DEV,),
        out_shape=jax.ShapeDtypeStruct((CLUS_DEV, 1, 2 * rows), F32),
        in_specs=[spec] * (4 * half) + [pl.BlockSpec((1, 1, rows), lambda c: (c, 0, 0))],
        out_specs=pl.BlockSpec((1, 1, 2 * rows), lambda c: (c, 0, 0)),
        scratch_shapes=[pltpu.VMEM((rows, width), BF)] * 4 + [pltpu.VMEM((1, rows), F32)] * 2,
        compiler_params=pltpu.CompilerParams(vmem_limit_bytes=48 * 2**20),
        cost_estimate=pl.CostEstimate(
            flops=2 * CLUS_DEV * 5 * rows * rows * width,
            bytes_accessed=16 * CLUS_DEV * rows * width,
            transcendentals=0,
        ),
        name="far",
    )(*own, *other, near_best)


def local(embeddings, cluster_ids):
    owners = lax.axis_size("clus")
    clusters = CLUS_DEV * owners
    rows, width = embeddings.shape
    per_source = 2 * rows // clusters
    half = owners // 2
    far_steps = list(range(half, owners))
    near_steps = list(range(half))

    def to_owner(block, step):
        return lax.ppermute(block, "clus", [(i, i ^ step) for i in range(owners)])

    def to_later(block):
        return lax.ppermute(block, "blk", [(0, 1)])

    unit, tgt, *far_out = call_pack_first(embeddings, cluster_ids, far_steps, clusters, per_source)
    far_in = [to_owner(block, step) for step, block in zip(far_steps, far_out)]
    near_out = call_pack_rest(unit, tgt, near_steps, per_source)
    near_in = [near_out[0]] + [
        to_owner(block, step) for step, block in zip(near_steps[1:], near_out[1:])
    ]
    shape = (CLUS_DEV, per_source, width)
    near_in = [block.reshape(shape) for block in near_in]
    far_in = [block.reshape(shape) for block in far_in]
    near_other = [to_later(block) for block in near_in]
    far_other = [to_later(block) for block in far_in]
    near_best = call_near(near_in, near_other, half)
    best = call_far(near_in + far_in, near_other + far_other, near_best, half)
    return best.reshape(CLUS_DEV, rows)


def solution(mesh):
    placed = (P(("groups", "clus", "blk"), None), P(("groups", "clus", "blk"), None))
    return jax.shard_map(
        local, mesh=mesh, in_specs=placed, out_specs=P(("groups", "clus"), "blk"), check_vma=False
    )
```

```python
import functools

import jax
import jax.numpy as jnp
from jax import lax
from jax.experimental import pallas as pl
from jax.experimental.pallas import tpu as pltpu
from jax.sharding import PartitionSpec as P

CLUS_DEV = 2
LANES = 128
MARK = 2.0
BF = jnp.bfloat16
F32 = jnp.float32


def iota(shape, dim):
    return lax.broadcasted_iota(jnp.int32, shape, dim)


def matmul(a, b, contract):
    return lax.dot_general(a, b, (contract, ((), ())), preferred_element_type=F32)


def targets(ids, clusters, per_source):
    groups = ids.shape[1] // LANES
    parts = [ids[:, g * LANES : (g + 1) * LANES] for g in range(groups)]
    hot = jnp.concatenate(
        [(iota((clusters, LANES), 0) == part).astype(F32) for part in parts], axis=0
    )
    stacked = groups * clusters
    earlier = (iota((LANES, LANES), 0) < iota((LANES, LANES), 1)).astype(F32).astype(BF)
    within = matmul(hot.astype(BF), earlier, ((1,), (0,)))
    totals = jnp.broadcast_to(jnp.sum(hot, axis=1, keepdims=True), (stacked, LANES))
    a, b = iota((stacked, stacked), 0), iota((stacked, stacked), 1)
    chunks_before = ((a % clusters == b % clusters) & (b < a)).astype(F32).astype(BF)
    before = within + matmul(chunks_before, totals.astype(BF), ((1,), (0,)))
    picked = hot * before
    out = [
        jnp.sum(picked[g * clusters : (g + 1) * clusters], axis=0, keepdims=True).astype(jnp.int32)
        + parts[g] * per_source
        for g in range(groups)
    ]
    return jnp.concatenate(out, axis=1)


def pack_block(unit, tgt, dest, width):
    hit = (tgt - dest * width) == iota((width, tgt.shape[1]), 0)
    hot = hit.astype(F32)
    rows = matmul(hot.astype(BF), unit, ((1,), (0,)))
    empty = jnp.max(hot, axis=1, keepdims=True) < 0.5
    head = jnp.where(empty, F32(MARK), rows[:, :LANES])
    return head.astype(BF), rows[:, LANES:].astype(BF)


def store_blocks(unit, tgt, steps, width, outs):
    me = lax.axis_index("clus")
    for step, out in zip(steps, outs):
        head, tail = pack_block(unit, tgt, me ^ step, width)
        out[:, :LANES] = head
        out[:, LANES:] = tail


def pack_first(steps, clusters, per_source, emb, ids, unit, tgt, *outs):
    values = emb[...].astype(F32)
    scale = lax.rsqrt(jnp.sum(values * values, axis=1, keepdims=True) + 1e-6)
    unit[...] = (values * scale).astype(BF)
    tgt[...] = targets(ids[...], clusters, per_source)
    store_blocks(unit[...], tgt[...], steps, CLUS_DEV * per_source, outs)


def pack_rest(steps, per_source, unit, tgt, *outs):
    store_blocks(unit[...], tgt[...], steps, CLUS_DEV * per_source, outs)


VMEM = pl.BlockSpec(memory_space=pltpu.VMEM)


def kernel_call(kernel, shapes, inputs, flops, name, scratch=()):
    moved = sum(x.size * x.dtype.itemsize for x in list(inputs) + list(shapes))
    return pl.pallas_call(
        kernel,
        out_shape=shapes,
        in_specs=[VMEM] * len(inputs),
        out_specs=[VMEM] * len(shapes),
        scratch_shapes=scratch,
        compiler_params=pltpu.CompilerParams(vmem_limit_bytes=40 * 2**20),
        cost_estimate=pl.CostEstimate(flops=int(flops), bytes_accessed=moved, transcendentals=0),
        name=name,
    )(*inputs)


def call_pack_first(emb, ids, steps, clusters, per_source):
    block = jax.ShapeDtypeStruct((CLUS_DEV * per_source, emb.shape[1]), BF)
    shapes = [jax.ShapeDtypeStruct(emb.shape, BF), jax.ShapeDtypeStruct(ids.shape, jnp.int32)]
    return kernel_call(
        functools.partial(pack_first, steps, clusters, per_source),
        shapes + [block] * len(steps),
        [emb, ids],
        2 * len(steps) * block.shape[0] * emb.size,
        "pack_first",
    )


def call_pack_rest(unit, tgt, steps, per_source):
    block = jax.ShapeDtypeStruct((CLUS_DEV * per_source, unit.shape[1]), BF)
    return kernel_call(
        functools.partial(pack_rest, steps, per_source),
        [block] * len(steps),
        [unit, tgt],
        2 * len(steps) * block.shape[0] * unit.size,
        "pack_rest",
    )


CHUNK = 256


def raise_best(best, keys, queries, triangular=False):
    rows = queries.shape[0]
    chunk = min(CHUNK, rows)
    for start in range(0, rows, chunk):
        count = start + chunk if triangular else keys.shape[0]
        sims = matmul(keys[:count, :], queries[start : start + chunk, :], ((1,), (1,)))
        filled = keys[:count, :LANES].astype(F32) < 1.5
        for first in range(0, chunk, LANES):
            allowed = filled
            if triangular:
                allowed = filled & (
                    iota((count, LANES), 0) < iota((count, LANES), 1) + (start + first)
                )
            part = jnp.where(allowed, sims[:, first : first + LANES], F32(-1.0))
            window = slice(start + first, start + first + LANES)
            best[:, window] = jnp.maximum(best[:, window], jnp.max(part, axis=0, keepdims=True))


def gather_group(blocks, cluster, out, me):
    per = blocks[0].shape[0] // CLUS_DEV
    for step, block in enumerate(blocks):
        place = (me & (len(blocks) - 1)) ^ step
        rows = pl.ds(pl.multiple_of(place * per, per), per)
        out[rows, :] = block[cluster * per : (cluster + 1) * per, :]


def score_pair(bests, groups, new, old, bit, me):
    later = (me & bit) == 0

    @pl.when(later)
    def _():
        raise_best(bests[new], groups[old], groups[new])

    @pl.when(jnp.logical_not(later))
    def _():
        raise_best(bests[old], groups[new], groups[old])


def group_bits(owners):
    return [owners // 2, owners // 4, owners // 8]


def first_kernel(*refs):
    blocks, (cat, best) = refs[:-2], refs[-2:]
    me = lax.axis_index("clus")
    best[...] = jnp.full(best.shape, -1.0, F32)
    for c in range(CLUS_DEV):
        gather_group(blocks, c, cat.at[c], me)
        raise_best(best.at[c : c + 1], cat.at[c], cat.at[c], True)


def middle_kernel(bits, fresh, *refs):
    old = len(bits)
    cats, others, refs = refs[:old], refs[old : 2 * old], refs[2 * old :]
    old_bests, blocks = refs[:old], refs[old : old + fresh]
    cat, bests = refs[old + fresh], refs[old + fresh + 1 :]
    me = lax.axis_index("clus")
    for before, best in zip(old_bests, bests):
        best[...] = before[...]
    bests[old][...] = jnp.full(bests[old].shape, -1.0, F32)
    for c in range(CLUS_DEV):
        gather_group(blocks, c, cat.at[c], me)
        groups = [x.at[c] for x in cats] + [cat.at[c]]
        rows = [best.at[c : c + 1] for best in bests]
        raise_best(rows[old], groups[old], groups[old], True)
        for i, bit in enumerate(bits):
            score_pair(rows, groups, old, i, bit, me)

    @pl.when(lax.axis_index("blk") == 1)
    def _():
        for c in range(CLUS_DEV):
            rows = [best.at[c : c + 1] for best in bests]
            for i in range(old):
                raise_best(rows[i], others[old - 1].at[c], cats[i].at[c])
                raise_best(rows[old], others[i].at[c], cat.at[c])


def filled_queries(rows):
    ones = jnp.ones((8, LANES), BF)
    return matmul(ones, rows[:, :LANES], ((1,), (1,)))[:1] < 100.0


def last_kernel(bits, fresh, *refs):
    old = len(bits)
    cats, refs = refs[:old], refs[old:]
    others, refs = refs[: old - 1], refs[old - 1 :]
    late, refs = refs[:fresh], refs[fresh:]
    old_bests, refs = refs[:old], refs[old:]
    blocks, other_blocks, out = refs[:fresh], refs[fresh : 2 * fresh], refs[2 * fresh]
    cat, late_cat, *bests = refs[2 * fresh + 1 :]
    me = lax.axis_index("clus")
    for before, best in zip(old_bests, bests):
        best[...] = before[...]
    bests[old][...] = jnp.full(bests[old].shape, -1.0, F32)
    size = cat.shape[1]
    for c in range(CLUS_DEV):
        gather_group(blocks, c, cat.at[c], me)
        groups = [x.at[c] for x in cats] + [cat.at[c]]
        rows = [best.at[c : c + 1] for best in bests]
        raise_best(rows[old], groups[old], groups[old], True)
        for i, bit in enumerate(bits):
            score_pair(rows, groups, old, i, bit, me)

    @pl.when(lax.axis_index("blk") == 1)
    def _():
        for c in range(CLUS_DEV):
            rows = [best.at[c : c + 1] for best in bests]
            gather_group(late, c, late_cat.at[:size], me)
            gather_group(other_blocks, c, late_cat.at[size:], me)
            for i in range(old):
                raise_best(rows[i], late_cat, cats[i].at[c])
            raise_best(rows[old], late_cat, cat.at[c])
            for i in range(old - 1):
                raise_best(rows[old], others[i].at[c], cat.at[c])

    total = out.shape[1]
    start = 0
    for c in range(CLUS_DEV):
        start = 0
        for group, best in zip(list(cats) + [cat], bests):
            count = group.shape[1]
            per = blocks[0].shape[0] // CLUS_DEV
            sources = count // per
            base = (me ^ (start // per)) & ~(sources - 1)
            at = pl.ds(pl.multiple_of(base * per, LANES), count)
            kept = filled_queries(group.at[c])
            out[c : c + 1, at] = jnp.where(kept, best[c : c + 1, :], F32(0.0))
            start += count
    assert start == total


def shape_of(sources, per, width):
    return [
        jax.ShapeDtypeStruct((CLUS_DEV, sources * per, width), BF),
        jax.ShapeDtypeStruct((CLUS_DEV, sources * per), F32),
    ]


def local(embeddings, cluster_ids):
    owners = lax.axis_size("clus")
    clusters = CLUS_DEV * owners
    rows, width = embeddings.shape
    per = 2 * rows // clusters
    bits = group_bits(owners)
    bounds = [0, owners // 2, owners // 2 + owners // 4, owners - owners // 8, owners]
    steps = [list(range(a, b)) for a, b in zip(bounds, bounds[1:])]
    unit_flops = 2 * CLUS_DEV * per * per * width

    def to_owner(block, step):
        return lax.ppermute(block, "clus", [(i, i ^ step) for i in range(owners)])

    def to_later(block):
        return lax.ppermute(block, "blk", [(0, 1)])

    def after(block, done):
        return lax.optimization_barrier((block, done))

    unit, tgt, ahead = call_pack_first(embeddings, cluster_ids, steps[1][:1], clusters, per)
    far1 = [to_owner(ahead, steps[1][0])]
    near_out = call_pack_rest(unit, tgt, steps[0] + steps[1][1:], per)
    near = [near_out[0]] + [to_owner(b, s) for s, b in zip(steps[0][1:], near_out[1:])]
    far1 += [to_owner(b, s) for s, b in zip(steps[1][1:], near_out[len(steps[0]) :])]
    far_out = call_pack_rest(unit, tgt, steps[2] + steps[3], per)
    held, near[-1] = after(far_out[: len(steps[2])], near[-1])
    far2 = [to_owner(b, s) for s, b in zip(steps[2], held)]

    n0, n1, n2, n3 = [len(x) for x in steps]
    cat0, best0 = kernel_call(
        first_kernel, shape_of(n0, per, width), near, unit_flops * n0 * n0, "first"
    )
    oth0 = to_later(cat0)
    held, far1[0] = after(far_out[len(steps[2]) :], far1[0])
    far3 = [to_owner(b, s) for s, b in zip(steps[3], held)]
    cat1, best0, best1 = kernel_call(
        functools.partial(middle_kernel, bits[:1], n1),
        shape_of(n1, per, width)[:1] + [best0, shape_of(n1, per, width)[1]],
        [cat0, oth0, best0] + far1,
        unit_flops * (n0 * n0 + 2 * n0 * n1 + n1 * n1),
        "second",
    )
    oth1 = to_later(cat1)
    cat2, best0, best1, best2 = kernel_call(
        functools.partial(middle_kernel, bits[:2], n2),
        shape_of(n2, per, width)[:1] + [best0, best1, shape_of(n2, per, width)[1]],
        [cat0, cat1, oth0, oth1, best0, best1] + far2,
        unit_flops * (n0 * n1 + n1 * n1 + 2 * n2 * (n0 + n1)),
        "third",
    )
    oth2 = [to_later(b) for b in far2]
    oth3 = [to_later(b) for b in far3]
    (best,) = kernel_call(
        functools.partial(last_kernel, bits, n3),
        [jax.ShapeDtypeStruct((CLUS_DEV, rows), F32)],
        [cat0, cat1, cat2, oth0, oth1] + oth2 + [best0, best1, best2] + far3 + oth3,
        unit_flops * 4 * n3 * (n0 + n1 + n2),
        "last",
        [
            pltpu.VMEM((CLUS_DEV, n3 * per, width), BF),
            pltpu.VMEM((2 * n3 * per, width), BF),
        ]
        + [pltpu.VMEM((CLUS_DEV, n * per), F32) for n in (n0, n1, n2, n3)],
    )
    return best


def solution(mesh):
    placed = (P(("groups", "clus", "blk"), None), P(("groups", "clus", "blk"), None))
    return jax.shard_map(
        local, mesh=mesh, in_specs=placed, out_specs=P(("groups", "clus"), "blk"), check_vma=False
    )
```

```python
import functools

import jax
import jax.numpy as jnp
from jax import lax
from jax.experimental import pallas as pl
from jax.experimental.pallas import tpu as pltpu
from jax.sharding import PartitionSpec as P

CLUS_DEV = 2
LANES = 128
MARK = 2.0
BF = jnp.bfloat16
F32 = jnp.float32


def iota(shape, dim):
    return lax.broadcasted_iota(jnp.int32, shape, dim)


def matmul(a, b, contract):
    return lax.dot_general(a, b, (contract, ((), ())), preferred_element_type=F32)


def targets(ids, clusters, per_source):
    groups = ids.shape[1] // LANES
    parts = [ids[:, g * LANES : (g + 1) * LANES] for g in range(groups)]
    hot = jnp.concatenate(
        [(iota((clusters, LANES), 0) == part).astype(F32) for part in parts], axis=0
    )
    stacked = groups * clusters
    earlier = (iota((LANES, LANES), 0) < iota((LANES, LANES), 1)).astype(F32).astype(BF)
    within = matmul(hot.astype(BF), earlier, ((1,), (0,)))
    totals = jnp.broadcast_to(jnp.sum(hot, axis=1, keepdims=True), (stacked, LANES))
    a, b = iota((stacked, stacked), 0), iota((stacked, stacked), 1)
    chunks_before = ((a % clusters == b % clusters) & (b < a)).astype(F32).astype(BF)
    before = within + matmul(chunks_before, totals.astype(BF), ((1,), (0,)))
    picked = hot * before
    out = [
        jnp.sum(picked[g * clusters : (g + 1) * clusters], axis=0, keepdims=True).astype(jnp.int32)
        + parts[g] * per_source
        for g in range(groups)
    ]
    return jnp.concatenate(out, axis=1)


def pack_block(unit, tgt, dest, width):
    hit = (tgt - dest * width) == iota((width, tgt.shape[1]), 0)
    hot = hit.astype(F32)
    rows = matmul(hot.astype(BF), unit, ((1,), (0,)))
    empty = jnp.max(hot, axis=1, keepdims=True) < 0.5
    head = jnp.where(empty, F32(MARK), rows[:, :LANES])
    return head.astype(BF), rows[:, LANES:].astype(BF)


def store_blocks(unit, tgt, steps, width, outs):
    me = lax.axis_index("clus")
    for step, out in zip(steps, outs):
        head, tail = pack_block(unit, tgt, me ^ step, width)
        out[:, :LANES] = head
        out[:, LANES:] = tail


def pack_first(steps, clusters, per_source, emb, ids, unit, tgt, *outs):
    values = emb[...].astype(F32)
    scale = lax.rsqrt(jnp.sum(values * values, axis=1, keepdims=True) + 1e-6)
    unit[...] = (values * scale).astype(BF)
    tgt[...] = targets(ids[...], clusters, per_source)
    store_blocks(unit[...], tgt[...], steps, CLUS_DEV * per_source, outs)


def pack_rest(steps, per_source, unit, tgt, *outs):
    store_blocks(unit[...], tgt[...], steps, CLUS_DEV * per_source, outs)


VMEM = pl.BlockSpec(memory_space=pltpu.VMEM)


def kernel_call(kernel, shapes, inputs, name, scratch=()):
    return pl.pallas_call(
        kernel,
        out_shape=shapes,
        in_specs=[VMEM] * len(inputs),
        out_specs=[VMEM] * len(shapes),
        scratch_shapes=scratch,
        compiler_params=pltpu.CompilerParams(vmem_limit_bytes=40 * 2**20),
        cost_estimate=pl.CostEstimate(flops=1000, bytes_accessed=1000, transcendentals=0),
        name=name,
    )(*inputs)


def call_pack_first(emb, ids, steps, clusters, per_source):
    block = jax.ShapeDtypeStruct((CLUS_DEV * per_source, emb.shape[1]), BF)
    shapes = [jax.ShapeDtypeStruct(emb.shape, BF), jax.ShapeDtypeStruct(ids.shape, jnp.int32)]
    return kernel_call(
        functools.partial(pack_first, steps, clusters, per_source),
        shapes + [block] * len(steps),
        [emb, ids],
        "pack_first",
    )


def call_pack_rest(unit, tgt, steps, per_source):
    block = jax.ShapeDtypeStruct((CLUS_DEV * per_source, unit.shape[1]), BF)
    return kernel_call(
        functools.partial(pack_rest, steps, per_source),
        [block] * len(steps),
        [unit, tgt],
        "pack_rest",
    )


CHUNK = 256


def raise_best(best, keys, queries, triangular=False):
    rows = queries.shape[0]
    chunk = min(CHUNK, rows)
    for start in range(0, rows, chunk):
        count = start + chunk if triangular else keys.shape[0]
        sims = matmul(keys[:count, :], queries[start : start + chunk, :], ((1,), (1,)))
        filled = keys[:count, :LANES].astype(F32) < 1.5
        for first in range(0, chunk, LANES):
            allowed = filled
            if triangular:
                allowed = filled & (
                    iota((count, LANES), 0) < iota((count, LANES), 1) + (start + first)
                )
            part = jnp.where(allowed, sims[:, first : first + LANES], F32(-1.0))
            window = slice(start + first, start + first + LANES)
            best[:, window] = jnp.maximum(best[:, window], jnp.max(part, axis=0, keepdims=True))


def gather_group(blocks, cluster, out, me):
    per = blocks[0].shape[0] // CLUS_DEV
    for step, block in enumerate(blocks):
        place = (me & (len(blocks) - 1)) ^ step
        rows = pl.ds(pl.multiple_of(place * per, per), per)
        out[rows, :] = block[cluster * per : (cluster + 1) * per, :]


def score_pair(bests, groups, new, old, bit, me):
    later = (me & bit) == 0

    @pl.when(later)
    def _():
        raise_best(bests[new], groups[old], groups[new])

    @pl.when(jnp.logical_not(later))
    def _():
        raise_best(bests[old], groups[new], groups[old])


def own_early(split, bit, *refs):
    blocks, (send, best) = refs[:-2], refs[-2:]
    per = blocks[0].shape[0] // CLUS_DEV
    cut = split * per
    me = lax.axis_index("clus")
    best[...] = jnp.full(best.shape, -1.0, F32)
    for c in range(CLUS_DEV):
        near, far = send.at[1, c, :cut], send.at[1, c, cut:]
        gather_group(blocks[:split], c, near, me)
        gather_group(blocks[split:], c, far, me)
        rows = [best.at[c : c + 1, :cut], best.at[c : c + 1, cut:]]
        raise_best(rows[0], near, near, True)
        raise_best(rows[1], far, far, True)
        score_pair(rows, [near, far], 1, 0, bit, me)


def cross_early(send, received, before, best):
    best[...] = before[...]

    @pl.when(lax.axis_index("blk") == 1)
    def _():
        for c in range(CLUS_DEV):
            raise_best(best.at[c : c + 1], received.at[0, c], send.at[1, c])


def own_late(cuts, bits, *refs):
    send, before = refs[:2]
    blocks, (cat, best, best_late) = refs[2:-3], refs[-3:]
    me = lax.axis_index("clus")
    best[...] = before[...]
    best_late[...] = jnp.full(best_late.shape, -1.0, F32)
    for c in range(CLUS_DEV):
        late = cat.at[c]
        gather_group(blocks, c, late, me)
        groups, rows = [late], [best_late.at[c : c + 1]]
        for a, b in zip(cuts, cuts[1:]):
            groups.append(send.at[1, c, a:b])
            rows.append(best.at[c : c + 1, a:b])
        raise_best(rows[0], late, late, True)
        for i, bit in enumerate(bits):
            score_pair(rows, groups, 0, i + 1, bit, me)


def filled_queries(rows):
    ones = jnp.ones((8, LANES), BF)
    return matmul(ones, rows[:, :LANES], ((1,), (1,)))[:1] < 100.0


def cross_late(cuts, send, received, cat, before, before_late, *refs):
    others, (out, keys, best, best_late) = refs[:-4], refs[-4:]
    per = others[0].shape[0] // CLUS_DEV
    me = lax.axis_index("clus")
    best[...] = before[...]
    best_late[...] = before_late[...]

    @pl.when(lax.axis_index("blk") == 1)
    def _():
        for c in range(CLUS_DEV):
            for i, other in enumerate(others):
                keys[i * per : (i + 1) * per, :] = other[c * per : (c + 1) * per, :]
            raise_best(best.at[c : c + 1], keys, send.at[1, c])
            raise_best(best_late.at[c : c + 1], keys, cat.at[c])
            raise_best(best_late.at[c : c + 1], received.at[0, c], cat.at[c])

    for c in range(CLUS_DEV):
        parts = [
            (a, b - a, send.at[1, c, a:b], best.at[c : c + 1, a:b]) for a, b in zip(cuts, cuts[1:])
        ]
        parts.append((cuts[-1], cat.shape[1], cat.at[c], best_late.at[c : c + 1]))
        for start, count, rows, value in parts:
            sources = count // per
            base = (me ^ (start // per)) & ~(sources - 1)
            at = pl.ds(pl.multiple_of(base * per, LANES), count)
            out[c : c + 1, at] = jnp.where(filled_queries(rows), value[...], F32(0.0))


def local(embeddings, cluster_ids):
    owners = lax.axis_size("clus")
    clusters = CLUS_DEV * owners
    rows, width = embeddings.shape
    per = 2 * rows // clusters
    bits = [owners // 2, owners // 4]
    bounds = [0, owners // 2, owners // 2 + owners // 4, owners]
    cuts = [x * per for x in bounds[:3]]
    near, mid, late = [list(range(a, b)) for a, b in zip(bounds, bounds[1:])]

    def to_owner(block, step):
        return lax.ppermute(block, "clus", [(i, i ^ step) for i in range(owners)])

    unit, tgt, ahead = call_pack_first(embeddings, cluster_ids, mid[:1], clusters, per)
    sent = [to_owner(ahead, mid[0])]
    order = mid[1:] + near
    packed = dict(zip(order, call_pack_rest(unit, tgt, order, per)))
    arrived = {0: packed.pop(0), mid[0]: sent[0]}
    for step, block in packed.items():
        arrived[step] = to_owner(block, step)
    for step, block in zip(late, call_pack_rest(unit, tgt, late, per)):
        arrived[step] = to_owner(block, step)

    early = cuts[-1]
    late_rows = rows - early
    send, best = kernel_call(
        functools.partial(own_early, len(near), bits[0]),
        [
            jax.ShapeDtypeStruct((2, CLUS_DEV, early, width), BF),
            jax.ShapeDtypeStruct((CLUS_DEV, early), F32),
        ],
        [arrived[s] for s in near + mid],
        "own_early",
    )
    received = lax.all_to_all(send, "blk", split_axis=0, concat_axis=0, tiled=True)
    (best,) = kernel_call(cross_early, [best], [send, received, best], "cross_early")
    *last, best = lax.optimization_barrier((*[arrived[s] for s in late], best))
    cat, best, best_late = kernel_call(
        functools.partial(own_late, cuts, bits),
        [
            jax.ShapeDtypeStruct((CLUS_DEV, late_rows, width), BF),
            best,
            jax.ShapeDtypeStruct((CLUS_DEV, late_rows), F32),
        ],
        [send, best] + last,
        "own_late",
    )
    others = [lax.ppermute(block, "blk", [(0, 1)]) for block in last]
    (out,) = kernel_call(
        functools.partial(cross_late, cuts),
        [jax.ShapeDtypeStruct((CLUS_DEV, rows), F32)],
        [send, received, cat, best, best_late] + others,
        "cross_late",
        [
            pltpu.VMEM((late_rows, width), BF),
            pltpu.VMEM((CLUS_DEV, early), F32),
            pltpu.VMEM((CLUS_DEV, late_rows), F32),
        ],
    )
    return out


def solution(mesh):
    placed = (P(("groups", "clus", "blk"), None), P(("groups", "clus", "blk"), None))
    return jax.shard_map(
        local, mesh=mesh, in_specs=placed, out_specs=P(("groups", "clus"), "blk"), check_vma=False
    )
```

```python
import functools

import jax
import jax.numpy as jnp
from jax import lax
from jax.experimental import pallas as pl
from jax.experimental.pallas import tpu as pltpu
from jax.sharding import PartitionSpec as P

CLUS_DEV = 2
LANES = 128
MARK = 2.0
BF = jnp.bfloat16
F32 = jnp.float32


def iota(shape, dim):
    return lax.broadcasted_iota(jnp.int32, shape, dim)


def matmul(a, b, contract):
    return lax.dot_general(a, b, (contract, ((), ())), preferred_element_type=F32)


def targets(ids, clusters, per_source):
    groups = ids.shape[1] // LANES
    parts = [ids[:, g * LANES : (g + 1) * LANES] for g in range(groups)]
    hot = jnp.concatenate(
        [(iota((clusters, LANES), 0) == part).astype(F32) for part in parts], axis=0
    )
    stacked = groups * clusters
    earlier = (iota((LANES, LANES), 0) < iota((LANES, LANES), 1)).astype(F32).astype(BF)
    within = matmul(hot.astype(BF), earlier, ((1,), (0,)))
    totals = jnp.broadcast_to(jnp.sum(hot, axis=1, keepdims=True), (stacked, LANES))
    a, b = iota((stacked, stacked), 0), iota((stacked, stacked), 1)
    chunks_before = ((a % clusters == b % clusters) & (b < a)).astype(F32).astype(BF)
    before = within + matmul(chunks_before, totals.astype(BF), ((1,), (0,)))
    picked = hot * before
    out = [
        jnp.sum(picked[g * clusters : (g + 1) * clusters], axis=0, keepdims=True).astype(jnp.int32)
        + parts[g] * per_source
        for g in range(groups)
    ]
    return jnp.concatenate(out, axis=1)


def pack_block(unit, tgt, dest, width):
    hit = (tgt - dest * width) == iota((width, tgt.shape[1]), 0)
    hot = hit.astype(F32)
    rows = matmul(hot.astype(BF), unit, ((1,), (0,)))
    empty = jnp.max(hot, axis=1, keepdims=True) < 0.5
    head = jnp.where(empty, F32(MARK), rows[:, :LANES])
    return head.astype(BF), rows[:, LANES:].astype(BF)


def store_blocks(unit, tgt, steps, width, outs):
    me = lax.axis_index("clus")
    for step, out in zip(steps, outs):
        head, tail = pack_block(unit, tgt, me ^ step, width)
        out[:, :LANES] = head
        out[:, LANES:] = tail


def pack_first(steps, clusters, per_source, emb, ids, unit, tgt, *outs):
    values = emb[...].astype(F32)
    scale = lax.rsqrt(jnp.sum(values * values, axis=1, keepdims=True) + 1e-6)
    unit[...] = (values * scale).astype(BF)
    tgt[...] = targets(ids[...], clusters, per_source)
    store_blocks(unit[...], tgt[...], steps, CLUS_DEV * per_source, outs)


def pack_rest(steps, per_source, unit, tgt, *outs):
    store_blocks(unit[...], tgt[...], steps, CLUS_DEV * per_source, outs)


VMEM = pl.BlockSpec(memory_space=pltpu.VMEM)


def kernel_call(kernel, shapes, inputs, name, scratch=()):
    return pl.pallas_call(
        kernel,
        out_shape=shapes,
        in_specs=[VMEM] * len(inputs),
        out_specs=[VMEM] * len(shapes),
        scratch_shapes=scratch,
        compiler_params=pltpu.CompilerParams(vmem_limit_bytes=20 * 2**20),
        cost_estimate=pl.CostEstimate(flops=1000, bytes_accessed=1000, transcendentals=0),
        name=name,
    )(*inputs)


def call_pack_first(emb, ids, steps, clusters, per_source):
    block = jax.ShapeDtypeStruct((CLUS_DEV * per_source, emb.shape[1]), BF)
    shapes = [jax.ShapeDtypeStruct(emb.shape, BF), jax.ShapeDtypeStruct(ids.shape, jnp.int32)]
    return kernel_call(
        functools.partial(pack_first, steps, clusters, per_source),
        shapes + [block] * len(steps),
        [emb, ids],
        "pack_first",
    )


def call_pack_rest(unit, tgt, steps, per_source):
    block = jax.ShapeDtypeStruct((CLUS_DEV * per_source, unit.shape[1]), BF)
    return kernel_call(
        functools.partial(pack_rest, steps, per_source),
        [block] * len(steps),
        [unit, tgt],
        "pack_rest",
    )


CHUNK = 256


def raise_best(best, keys, queries, triangular=False):
    rows = queries.shape[0]
    for start in range(0, rows, CHUNK):
        chunk = min(CHUNK, rows - start)
        count = start + chunk if triangular else keys.shape[0]
        sims = matmul(keys[:count, :], queries[start : start + chunk, :], ((1,), (1,)))
        filled = keys[:count, :LANES].astype(F32) < 1.5
        for first in range(0, chunk, LANES):
            allowed = filled
            if triangular:
                allowed = filled & (
                    iota((count, LANES), 0) < iota((count, LANES), 1) + (start + first)
                )
            part = jnp.where(allowed, sims[:, first : first + LANES], F32(-1.0))
            window = slice(start + first, start + first + LANES)
            best[:, window] = jnp.maximum(best[:, window], jnp.max(part, axis=0, keepdims=True))


def gather_group(blocks, cluster, out, me):
    per = blocks[0].shape[0] // CLUS_DEV
    for step, block in enumerate(blocks):
        place = (me & (len(blocks) - 1)) ^ step
        rows = pl.ds(pl.multiple_of(place * per, per), per)
        out[rows, :] = block[cluster * per : (cluster + 1) * per, :]


def score_pair(bests, groups, new, old, bit, me):
    later = (me & bit) == 0

    @pl.when(later)
    def _():
        raise_best(bests[new], groups[old], groups[new])

    @pl.when(jnp.logical_not(later))
    def _():
        raise_best(bests[old], groups[new], groups[old])


def own_stage(cuts, bits, held, first, *refs):
    stages, refs = refs[:held], refs[held:]
    blocks, (send, best) = list(refs[:-2]), refs[-2:]
    before = blocks.pop(0) if held else None
    per = blocks[0].shape[0] // CLUS_DEV
    me = lax.axis_index("clus")
    core = lax.axis_index("blk")
    spans = list(zip(cuts, cuts[1:]))
    base = spans[first][0]
    if held:
        best[:, :base] = before[:, :base]
    best[:, base:] = jnp.full((CLUS_DEV, best.shape[1] - base), -1.0, F32)
    for c in range(CLUS_DEV):
        rows = [best.at[c : c + 1, a:b] for a, b in spans]
        groups = []
        for stage in stages:
            start = spans[len(groups)][0]
            end = start + stage.shape[2]
            while len(groups) < first and spans[len(groups)][0] < end:
                a, b = spans[len(groups)]
                groups.append(stage.at[core, c, a - start : b - start])
        for i in range(first, len(spans)):
            a, b = spans[i]
            group = send.at[1, c, a - base : b - base]
            gather_group(blocks[(a - base) // per : (b - base) // per], c, group, me)
            groups.append(group)
            raise_best(rows[i], group, group, True)
            for j in range(i):
                score_pair(rows, groups, i, j, bits[j], me)
        send[0, c] = send[1, c]


def cross_stage(cuts, held, *refs):
    stages, before, best = refs[: held + 1], refs[held + 1], refs[held + 2]
    best[...] = before[...]

    @pl.when(lax.axis_index("blk") == 1)
    def _():
        new = stages[-1]
        for c in range(CLUS_DEV):
            base = 0
            for stage in stages:
                end = base + stage.shape[2]
                raise_best(best.at[c : c + 1, base:end], new.at[0, c], stage.at[1, c])
                base = end
            start = base - new.shape[2]
            for stage in stages[:-1]:
                raise_best(best.at[c : c + 1, start:base], stage.at[0, c], new.at[1, c])


def filled_queries(rows):
    ones = jnp.ones((8, LANES), BF)
    return matmul(ones, rows[:, :LANES], ((1,), (1,)))[:1] < 100.0


def cross_last(cuts, held, *refs):
    stages, (send, before), refs = refs[:held], refs[held : held + 2], refs[held + 2 :]
    others, (out, keys, best) = refs[:-3], refs[-3:]
    per = others[0].shape[0] // CLUS_DEV
    me = lax.axis_index("clus")
    core = lax.axis_index("blk")
    best[...] = before[...]
    start = best.shape[1] - send.shape[2]

    @pl.when(core == 1)
    def _():
        for c in range(CLUS_DEV):
            for i, other in enumerate(others):
                keys[i * per : (i + 1) * per, :] = other[c * per : (c + 1) * per, :]
            base = 0
            for stage in stages:
                end = base + stage.shape[2]
                raise_best(best.at[c : c + 1, base:end], keys, stage.at[1, c])
                raise_best(best.at[c : c + 1, start:], stage.at[0, c], send.at[1, c])
                base = end
            raise_best(best.at[c : c + 1, start:], keys, send.at[1, c])

    for c in range(CLUS_DEV):
        whole = [(stage.shape[2], stage.at[core, c]) for stage in stages]
        whole.append((send.shape[2], send.at[1, c]))
        base = 0
        for size, rows in whole:
            kept = jnp.where(filled_queries(rows), best[c : c + 1, base : base + size], F32(0.0))
            for a, b in zip(cuts, cuts[1:]):
                if base <= a < base + size:
                    place = (me ^ (a // per)) & ~((b - a) // per - 1)
                    at = pl.ds(pl.multiple_of(place * per, LANES), b - a)
                    out[c : c + 1, at] = kept[:, a - base : b - base]
            base += size


def local(embeddings, cluster_ids):
    owners = lax.axis_size("clus")
    clusters = CLUS_DEV * owners
    rows, width = embeddings.shape
    per = 2 * rows // clusters
    bits = [owners // 2, owners // 4, owners // 8]
    bounds = [0, owners // 2, owners // 2 + owners // 4, owners - owners // 8, owners]
    cuts = [x * per for x in bounds]
    near, far1, far2, far3 = [list(range(a, b)) for a, b in zip(bounds, bounds[1:])]
    best_shape = jax.ShapeDtypeStruct((CLUS_DEV, rows), F32)

    def to_owner(block, step):
        return lax.ppermute(block, "clus", [(i, i ^ step) for i in range(owners)])

    def stage_shape(sources):
        return jax.ShapeDtypeStruct((2, CLUS_DEV, sources * per, width), BF)

    def to_both(send):
        return lax.all_to_all(send, "blk", split_axis=0, concat_axis=0, tiled=True)

    arrived = {}
    lead = near[1 : 1 + len(far2) + len(far3)]
    unit, tgt, *packed = call_pack_first(embeddings, cluster_ids, lead, clusters, per)
    for steps in (far1, near[len(lead) + 1 :] + [0], far2 + far3, []):
        for step, block in zip(lead, packed):
            arrived[step] = to_owner(block, step) if step else block
        lead, packed = steps, call_pack_rest(unit, tgt, steps, per) if steps else []

    early = near + far1
    send, best = kernel_call(
        functools.partial(own_stage, cuts[:3], bits, 0, 0),
        [stage_shape(len(early)), best_shape],
        [arrived[s] for s in early],
        "own_early",
    )
    stages = [to_both(send)]
    (best,) = kernel_call(
        functools.partial(cross_stage, cuts, 0), [best_shape], stages + [best], "cross_early"
    )
    *new, best = lax.optimization_barrier((*[arrived[s] for s in far2], best))
    send, best = kernel_call(
        functools.partial(own_stage, cuts[:4], bits, 1, 2),
        [stage_shape(len(far2)), best_shape],
        stages + [best] + new,
        "own_middle",
    )
    stages.append(to_both(send))
    (best,) = kernel_call(
        functools.partial(cross_stage, cuts, 1), [best_shape], stages + [best], "cross_middle"
    )
    *new, best = lax.optimization_barrier((*[arrived[s] for s in far3], best))
    send, best = kernel_call(
        functools.partial(own_stage, cuts, bits, 2, 3),
        [stage_shape(len(far3)), best_shape],
        stages + [best] + new,
        "own_last",
    )
    others = [lax.ppermute(block, "blk", [(0, 1)]) for block in new]
    (out,) = kernel_call(
        functools.partial(cross_last, cuts, 2),
        [best_shape],
        stages + [send, best] + others,
        "cross_last",
        [pltpu.VMEM((len(far3) * per, width), BF), pltpu.VMEM((CLUS_DEV, rows), F32)],
    )
    return out


def solution(mesh):
    placed = (P(("groups", "clus", "blk"), None), P(("groups", "clus", "blk"), None))
    return jax.shard_map(
        local, mesh=mesh, in_specs=placed, out_specs=P(("groups", "clus"), "blk"), check_vma=False
    )
```

```python
import functools

import jax
import jax.numpy as jnp
from jax import lax
from jax.experimental import pallas as pl
from jax.experimental.pallas import tpu as pltpu
from jax.sharding import PartitionSpec as P

CLUS_DEV = 2
LANES = 128
MARK = 2.0
BF = jnp.bfloat16
F32 = jnp.float32


def iota(shape, dim):
    return lax.broadcasted_iota(jnp.int32, shape, dim)


def matmul(a, b, contract):
    return lax.dot_general(a, b, (contract, ((), ())), preferred_element_type=F32)


def targets(ids, clusters, per_source):
    groups = ids.shape[1] // LANES
    parts = [ids[:, g * LANES : (g + 1) * LANES] for g in range(groups)]
    hot = jnp.concatenate(
        [(iota((clusters, LANES), 0) == part).astype(F32) for part in parts], axis=0
    )
    stacked = groups * clusters
    earlier = (iota((LANES, LANES), 0) < iota((LANES, LANES), 1)).astype(F32).astype(BF)
    within = matmul(hot.astype(BF), earlier, ((1,), (0,)))
    totals = jnp.broadcast_to(jnp.sum(hot, axis=1, keepdims=True), (stacked, LANES))
    a, b = iota((stacked, stacked), 0), iota((stacked, stacked), 1)
    chunks_before = ((a % clusters == b % clusters) & (b < a)).astype(F32).astype(BF)
    before = within + matmul(chunks_before, totals.astype(BF), ((1,), (0,)))
    picked = hot * before
    out = [
        jnp.sum(picked[g * clusters : (g + 1) * clusters], axis=0, keepdims=True).astype(jnp.int32)
        + parts[g] * per_source
        for g in range(groups)
    ]
    return jnp.concatenate(out, axis=1)


def pack_block(unit, tgt, dest, width):
    hit = (tgt - dest * width) == iota((width, tgt.shape[1]), 0)
    hot = hit.astype(F32)
    rows = matmul(hot.astype(BF), unit, ((1,), (0,)))
    empty = jnp.max(hot, axis=1, keepdims=True) < 0.5
    head = jnp.where(empty, F32(MARK), rows[:, :LANES])
    return head.astype(BF), rows[:, LANES:].astype(BF)


def store_blocks(unit, tgt, steps, width, outs):
    me = lax.axis_index("clus")
    for step, out in zip(steps, outs):
        head, tail = pack_block(unit, tgt, me ^ step, width)
        out[:, :LANES] = head
        out[:, LANES:] = tail


def pack_first(steps, clusters, per_source, emb, ids, unit, tgt, *outs):
    values = emb[...].astype(F32)
    scale = lax.rsqrt(jnp.sum(values * values, axis=1, keepdims=True) + 1e-6)
    unit[...] = (values * scale).astype(BF)
    tgt[...] = targets(ids[...], clusters, per_source)
    store_blocks(unit[...], tgt[...], steps, CLUS_DEV * per_source, outs)


def pack_rest(steps, per_source, unit, tgt, *outs):
    store_blocks(unit[...], tgt[...], steps, CLUS_DEV * per_source, outs)


VMEM = pl.BlockSpec(memory_space=pltpu.VMEM)


def kernel_call(kernel, shapes, inputs, name, scratch=()):
    return pl.pallas_call(
        kernel,
        out_shape=shapes,
        in_specs=[VMEM] * len(inputs),
        out_specs=[VMEM] * len(shapes),
        scratch_shapes=scratch,
        compiler_params=pltpu.CompilerParams(vmem_limit_bytes=20 * 2**20),
        cost_estimate=pl.CostEstimate(flops=1000, bytes_accessed=1000, transcendentals=0),
        name=name,
    )(*inputs)


def call_pack_first(emb, ids, steps, clusters, per_source):
    block = jax.ShapeDtypeStruct((CLUS_DEV * per_source, emb.shape[1]), BF)
    shapes = [jax.ShapeDtypeStruct(emb.shape, BF), jax.ShapeDtypeStruct(ids.shape, jnp.int32)]
    return kernel_call(
        functools.partial(pack_first, steps, clusters, per_source),
        shapes + [block] * len(steps),
        [emb, ids],
        "pack_first",
    )


def call_pack_rest(unit, tgt, steps, per_source):
    block = jax.ShapeDtypeStruct((CLUS_DEV * per_source, unit.shape[1]), BF)
    return kernel_call(
        functools.partial(pack_rest, steps, per_source),
        [block] * len(steps),
        [unit, tgt],
        "pack_rest",
    )


CHUNK = 256


def raise_best(best, keys, queries, triangular=False):
    rows = queries.shape[0]
    for start in range(0, rows, CHUNK):
        chunk = min(CHUNK, rows - start)
        count = start + chunk if triangular else keys.shape[0]
        sims = matmul(keys[:count, :], queries[start : start + chunk, :], ((1,), (1,)))
        filled = keys[:count, :LANES].astype(F32) < 1.5
        for first in range(0, chunk, LANES):
            allowed = filled
            if triangular:
                allowed = filled & (
                    iota((count, LANES), 0) < iota((count, LANES), 1) + (start + first)
                )
            part = jnp.where(allowed, sims[:, first : first + LANES], F32(-1.0))
            window = slice(start + first, start + first + LANES)
            best[:, window] = jnp.maximum(best[:, window], jnp.max(part, axis=0, keepdims=True))


def gather_group(blocks, cluster, out, me):
    per = blocks[0].shape[0] // CLUS_DEV
    for step, block in enumerate(blocks):
        place = (me & (len(blocks) - 1)) ^ step
        rows = pl.ds(pl.multiple_of(place * per, per), per)
        out[rows, :] = block[cluster * per : (cluster + 1) * per, :]


def score_pair(bests, groups, new, old, bit, me):
    later = (me & bit) == 0

    @pl.when(later)
    def _():
        raise_best(bests[new], groups[old], groups[new])

    @pl.when(jnp.logical_not(later))
    def _():
        raise_best(bests[old], groups[new], groups[old])


def own_stage(cuts, bits, held, first, *refs):
    stages, refs = refs[:held], refs[held:]
    blocks, (send, best) = list(refs[:-2]), refs[-2:]
    before = blocks.pop(0) if held else None
    per = blocks[0].shape[0] // CLUS_DEV
    me = lax.axis_index("clus")
    core = lax.axis_index("blk")
    spans = list(zip(cuts, cuts[1:]))
    base = spans[first][0]
    if held:
        best[:, :base] = before[:, :base]
    best[:, base:] = jnp.full((CLUS_DEV, best.shape[1] - base), -1.0, F32)
    for c in range(CLUS_DEV):
        rows = [best.at[c : c + 1, a:b] for a, b in spans]
        groups = []
        for stage in stages:
            start = spans[len(groups)][0]
            end = start + stage.shape[2]
            while len(groups) < first and spans[len(groups)][0] < end:
                a, b = spans[len(groups)]
                groups.append(stage.at[core, c, a - start : b - start])
        for i in range(first, len(spans)):
            a, b = spans[i]
            group = send.at[1, c, a - base : b - base]
            gather_group(blocks[(a - base) // per : (b - base) // per], c, group, me)
            groups.append(group)
            raise_best(rows[i], group, group, True)
            for j in range(i):
                score_pair(rows, groups, i, j, bits[j], me)
        send[0, c] = send[1, c]


def cross_stage(cuts, held, *refs):
    stages, before, best = refs[: held + 1], refs[held + 1], refs[held + 2]
    best[...] = before[...]

    @pl.when(lax.axis_index("blk") == 1)
    def _():
        new = stages[-1]
        for c in range(CLUS_DEV):
            base = 0
            for stage in stages:
                end = base + stage.shape[2]
                raise_best(best.at[c : c + 1, base:end], new.at[0, c], stage.at[1, c])
                base = end
            start = base - new.shape[2]
            for stage in stages[:-1]:
                raise_best(best.at[c : c + 1, start:base], stage.at[0, c], new.at[1, c])


def filled_queries(rows):
    ones = jnp.ones((8, LANES), BF)
    return matmul(ones, rows[:, :LANES], ((1,), (1,)))[:1] < 100.0


def cross_last(cuts, held, *refs):
    stages, (send, before), refs = refs[:held], refs[held : held + 2], refs[held + 2 :]
    others, (out, keys, best) = refs[:-3], refs[-3:]
    per = others[0].shape[0] // CLUS_DEV
    me = lax.axis_index("clus")
    core = lax.axis_index("blk")
    best[...] = before[...]
    start = best.shape[1] - send.shape[2]

    @pl.when(core == 1)
    def _():
        for c in range(CLUS_DEV):
            for i, other in enumerate(others):
                keys[i * per : (i + 1) * per, :] = other[c * per : (c + 1) * per, :]
            base = 0
            for stage in stages:
                end = base + stage.shape[2]
                raise_best(best.at[c : c + 1, base:end], keys, stage.at[1, c])
                raise_best(best.at[c : c + 1, start:], stage.at[0, c], send.at[1, c])
                base = end
            raise_best(best.at[c : c + 1, start:], keys, send.at[1, c])

    for c in range(CLUS_DEV):
        whole = [(stage.shape[2], stage.at[core, c]) for stage in stages]
        whole.append((send.shape[2], send.at[1, c]))
        base = 0
        for size, rows in whole:
            kept = jnp.where(filled_queries(rows), best[c : c + 1, base : base + size], F32(0.0))
            for a, b in zip(cuts, cuts[1:]):
                if base <= a < base + size:
                    place = (me ^ (a // per)) & ~((b - a) // per - 1)
                    at = pl.ds(pl.multiple_of(place * per, LANES), b - a)
                    out[c : c + 1, at] = kept[:, a - base : b - base]
            base += size


def local(embeddings, cluster_ids):
    owners = lax.axis_size("clus")
    clusters = CLUS_DEV * owners
    rows, width = embeddings.shape
    per = 2 * rows // clusters
    bits = [owners // 2, owners // 4, owners // 8]
    bounds = [0, owners // 2, owners // 2 + owners // 4, owners - owners // 8, owners]
    cuts = [x * per for x in bounds]
    near, far1, far2, far3 = [list(range(a, b)) for a, b in zip(bounds, bounds[1:])]
    best_shape = jax.ShapeDtypeStruct((CLUS_DEV, rows), F32)

    def to_owner(block, step):
        return lax.ppermute(block, "clus", [(i, i ^ step) for i in range(owners)])

    def stage_shape(sources):
        return jax.ShapeDtypeStruct((2, CLUS_DEV, sources * per, width), BF)

    def to_both(send):
        return lax.all_to_all(send, "blk", split_axis=0, concat_axis=0, tiled=True)

    arrived = {}
    lead = [near[-1], far1[0]]
    unit, tgt, *packed = call_pack_first(embeddings, cluster_ids, lead, clusters, per)
    for steps in (near[1:-1] + far1[1:] + [0], []):
        for step, block in zip(lead, packed):
            arrived[step] = to_owner(block, step) if step else block
        lead, packed = steps, call_pack_rest(unit, tgt, steps, per) if steps else []
    packed = call_pack_rest(unit, tgt, far2 + far3, per)
    for steps, gate in ((far2, near[-1]), (far3, far1[0])):
        *held, arrived[gate] = lax.optimization_barrier(
            (*packed[: len(steps)], arrived[gate])
        )
        packed = packed[len(steps) :]
        for step, block in zip(steps, held):
            arrived[step] = to_owner(block, step)

    early = near + far1
    send, best = kernel_call(
        functools.partial(own_stage, cuts[:3], bits, 0, 0),
        [stage_shape(len(early)), best_shape],
        [arrived[s] for s in early],
        "own_early",
    )
    stages = [to_both(send)]
    (best,) = kernel_call(
        functools.partial(cross_stage, cuts, 0), [best_shape], stages + [best], "cross_early"
    )
    *new, best = lax.optimization_barrier((*[arrived[s] for s in far2], best))
    send, best = kernel_call(
        functools.partial(own_stage, cuts[:4], bits, 1, 2),
        [stage_shape(len(far2)), best_shape],
        stages + [best] + new,
        "own_middle",
    )
    stages.append(to_both(send))
    (best,) = kernel_call(
        functools.partial(cross_stage, cuts, 1), [best_shape], stages + [best], "cross_middle"
    )
    *new, best = lax.optimization_barrier((*[arrived[s] for s in far3], best))
    send, best = kernel_call(
        functools.partial(own_stage, cuts, bits, 2, 3),
        [stage_shape(len(far3)), best_shape],
        stages + [best] + new,
        "own_last",
    )
    others = [lax.ppermute(block, "blk", [(0, 1)]) for block in new]
    (out,) = kernel_call(
        functools.partial(cross_last, cuts, 2),
        [best_shape],
        stages + [send, best] + others,
        "cross_last",
        [pltpu.VMEM((len(far3) * per, width), BF), pltpu.VMEM((CLUS_DEV, rows), F32)],
    )
    return out


def solution(mesh):
    placed = (P(("groups", "clus", "blk"), None), P(("groups", "clus", "blk"), None))
    return jax.shard_map(
        local, mesh=mesh, in_specs=placed, out_specs=P(("groups", "clus"), "blk"), check_vma=False
    )
```

```python
import functools

import jax
import jax.numpy as jnp
from jax import lax
from jax.experimental import pallas as pl
from jax.experimental.pallas import tpu as pltpu
from jax.sharding import PartitionSpec as P

CLUS_DEV = 2
LANES = 128
MARK = 2.0
BF = jnp.bfloat16
F32 = jnp.float32


def iota(shape, dim):
    return lax.broadcasted_iota(jnp.int32, shape, dim)


def matmul(a, b, contract):
    return lax.dot_general(a, b, (contract, ((), ())), preferred_element_type=F32)


def targets(ids, clusters, per_source):
    groups = ids.shape[1] // LANES
    parts = [ids[:, g * LANES : (g + 1) * LANES] for g in range(groups)]
    hot = jnp.concatenate(
        [(iota((clusters, LANES), 0) == part).astype(F32) for part in parts], axis=0
    )
    stacked = groups * clusters
    earlier = (iota((LANES, LANES), 0) < iota((LANES, LANES), 1)).astype(F32).astype(BF)
    within = matmul(hot.astype(BF), earlier, ((1,), (0,)))
    totals = jnp.broadcast_to(jnp.sum(hot, axis=1, keepdims=True), (stacked, LANES))
    a, b = iota((stacked, stacked), 0), iota((stacked, stacked), 1)
    chunks_before = ((a % clusters == b % clusters) & (b < a)).astype(F32).astype(BF)
    before = within + matmul(chunks_before, totals.astype(BF), ((1,), (0,)))
    picked = hot * before
    out = [
        jnp.sum(picked[g * clusters : (g + 1) * clusters], axis=0, keepdims=True).astype(jnp.int32)
        + parts[g] * per_source
        for g in range(groups)
    ]
    return jnp.concatenate(out, axis=1)


def pack_block(unit, tgt, dest, width):
    hit = (tgt - dest * width) == iota((width, tgt.shape[1]), 0)
    hot = hit.astype(F32)
    rows = matmul(hot.astype(BF), unit, ((1,), (0,)))
    empty = jnp.max(hot, axis=1, keepdims=True) < 0.5
    head = jnp.where(empty, F32(MARK), rows[:, :LANES])
    return head.astype(BF), rows[:, LANES:].astype(BF)


def store_blocks(unit, tgt, steps, width, outs):
    me = lax.axis_index("clus")
    for step, out in zip(steps, outs):
        head, tail = pack_block(unit, tgt, me ^ step, width)
        out[:, :LANES] = head
        out[:, LANES:] = tail


PIECES = 4


def pack_first(steps, clusters, per_source, emb, ids, unit, tgt, *refs):
    outs, (raw, raw_ids, sems, ids_sem) = refs[:-4], refs[-4:]
    size = emb.shape[0] // PIECES
    ids_copy = pltpu.make_async_copy(ids, raw_ids, ids_sem)
    ids_copy.start()
    windows = [pl.ds(piece * size, size) for piece in range(PIECES)]
    copies = [
        pltpu.make_async_copy(emb.at[window], raw.at[window], sems.at[piece])
        for piece, window in enumerate(windows)
    ]
    for copy in copies:
        copy.start()
    ids_copy.wait()
    tgt[...] = targets(raw_ids[...], clusters, per_source)
    for copy, window in zip(copies, windows):
        copy.wait()
        values = raw[window, :].astype(F32)
        scale = lax.rsqrt(jnp.sum(values * values, axis=1, keepdims=True) + 1e-6)
        unit[window, :] = (values * scale).astype(BF)
    store_blocks(unit[...], tgt[...], steps, CLUS_DEV * per_source, outs)


def pack_rest(steps, per_source, unit, tgt, *outs):
    store_blocks(unit[...], tgt[...], steps, CLUS_DEV * per_source, outs)


VMEM = pl.BlockSpec(memory_space=pltpu.VMEM)


def kernel_call(kernel, shapes, inputs, name, scratch=(), inputs_in=VMEM):
    return pl.pallas_call(
        kernel,
        out_shape=shapes,
        in_specs=[inputs_in] * len(inputs),
        out_specs=[VMEM] * len(shapes),
        scratch_shapes=scratch,
        compiler_params=pltpu.CompilerParams(vmem_limit_bytes=20 * 2**20),
        cost_estimate=pl.CostEstimate(flops=1000, bytes_accessed=1000, transcendentals=0),
        name=name,
    )(*inputs)


def call_pack_first(emb, ids, steps, clusters, per_source):
    block = jax.ShapeDtypeStruct((CLUS_DEV * per_source, emb.shape[1]), BF)
    shapes = [jax.ShapeDtypeStruct(emb.shape, BF), jax.ShapeDtypeStruct(ids.shape, jnp.int32)]
    return kernel_call(
        functools.partial(pack_first, steps, clusters, per_source),
        shapes + [block] * len(steps),
        [emb, ids],
        inputs_in=pl.BlockSpec(memory_space=pltpu.HBM),
        name="pack_first",
        scratch=[
            pltpu.VMEM(emb.shape, BF),
            pltpu.VMEM(ids.shape, jnp.int32),
            pltpu.SemaphoreType.DMA((PIECES,)),
            pltpu.SemaphoreType.DMA,
        ],
    )


def call_pack_rest(unit, tgt, steps, per_source):
    block = jax.ShapeDtypeStruct((CLUS_DEV * per_source, unit.shape[1]), BF)
    return kernel_call(
        functools.partial(pack_rest, steps, per_source),
        [block] * len(steps),
        [unit, tgt],
        "pack_rest",
    )


CHUNK = 256


def raise_best(best, keys, queries, triangular=False):
    rows = queries.shape[0]
    for start in range(0, rows, CHUNK):
        chunk = min(CHUNK, rows - start)
        count = start + chunk if triangular else keys.shape[0]
        sims = matmul(keys[:count, :], queries[start : start + chunk, :], ((1,), (1,)))
        filled = keys[:count, :LANES].astype(F32) < 1.5
        for first in range(0, chunk, LANES):
            allowed = filled
            if triangular:
                allowed = filled & (
                    iota((count, LANES), 0) < iota((count, LANES), 1) + (start + first)
                )
            part = jnp.where(allowed, sims[:, first : first + LANES], F32(-1.0))
            window = slice(start + first, start + first + LANES)
            best[:, window] = jnp.maximum(best[:, window], jnp.max(part, axis=0, keepdims=True))


def gather_group(blocks, cluster, out, me):
    per = blocks[0].shape[0] // CLUS_DEV
    for step, block in enumerate(blocks):
        place = (me & (len(blocks) - 1)) ^ step
        rows = pl.ds(pl.multiple_of(place * per, per), per)
        out[rows, :] = block[cluster * per : (cluster + 1) * per, :]


def score_pair(bests, groups, new, old, bit, me):
    later = (me & bit) == 0

    @pl.when(later)
    def _():
        raise_best(bests[new], groups[old], groups[new])

    @pl.when(jnp.logical_not(later))
    def _():
        raise_best(bests[old], groups[new], groups[old])


def own_stage(cuts, bits, held, first, *refs):
    stages, refs = refs[:held], refs[held:]
    blocks, (send, best) = list(refs[:-2]), refs[-2:]
    before = blocks.pop(0) if held else None
    per = blocks[0].shape[0] // CLUS_DEV
    me = lax.axis_index("clus")
    core = lax.axis_index("blk")
    spans = list(zip(cuts, cuts[1:]))
    base = spans[first][0]
    if held:
        best[:, :base] = before[:, :base]
    best[:, base:] = jnp.full((CLUS_DEV, best.shape[1] - base), -1.0, F32)
    for c in range(CLUS_DEV):
        rows = [best.at[c : c + 1, a:b] for a, b in spans]
        groups = []
        for stage in stages:
            start = spans[len(groups)][0]
            end = start + stage.shape[2]
            while len(groups) < first and spans[len(groups)][0] < end:
                a, b = spans[len(groups)]
                groups.append(stage.at[core, c, a - start : b - start])
        for i in range(first, len(spans)):
            a, b = spans[i]
            group = send.at[1, c, a - base : b - base]
            gather_group(blocks[(a - base) // per : (b - base) // per], c, group, me)
            groups.append(group)
            raise_best(rows[i], group, group, True)
            for j in range(i):
                score_pair(rows, groups, i, j, bits[j], me)
        send[0, c] = send[1, c]


def cross_stage(cuts, held, *refs):
    stages, before, best = refs[: held + 1], refs[held + 1], refs[held + 2]
    best[...] = before[...]

    @pl.when(lax.axis_index("blk") == 1)
    def _():
        new = stages[-1]
        for c in range(CLUS_DEV):
            base = 0
            for stage in stages:
                end = base + stage.shape[2]
                raise_best(best.at[c : c + 1, base:end], new.at[0, c], stage.at[1, c])
                base = end
            start = base - new.shape[2]
            for stage in stages[:-1]:
                raise_best(best.at[c : c + 1, start:base], stage.at[0, c], new.at[1, c])


def filled_queries(rows):
    ones = jnp.ones((8, LANES), BF)
    return matmul(ones, rows[:, :LANES], ((1,), (1,)))[:1] < 100.0


def cross_last(cuts, held, *refs):
    stages, (send, before), refs = refs[:held], refs[held : held + 2], refs[held + 2 :]
    others, (out, keys, best) = refs[:-3], refs[-3:]
    per = others[0].shape[0] // CLUS_DEV
    me = lax.axis_index("clus")
    core = lax.axis_index("blk")
    best[...] = before[...]
    start = best.shape[1] - send.shape[2]

    @pl.when(core == 1)
    def _():
        for c in range(CLUS_DEV):
            for i, other in enumerate(others):
                keys[i * per : (i + 1) * per, :] = other[c * per : (c + 1) * per, :]
            base = 0
            for stage in stages:
                end = base + stage.shape[2]
                raise_best(best.at[c : c + 1, base:end], keys, stage.at[1, c])
                raise_best(best.at[c : c + 1, start:], stage.at[0, c], send.at[1, c])
                base = end
            raise_best(best.at[c : c + 1, start:], keys, send.at[1, c])

    for c in range(CLUS_DEV):
        whole = [(stage.shape[2], stage.at[core, c]) for stage in stages]
        whole.append((send.shape[2], send.at[1, c]))
        base = 0
        for size, rows in whole:
            kept = jnp.where(filled_queries(rows), best[c : c + 1, base : base + size], F32(0.0))
            for a, b in zip(cuts, cuts[1:]):
                if base <= a < base + size:
                    place = (me ^ (a // per)) & ~((b - a) // per - 1)
                    at = pl.ds(pl.multiple_of(place * per, LANES), b - a)
                    out[c : c + 1, at] = kept[:, a - base : b - base]
            base += size


def local(embeddings, cluster_ids):
    owners = lax.axis_size("clus")
    clusters = CLUS_DEV * owners
    rows, width = embeddings.shape
    per = 2 * rows // clusters
    bits = [owners // 2, owners // 4, owners // 8]
    bounds = [0, owners // 2, owners // 2 + owners // 4, owners - owners // 8, owners]
    cuts = [x * per for x in bounds]
    near, far1, far2, far3 = [list(range(a, b)) for a, b in zip(bounds, bounds[1:])]
    best_shape = jax.ShapeDtypeStruct((CLUS_DEV, rows), F32)

    def to_owner(block, step):
        return lax.ppermute(block, "clus", [(i, i ^ step) for i in range(owners)])

    def stage_shape(sources):
        return jax.ShapeDtypeStruct((2, CLUS_DEV, sources * per, width), BF)

    def to_both(send):
        return lax.all_to_all(send, "blk", split_axis=0, concat_axis=0, tiled=True)

    arrived = {}
    lead = [near[-1], far1[0]]
    unit, tgt, *packed = call_pack_first(embeddings, cluster_ids, lead, clusters, per)
    for steps in (near[1:-1] + far1[1:] + [0], []):
        for step, block in zip(lead, packed):
            arrived[step] = to_owner(block, step) if step else block
        lead, packed = steps, call_pack_rest(unit, tgt, steps, per) if steps else []
    packed = call_pack_rest(unit, tgt, far2 + far3, per)
    for steps, gate in ((far2, near[-1]), (far3, far1[-1])):
        *held, arrived[gate] = lax.optimization_barrier(
            (*packed[: len(steps)], arrived[gate])
        )
        packed = packed[len(steps) :]
        for step, block in zip(steps, held):
            arrived[step] = to_owner(block, step)

    early = near + far1
    send, best = kernel_call(
        functools.partial(own_stage, cuts[:3], bits, 0, 0),
        [stage_shape(len(early)), best_shape],
        [arrived[s] for s in early],
        "own_early",
    )
    stages = [to_both(send)]
    (best,) = kernel_call(
        functools.partial(cross_stage, cuts, 0), [best_shape], stages + [best], "cross_early"
    )
    *new, best = lax.optimization_barrier((*[arrived[s] for s in far2], best))
    send, best = kernel_call(
        functools.partial(own_stage, cuts[:4], bits, 1, 2),
        [stage_shape(len(far2)), best_shape],
        stages + [best] + new,
        "own_middle",
    )
    stages.append(to_both(send))
    (best,) = kernel_call(
        functools.partial(cross_stage, cuts, 1), [best_shape], stages + [best], "cross_middle"
    )
    *new, best = lax.optimization_barrier((*[arrived[s] for s in far3], best))
    send, best = kernel_call(
        functools.partial(own_stage, cuts, bits, 2, 3),
        [stage_shape(len(far3)), best_shape],
        stages + [best] + new,
        "own_last",
    )
    others = [lax.ppermute(block, "blk", [(0, 1)]) for block in new]
    (out,) = kernel_call(
        functools.partial(cross_last, cuts, 2),
        [best_shape],
        stages + [send, best] + others,
        "cross_last",
        [pltpu.VMEM((len(far3) * per, width), BF), pltpu.VMEM((CLUS_DEV, rows), F32)],
    )
    return out


def solution(mesh):
    placed = (P(("groups", "clus", "blk"), None), P(("groups", "clus", "blk"), None))
    return jax.shard_map(
        local, mesh=mesh, in_specs=placed, out_specs=P(("groups", "clus"), "blk"), check_vma=False
    )
```

```python
import functools

import jax
import jax.numpy as jnp
from jax import lax
from jax.experimental import pallas as pl
from jax.experimental.pallas import tpu as pltpu
from jax.sharding import PartitionSpec as P

CLUS_DEV = 2
LANES = 128
MARK = 2.0
BF = jnp.bfloat16
F32 = jnp.float32


def iota(shape, dim):
    return lax.broadcasted_iota(jnp.int32, shape, dim)


def matmul(a, b, contract):
    return lax.dot_general(a, b, (contract, ((), ())), preferred_element_type=F32)


def targets(ids, clusters, per_source):
    groups = ids.shape[1] // LANES
    parts = [ids[:, g * LANES : (g + 1) * LANES] for g in range(groups)]
    hot = jnp.concatenate(
        [(iota((clusters, LANES), 0) == part).astype(F32) for part in parts], axis=0
    )
    stacked = groups * clusters
    earlier = (iota((LANES, LANES), 0) < iota((LANES, LANES), 1)).astype(F32).astype(BF)
    within = matmul(hot.astype(BF), earlier, ((1,), (0,)))
    totals = jnp.broadcast_to(jnp.sum(hot, axis=1, keepdims=True), (stacked, LANES))
    a, b = iota((stacked, stacked), 0), iota((stacked, stacked), 1)
    chunks_before = ((a % clusters == b % clusters) & (b < a)).astype(F32).astype(BF)
    before = within + matmul(chunks_before, totals.astype(BF), ((1,), (0,)))
    picked = hot * before
    out = [
        jnp.sum(picked[g * clusters : (g + 1) * clusters], axis=0, keepdims=True).astype(jnp.int32)
        + parts[g] * per_source
        for g in range(groups)
    ]
    return jnp.concatenate(out, axis=1)


def pack_block(unit, tgt, dest, width):
    hit = (tgt - dest * width) == iota((width, tgt.shape[1]), 0)
    hot = hit.astype(F32)
    rows = matmul(hot.astype(BF), unit, ((1,), (0,)))
    empty = jnp.max(hot, axis=1, keepdims=True) < 0.5
    head = jnp.where(empty, F32(MARK), rows[:, :LANES])
    return head.astype(BF), rows[:, LANES:].astype(BF)


def store_blocks(unit, tgt, steps, width, outs):
    me = lax.axis_index("clus")
    for step, out in zip(steps, outs):
        head, tail = pack_block(unit, tgt, me ^ step, width)
        out[:, :LANES] = head
        out[:, LANES:] = tail


def pack_first(steps, clusters, per_source, emb, ids, unit, tgt, *outs):
    values = emb[...].astype(F32)
    scale = lax.rsqrt(jnp.sum(values * values, axis=1, keepdims=True) + 1e-6)
    unit[...] = (values * scale).astype(BF)
    tgt[...] = targets(ids[...], clusters, per_source)
    store_blocks(unit[...], tgt[...], steps, CLUS_DEV * per_source, outs)


def pack_rest(steps, per_source, unit, tgt, *outs):
    store_blocks(unit[...], tgt[...], steps, CLUS_DEV * per_source, outs)


VMEM = pl.BlockSpec(memory_space=pltpu.VMEM)


def kernel_call(kernel, shapes, inputs, name, scratch=()):
    return pl.pallas_call(
        kernel,
        out_shape=shapes,
        in_specs=[VMEM] * len(inputs),
        out_specs=[VMEM] * len(shapes),
        scratch_shapes=scratch,
        compiler_params=pltpu.CompilerParams(vmem_limit_bytes=20 * 2**20),
        cost_estimate=pl.CostEstimate(flops=1000, bytes_accessed=1000, transcendentals=0),
        name=name,
    )(*inputs)


def call_pack_first(emb, ids, steps, clusters, per_source):
    block = jax.ShapeDtypeStruct((CLUS_DEV * per_source, emb.shape[1]), BF)
    shapes = [jax.ShapeDtypeStruct(emb.shape, BF), jax.ShapeDtypeStruct(ids.shape, jnp.int32)]
    return kernel_call(
        functools.partial(pack_first, steps, clusters, per_source),
        shapes + [block] * len(steps),
        [emb, ids],
        "pack_first",
    )


def call_pack_rest(unit, tgt, steps, per_source):
    block = jax.ShapeDtypeStruct((CLUS_DEV * per_source, unit.shape[1]), BF)
    return kernel_call(
        functools.partial(pack_rest, steps, per_source),
        [block] * len(steps),
        [unit, tgt],
        "pack_rest",
    )


CHUNK = 256


def raise_best(best, keys, queries, triangular=False):
    rows = queries.shape[0]
    for start in range(0, rows, CHUNK):
        chunk = min(CHUNK, rows - start)
        count = start + chunk if triangular else keys.shape[0]
        sims = matmul(keys[:count, :], queries[start : start + chunk, :], ((1,), (1,)))
        filled = keys[:count, :LANES].astype(F32) < 1.5
        for first in range(0, chunk, LANES):
            allowed = filled
            if triangular:
                allowed = filled & (
                    iota((count, LANES), 0) < iota((count, LANES), 1) + (start + first)
                )
            part = jnp.where(allowed, sims[:, first : first + LANES], F32(-1.0))
            window = slice(start + first, start + first + LANES)
            best[:, window] = jnp.maximum(best[:, window], jnp.max(part, axis=0, keepdims=True))


def gather_group(blocks, cluster, out, me):
    per = blocks[0].shape[0] // CLUS_DEV
    for step, block in enumerate(blocks):
        place = (me & (len(blocks) - 1)) ^ step
        rows = pl.ds(pl.multiple_of(place * per, per), per)
        out[rows, :] = block[cluster * per : (cluster + 1) * per, :]


def score_pair(bests, groups, new, old, bit, me):
    later = (me & bit) == 0

    @pl.when(later)
    def _():
        raise_best(bests[new], groups[old], groups[new])

    @pl.when(jnp.logical_not(later))
    def _():
        raise_best(bests[old], groups[new], groups[old])


def own_stage(cuts, bits, held, first, *refs):
    stages, refs = refs[:held], refs[held:]
    blocks, (send, best) = list(refs[:-2]), refs[-2:]
    before = blocks.pop(0) if held else None
    per = blocks[0].shape[0] // CLUS_DEV
    me = lax.axis_index("clus")
    core = lax.axis_index("blk")
    spans = list(zip(cuts, cuts[1:]))
    base = spans[first][0]
    if held:
        best[:, :base] = before[:, :base]
    best[:, base:] = jnp.full((CLUS_DEV, best.shape[1] - base), -1.0, F32)
    for c in range(CLUS_DEV):
        rows = [best.at[c : c + 1, a:b] for a, b in spans]
        groups = []
        for stage in stages:
            start = spans[len(groups)][0]
            end = start + stage.shape[2]
            while len(groups) < first and spans[len(groups)][0] < end:
                a, b = spans[len(groups)]
                groups.append(stage.at[core, c, a - start : b - start])
        for i in range(first, len(spans)):
            a, b = spans[i]
            group = send.at[1, c, a - base : b - base]
            gather_group(blocks[(a - base) // per : (b - base) // per], c, group, me)
            groups.append(group)
            raise_best(rows[i], group, group, True)
            for j in range(i):
                score_pair(rows, groups, i, j, bits[j], me)
        send[0, c] = send[1, c]


def cross_stage(cuts, held, *refs):
    stages, before, best = refs[: held + 1], refs[held + 1], refs[held + 2]
    best[...] = before[...]

    @pl.when(lax.axis_index("blk") == 1)
    def _():
        new = stages[-1]
        for c in range(CLUS_DEV):
            base = 0
            for stage in stages:
                end = base + stage.shape[2]
                raise_best(best.at[c : c + 1, base:end], new.at[0, c], stage.at[1, c])
                base = end
            start = base - new.shape[2]
            for stage in stages[:-1]:
                raise_best(best.at[c : c + 1, start:base], stage.at[0, c], new.at[1, c])


def filled_queries(rows):
    ones = jnp.ones((8, LANES), BF)
    return matmul(ones, rows[:, :LANES], ((1,), (1,)))[:1] < 100.0


def cross_last(cuts, held, *refs):
    stages, (send, before), refs = refs[:held], refs[held : held + 2], refs[held + 2 :]
    others, (out, keys, best) = refs[:-3], refs[-3:]
    per = others[0].shape[0] // CLUS_DEV
    me = lax.axis_index("clus")
    core = lax.axis_index("blk")
    best[...] = before[...]
    start = best.shape[1] - send.shape[2]

    @pl.when(core == 1)
    def _():
        for c in range(CLUS_DEV):
            for i, other in enumerate(others):
                keys[i * per : (i + 1) * per, :] = other[c * per : (c + 1) * per, :]
            base = 0
            for stage in stages:
                end = base + stage.shape[2]
                raise_best(best.at[c : c + 1, base:end], keys, stage.at[1, c])
                raise_best(best.at[c : c + 1, start:], stage.at[0, c], send.at[1, c])
                base = end
            raise_best(best.at[c : c + 1, start:], keys, send.at[1, c])

    for c in range(CLUS_DEV):
        whole = [(stage.shape[2], stage.at[core, c]) for stage in stages]
        whole.append((send.shape[2], send.at[1, c]))
        base = 0
        for size, rows in whole:
            kept = jnp.where(filled_queries(rows), best[c : c + 1, base : base + size], F32(0.0))
            for a, b in zip(cuts, cuts[1:]):
                if base <= a < base + size:
                    place = (me ^ (a // per)) & ~((b - a) // per - 1)
                    at = pl.ds(pl.multiple_of(place * per, LANES), b - a)
                    out[c : c + 1, at] = kept[:, a - base : b - base]
            base += size


def local(embeddings, cluster_ids):
    owners = lax.axis_size("clus")
    clusters = CLUS_DEV * owners
    rows, width = embeddings.shape
    per = 2 * rows // clusters
    bits = [owners // 2, owners // 4, owners // 8]
    bounds = [0, owners // 2, owners // 2 + owners // 4, owners - owners // 8, owners]
    cuts = [x * per for x in bounds]
    near, far1, far2, far3 = [list(range(a, b)) for a, b in zip(bounds, bounds[1:])]
    best_shape = jax.ShapeDtypeStruct((CLUS_DEV, rows), F32)

    def to_owner(block, step):
        return lax.ppermute(block, "clus", [(i, i ^ step) for i in range(owners)])

    def stage_shape(sources):
        return jax.ShapeDtypeStruct((2, CLUS_DEV, sources * per, width), BF)

    def to_both(send):
        return lax.all_to_all(send, "blk", split_axis=0, concat_axis=0, tiled=True)

    arrived = {}
    lead = far1
    unit, tgt, *packed = call_pack_first(embeddings, cluster_ids, lead, clusters, per)
    for steps in (near[1:] + [0], []):
        for step, block in zip(lead, packed):
            arrived[step] = to_owner(block, step) if step else block
        lead, packed = steps, call_pack_rest(unit, tgt, steps, per) if steps else []
    packed = call_pack_rest(unit, tgt, far2 + far3, per)
    for steps, gate in ((far2, far1[0]), (far3, far1[-1])):
        *held, arrived[gate] = lax.optimization_barrier(
            (*packed[: len(steps)], arrived[gate])
        )
        packed = packed[len(steps) :]
        for step, block in zip(steps, held):
            arrived[step] = to_owner(block, step)

    early = near + far1
    send, best = kernel_call(
        functools.partial(own_stage, cuts[:3], bits, 0, 0),
        [stage_shape(len(early)), best_shape],
        [arrived[s] for s in early],
        "own_early",
    )
    stages = [to_both(send)]
    (best,) = kernel_call(
        functools.partial(cross_stage, cuts, 0), [best_shape], stages + [best], "cross_early"
    )
    *new, best = lax.optimization_barrier((*[arrived[s] for s in far2], best))
    send, best = kernel_call(
        functools.partial(own_stage, cuts[:4], bits, 1, 2),
        [stage_shape(len(far2)), best_shape],
        stages + [best] + new,
        "own_middle",
    )
    stages.append(to_both(send))
    (best,) = kernel_call(
        functools.partial(cross_stage, cuts, 1), [best_shape], stages + [best], "cross_middle"
    )
    *new, best = lax.optimization_barrier((*[arrived[s] for s in far3], best))
    send, best = kernel_call(
        functools.partial(own_stage, cuts, bits, 2, 3),
        [stage_shape(len(far3)), best_shape],
        stages + [best] + new,
        "own_last",
    )
    others = [lax.ppermute(block, "blk", [(0, 1)]) for block in new]
    (out,) = kernel_call(
        functools.partial(cross_last, cuts, 2),
        [best_shape],
        stages + [send, best] + others,
        "cross_last",
        [pltpu.VMEM((len(far3) * per, width), BF), pltpu.VMEM((CLUS_DEV, rows), F32)],
    )
    return out


def solution(mesh):
    placed = (P(("groups", "clus", "blk"), None), P(("groups", "clus", "blk"), None))
    return jax.shard_map(
        local, mesh=mesh, in_specs=placed, out_specs=P(("groups", "clus"), "blk"), check_vma=False
    )
```

```python
import functools

import jax
import jax.numpy as jnp
from jax import lax
from jax.experimental import pallas as pl
from jax.experimental.pallas import tpu as pltpu
from jax.sharding import PartitionSpec as P

CLUS_DEV = 2
LANES = 128
MARK = 2.0
BF = jnp.bfloat16
F32 = jnp.float32


def iota(shape, dim):
    return lax.broadcasted_iota(jnp.int32, shape, dim)


def matmul(a, b, contract):
    return lax.dot_general(a, b, (contract, ((), ())), preferred_element_type=F32)


def targets(ids, clusters, per_source):
    groups = ids.shape[1] // LANES
    parts = [ids[:, g * LANES : (g + 1) * LANES] for g in range(groups)]
    hot = jnp.concatenate(
        [(iota((clusters, LANES), 0) == part).astype(F32) for part in parts], axis=0
    )
    stacked = groups * clusters
    earlier = (iota((LANES, LANES), 0) < iota((LANES, LANES), 1)).astype(F32).astype(BF)
    within = matmul(hot.astype(BF), earlier, ((1,), (0,)))
    totals = jnp.broadcast_to(jnp.sum(hot, axis=1, keepdims=True), (stacked, LANES))
    a, b = iota((stacked, stacked), 0), iota((stacked, stacked), 1)
    chunks_before = ((a % clusters == b % clusters) & (b < a)).astype(F32).astype(BF)
    before = within + matmul(chunks_before, totals.astype(BF), ((1,), (0,)))
    picked = hot * before
    out = [
        jnp.sum(picked[g * clusters : (g + 1) * clusters], axis=0, keepdims=True).astype(jnp.int32)
        + parts[g] * per_source
        for g in range(groups)
    ]
    return jnp.concatenate(out, axis=1)


def store_blocks(unit, tgt, picks, outs):
    me = lax.axis_index("clus")
    per = outs[0].shape[0]
    hits = [
        (tgt - ((me ^ step) * CLUS_DEV + cluster) * per == iota((per, tgt.shape[1]), 0)).astype(F32)
        for step, cluster in picks
    ]
    hot = jnp.concatenate(hits, axis=0) if len(hits) > 1 else hits[0]
    rows = matmul(hot.astype(BF), unit, ((1,), (0,)))
    empty = jnp.max(hot, axis=1, keepdims=True) < 0.5
    marked = jnp.where(empty, F32(MARK), rows[:, :LANES])
    for k, out in enumerate(outs):
        window = slice(k * per, (k + 1) * per)
        out[:, :LANES] = marked[window].astype(BF)
        out[:, LANES:] = rows[window, LANES:].astype(BF)


def pack_first(picks, clusters, emb, ids, unit, tgt, *outs):
    values = emb[...].astype(F32)
    scale = lax.rsqrt(jnp.sum(values * values, axis=1, keepdims=True) + 1e-6)
    unit[...] = (values * scale).astype(BF)
    tgt[...] = targets(ids[...], clusters, outs[0].shape[0])
    store_blocks(unit[...], tgt[...], picks, outs)


def pack_rest(picks, unit, tgt, *outs):
    store_blocks(unit[...], tgt[...], picks, outs)


VMEM = pl.BlockSpec(memory_space=pltpu.VMEM)


def kernel_call(kernel, shapes, inputs, name, scratch=()):
    return pl.pallas_call(
        kernel,
        out_shape=shapes,
        in_specs=[VMEM] * len(inputs),
        out_specs=[VMEM] * len(shapes),
        scratch_shapes=scratch,
        compiler_params=pltpu.CompilerParams(vmem_limit_bytes=20 * 2**20),
        cost_estimate=pl.CostEstimate(flops=1000, bytes_accessed=1000, transcendentals=0),
        name=name,
    )(*inputs)


CHUNK = 256


def raise_best(best, keys, queries, triangular=False):
    rows = queries.shape[0]
    for start in range(0, rows, CHUNK):
        chunk = min(CHUNK, rows - start)
        count = start + chunk if triangular else keys.shape[0]
        sims = matmul(keys[:count, :], queries[start : start + chunk, :], ((1,), (1,)))
        filled = keys[:count, :LANES].astype(F32) < 1.5
        for first in range(0, chunk, LANES):
            allowed = filled
            if triangular:
                allowed = filled & (
                    iota((count, LANES), 0) < iota((count, LANES), 1) + (start + first)
                )
            part = jnp.where(allowed, sims[:, first : first + LANES], F32(-1.0))
            window = slice(start + first, start + first + LANES)
            best[:, window] = jnp.maximum(best[:, window], jnp.max(part, axis=0, keepdims=True))


def gather_group(blocks, out, me):
    per = blocks[0].shape[0]
    for step, block in enumerate(blocks):
        place = (me & (len(blocks) - 1)) ^ step
        out[pl.ds(pl.multiple_of(place * per, per), per), :] = block[...]


def score_pair(bests, groups, new, old, bit, me):
    later = (me & bit) == 0

    @pl.when(later)
    def _():
        raise_best(bests[new], groups[old], groups[new])

    @pl.when(jnp.logical_not(later))
    def _():
        raise_best(bests[old], groups[new], groups[old])


def own_stage(cuts, bits, held, first, *refs):
    stages, refs = refs[:held], refs[held:]
    blocks, (send, best) = list(refs[:-2]), refs[-2:]
    before = blocks.pop(0) if held else None
    per = blocks[0].shape[0]
    me = lax.axis_index("clus")
    core = lax.axis_index("blk")
    spans = list(zip(cuts, cuts[1:]))
    base = spans[first][0]
    if held:
        best[:, :base] = before[:, :base]
    best[:, base:] = jnp.full((1, best.shape[1] - base), -1.0, F32)
    rows = [best.at[:, a:b] for a, b in spans]
    groups = []
    for stage in stages:
        start = spans[len(groups)][0]
        end = start + stage.shape[1]
        while len(groups) < first and spans[len(groups)][0] < end:
            a, b = spans[len(groups)]
            groups.append(stage.at[core, a - start : b - start])
    for i in range(first, len(spans)):
        a, b = spans[i]
        group = send.at[1, a - base : b - base]
        gather_group(blocks[(a - base) // per : (b - base) // per], group, me)
        groups.append(group)
        raise_best(rows[i], group, group, True)
        for j in range(i):
            score_pair(rows, groups, i, j, bits[j], me)
    send[0] = send[1]


def cross_stage(received, before, best):
    best[...] = before[...]

    @pl.when(lax.axis_index("blk") == 1)
    def _():
        raise_best(best.at[:, : received.shape[1]], received.at[0], received.at[1])


def filled_queries(rows):
    ones = jnp.ones((8, LANES), BF)
    return matmul(ones, rows[:, :LANES], ((1,), (1,)))[:1] < 100.0


def finish(cuts, per, whole, best, out, row):
    me = lax.axis_index("clus")
    base = 0
    for rows in whole:
        size = rows.shape[0]
        kept = jnp.where(filled_queries(rows), best[:, base : base + size], F32(0.0))
        for a, b in zip(cuts, cuts[1:]):
            if base <= a < base + size:
                place = (me ^ (a // per)) & ~((b - a) // per - 1)
                at = pl.ds(pl.multiple_of(place * per, LANES), b - a)
                out[row : row + 1, at] = kept[:, a - base : b - base]
        base += size


def cross_whole(cuts, per, received, before, out, best):
    cross_stage(received, before, best)
    finish(cuts, per, [received.at[lax.axis_index("blk")]], best, out, 0)


def cross_last(cuts, received, send, before, ready, *refs):
    others, (out, keys, best) = refs[:-3], refs[-3:]
    per = others[0].shape[0]
    core = lax.axis_index("blk")
    best[...] = before[...]
    start = received.shape[1]

    @pl.when(core == 1)
    def _():
        for i, other in enumerate(others):
            keys[i * per : (i + 1) * per, :] = other[...]
        raise_best(best.at[:, :start], keys, received.at[1])
        raise_best(best.at[:, start:], received.at[0], send.at[1])
        raise_best(best.at[:, start:], keys, send.at[1])

    out[0:1, :] = ready[...]
    finish(cuts, per, [received.at[core], send.at[1]], best, out, 1)


def local(embeddings, cluster_ids):
    owners = lax.axis_size("clus")
    clusters = CLUS_DEV * owners
    rows, width = embeddings.shape
    per = 2 * rows // clusters
    bits = [owners // 2, owners // 4, owners // 8]
    bounds = [0, owners // 2, owners // 2 + owners // 4, owners - owners // 8, owners]
    cuts = [x * per for x in bounds]
    near, far1, far2, far3 = [list(range(a, b)) for a, b in zip(bounds, bounds[1:])]
    best_shape = jax.ShapeDtypeStruct((1, rows), F32)
    block = jax.ShapeDtypeStruct((per, width), BF)

    def to_owner(block, step):
        return lax.ppermute(block, "clus", [(i, i ^ step) for i in range(owners)])

    def stage_shape(sources):
        return jax.ShapeDtypeStruct((2, sources * per, width), BF)

    def to_both(send):
        return lax.all_to_all(send, "blk", split_axis=0, concat_axis=0, tiled=True)

    arrived = [{}, {}]

    def dispatch(picks, packed):
        for (step, cluster), block in zip(picks, packed):
            arrived[cluster][step] = to_owner(block, step) if step else block

    picks = [(step, 0) for step in far1]
    unit, tgt, *packed = kernel_call(
        functools.partial(pack_first, picks, clusters),
        [
            jax.ShapeDtypeStruct(embeddings.shape, BF),
            jax.ShapeDtypeStruct(cluster_ids.shape, jnp.int32),
        ]
        + [block] * len(picks),
        [embeddings, cluster_ids],
        "pack_first",
    )
    dispatch(picks, packed)
    for steps, cluster in (
        (near[1:] + [0], 0),
        (far2 + far3, 0),
        (far1 + near, 1),
        (far2 + far3, 1),
    ):
        picks = [(step, cluster) for step in steps]
        packed = kernel_call(
            functools.partial(pack_rest, picks), [block] * len(picks), [unit, tgt], "pack_rest"
        )
        dispatch(picks, packed)

    send, best = kernel_call(
        functools.partial(own_stage, cuts, bits, 0, 0),
        [stage_shape(owners), best_shape],
        [arrived[0][s] for s in near + far1 + far2 + far3],
        "own_whole",
    )
    (ready,) = kernel_call(
        functools.partial(cross_whole, cuts, per),
        [best_shape],
        [to_both(send), best],
        "cross_whole",
        [pltpu.VMEM((1, rows), F32)],
    )
    order = far1 + near
    *early, ready = lax.optimization_barrier((*[arrived[1][s] for s in order], ready))
    early = [early[order.index(s)] for s in near + far1]
    send, best = kernel_call(
        functools.partial(own_stage, cuts[:3], bits, 0, 0),
        [stage_shape(len(early)), best_shape],
        early,
        "own_early",
    )
    received = to_both(send)
    (best,) = kernel_call(cross_stage, [best_shape], [received, best], "cross_early")
    *late, best = lax.optimization_barrier((*[arrived[1][s] for s in far2 + far3], best))
    send, best = kernel_call(
        functools.partial(own_stage, cuts, bits, 1, 2),
        [stage_shape(len(late)), best_shape],
        [received, best] + late,
        "own_last",
    )
    others = [lax.ppermute(block, "blk", [(0, 1)]) for block in late]
    (out,) = kernel_call(
        functools.partial(cross_last, cuts),
        [jax.ShapeDtypeStruct((CLUS_DEV, rows), F32)],
        [received, send, best, ready] + others,
        "cross_last",
        [pltpu.VMEM((len(late) * per, width), BF), pltpu.VMEM((1, rows), F32)],
    )
    return out


def solution(mesh):
    placed = (P(("groups", "clus", "blk"), None), P(("groups", "clus", "blk"), None))
    return jax.shard_map(
        local, mesh=mesh, in_specs=placed, out_specs=P(("groups", "clus"), "blk"), check_vma=False
    )
```

```python
import functools

import jax
import jax.numpy as jnp
from jax import lax
from jax.experimental import pallas as pl
from jax.experimental.pallas import tpu as pltpu
from jax.sharding import PartitionSpec as P

CLUS_DEV = 2
LANES = 128
MARK = 2.0
BF = jnp.bfloat16
F32 = jnp.float32


def iota(shape, dim):
    return lax.broadcasted_iota(jnp.int32, shape, dim)


def matmul(a, b, contract):
    return lax.dot_general(a, b, (contract, ((), ())), preferred_element_type=F32)


def targets(ids, clusters, per_source):
    groups = ids.shape[1] // LANES
    parts = [ids[:, g * LANES : (g + 1) * LANES] for g in range(groups)]
    hot = jnp.concatenate(
        [(iota((clusters, LANES), 0) == part).astype(F32) for part in parts], axis=0
    )
    stacked = groups * clusters
    earlier = (iota((LANES, LANES), 0) < iota((LANES, LANES), 1)).astype(F32).astype(BF)
    within = matmul(hot.astype(BF), earlier, ((1,), (0,)))
    totals = jnp.broadcast_to(jnp.sum(hot, axis=1, keepdims=True), (stacked, LANES))
    a, b = iota((stacked, stacked), 0), iota((stacked, stacked), 1)
    chunks_before = ((a % clusters == b % clusters) & (b < a)).astype(F32).astype(BF)
    before = within + matmul(chunks_before, totals.astype(BF), ((1,), (0,)))
    picked = hot * before
    out = [
        jnp.sum(picked[g * clusters : (g + 1) * clusters], axis=0, keepdims=True).astype(jnp.int32)
        + parts[g] * per_source
        for g in range(groups)
    ]
    return jnp.concatenate(out, axis=1)


def store_blocks(unit, tgt, per, picks, outs):
    me = lax.axis_index("clus")
    hits = []
    for (step, cluster), out in zip(picks, outs):
        base = ((me ^ step) * CLUS_DEV + cluster) * per
        hits.append((tgt - base == iota((out.shape[0], tgt.shape[1]), 0)).astype(F32))
    hot = jnp.concatenate(hits, axis=0) if len(hits) > 1 else hits[0]
    rows = matmul(hot.astype(BF), unit, ((1,), (0,)))
    empty = jnp.max(hot, axis=1, keepdims=True) < 0.5
    marked = jnp.where(empty, F32(MARK), rows[:, :LANES])
    first = 0
    for out in outs:
        window = slice(first, first + out.shape[0])
        out[:, :LANES] = marked[window].astype(BF)
        out[:, LANES:] = rows[window, LANES:].astype(BF)
        first += out.shape[0]


def pack_first(per, picks, clusters, emb, ids, unit, tgt, *outs):
    values = emb[...].astype(F32)
    scale = lax.rsqrt(jnp.sum(values * values, axis=1, keepdims=True) + 1e-6)
    unit[...] = (values * scale).astype(BF)
    tgt[...] = targets(ids[...], clusters, per)
    store_blocks(unit[...], tgt[...], per, picks, outs)


def pack_rest(per, picks, unit, tgt, *outs):
    store_blocks(unit[...], tgt[...], per, picks, outs)


VMEM = pl.BlockSpec(memory_space=pltpu.VMEM)


def kernel_call(kernel, shapes, inputs, name, scratch=()):
    return pl.pallas_call(
        kernel,
        out_shape=shapes,
        in_specs=[VMEM] * len(inputs),
        out_specs=[VMEM] * len(shapes),
        scratch_shapes=scratch,
        compiler_params=pltpu.CompilerParams(vmem_limit_bytes=20 * 2**20),
        cost_estimate=pl.CostEstimate(flops=1000, bytes_accessed=1000, transcendentals=0),
        name=name,
    )(*inputs)


CHUNK = 256


def raise_best(best, keys, queries, triangular=False):
    rows = queries.shape[0]
    for start in range(0, rows, CHUNK):
        chunk = min(CHUNK, rows - start)
        count = start + chunk if triangular else keys.shape[0]
        sims = matmul(keys[:count, :], queries[start : start + chunk, :], ((1,), (1,)))
        filled = keys[:count, :LANES].astype(F32) < 1.5
        for first in range(0, chunk, LANES):
            allowed = filled
            if triangular:
                allowed = filled & (
                    iota((count, LANES), 0) < iota((count, LANES), 1) + (start + first)
                )
            part = jnp.where(allowed, sims[:, first : first + LANES], F32(-1.0))
            window = slice(start + first, start + first + LANES)
            best[:, window] = jnp.maximum(best[:, window], jnp.max(part, axis=0, keepdims=True))


def gather_group(blocks, per, cluster, out, me):
    for step, block in enumerate(blocks):
        place = (me & (len(blocks) - 1)) ^ step
        first = cluster * per if block.shape[0] > per else 0
        rows = pl.ds(pl.multiple_of(place * per, per), per)
        out[rows, :] = block[first : first + per, :]


def score_pair(bests, groups, new, old, bit, me):
    later = (me & bit) == 0

    @pl.when(later)
    def _():
        raise_best(bests[new], groups[old], groups[new])

    @pl.when(jnp.logical_not(later))
    def _():
        raise_best(bests[old], groups[new], groups[old])


def own_stage(per, cluster, cuts, bits, held, first, *refs):
    stages, refs = refs[:held], refs[held:]
    blocks, (send, best) = list(refs[:-2]), refs[-2:]
    before = blocks.pop(0) if held else None
    me = lax.axis_index("clus")
    core = lax.axis_index("blk")
    spans = list(zip(cuts, cuts[1:]))
    base = spans[first][0]
    if held:
        best[:, :base] = before[:, :base]
    best[:, base:] = jnp.full((1, best.shape[1] - base), -1.0, F32)
    rows = [best.at[:, a:b] for a, b in spans]
    groups = []
    for stage in stages:
        start = spans[len(groups)][0]
        end = start + stage.shape[1]
        while len(groups) < first and spans[len(groups)][0] < end:
            a, b = spans[len(groups)]
            groups.append(stage.at[core, a - start : b - start])
    for i in range(first, len(spans)):
        a, b = spans[i]
        group = send.at[1, a - base : b - base]
        gather_group(blocks[(a - base) // per : (b - base) // per], per, cluster, group, me)
        groups.append(group)
        raise_best(rows[i], group, group, True)
        for j in range(i):
            score_pair(rows, groups, i, j, bits[j], me)
    send[0] = send[1]


def cross_stage(received, before, best):
    best[...] = before[...]

    @pl.when(lax.axis_index("blk") == 1)
    def _():
        raise_best(best.at[:, : received.shape[1]], received.at[0], received.at[1])


def filled_queries(rows):
    ones = jnp.ones((8, LANES), BF)
    return matmul(ones, rows[:, :LANES], ((1,), (1,)))[:1] < 100.0


def finish(cuts, per, whole, best, out, row):
    me = lax.axis_index("clus")
    base = 0
    for rows in whole:
        size = rows.shape[0]
        kept = jnp.where(filled_queries(rows), best[:, base : base + size], F32(0.0))
        for a, b in zip(cuts, cuts[1:]):
            if base <= a < base + size:
                place = (me ^ (a // per)) & ~((b - a) // per - 1)
                at = pl.ds(pl.multiple_of(place * per, LANES), b - a)
                out[row : row + 1, at] = kept[:, a - base : b - base]
        base += size


def cross_whole(cuts, per, received, before, out, best):
    cross_stage(received, before, best)
    finish(cuts, per, [received.at[lax.axis_index("blk")]], best, out, 0)


def cross_last(cuts, received, send, before, ready, *refs):
    others, (out, keys, best) = refs[:-3], refs[-3:]
    per = others[0].shape[0]
    core = lax.axis_index("blk")
    best[...] = before[...]
    start = received.shape[1]

    @pl.when(core == 1)
    def _():
        for i, other in enumerate(others):
            keys[i * per : (i + 1) * per, :] = other[...]
        raise_best(best.at[:, :start], keys, received.at[1])
        raise_best(best.at[:, start:], received.at[0], send.at[1])
        raise_best(best.at[:, start:], keys, send.at[1])

    out[0:1, :] = ready[...]
    finish(cuts, per, [received.at[core], send.at[1]], best, out, 1)


def local(embeddings, cluster_ids):
    owners = lax.axis_size("clus")
    clusters = CLUS_DEV * owners
    rows, width = embeddings.shape
    per = 2 * rows // clusters
    bits = [owners // 2, owners // 4, owners // 8]
    bounds = [0, owners // 2, owners // 2 + owners // 4, owners - owners // 8, owners]
    cuts = [x * per for x in bounds]
    near, far1, far2, far3 = [list(range(a, b)) for a, b in zip(bounds, bounds[1:])]
    best_shape = jax.ShapeDtypeStruct((1, rows), F32)
    block = jax.ShapeDtypeStruct((per, width), BF)

    def to_owner(block, step):
        return lax.ppermute(block, "clus", [(i, i ^ step) for i in range(owners)])

    def stage_shape(sources):
        return jax.ShapeDtypeStruct((2, sources * per, width), BF)

    def to_both(send):
        return lax.all_to_all(send, "blk", split_axis=0, concat_axis=0, tiled=True)

    arrived = [{}, {}]

    def dispatch(picks, packed):
        for (step, cluster), block in zip(picks, packed):
            arrived[cluster][step] = to_owner(block, step) if step else block

    picks = [(step, 0) for step in far1]
    unit, tgt, *packed = kernel_call(
        functools.partial(pack_first, per, picks, clusters),
        [
            jax.ShapeDtypeStruct(embeddings.shape, BF),
            jax.ShapeDtypeStruct(cluster_ids.shape, jnp.int32),
        ]
        + [block] * len(picks),
        [embeddings, cluster_ids],
        "pack_first",
    )
    dispatch(picks, packed)
    both = jax.ShapeDtypeStruct((CLUS_DEV * per, width), BF)
    for picks, shape in (
        ([(step, 0) for step in far2 + far3], block),
        ([(step, 0) for step in near[1:] + [0]], both),
        ([(step, 1) for step in far1], block),
        ([(step, 1) for step in far2 + far3], block),
    ):
        packed = kernel_call(
            functools.partial(pack_rest, per, picks), [shape] * len(picks), [unit, tgt], "pack_rest"
        )
        dispatch(picks, packed)

    send, best = kernel_call(
        functools.partial(own_stage, per, 0, cuts, bits, 0, 0),
        [stage_shape(owners), best_shape],
        [arrived[0][s] for s in near + far1 + far2 + far3],
        "own_whole",
    )
    (ready,) = kernel_call(
        functools.partial(cross_whole, cuts, per),
        [best_shape],
        [to_both(send), best],
        "cross_whole",
        [pltpu.VMEM((1, rows), F32)],
    )
    *early, ready = lax.optimization_barrier((*[arrived[1][s] for s in far1], ready))
    early = [arrived[0][s] for s in near] + early
    send, best = kernel_call(
        functools.partial(own_stage, per, 1, cuts[:3], bits, 0, 0),
        [stage_shape(len(near + far1)), best_shape],
        early,
        "own_early",
    )
    received = to_both(send)
    (best,) = kernel_call(cross_stage, [best_shape], [received, best], "cross_early")
    *late, best = lax.optimization_barrier((*[arrived[1][s] for s in far2 + far3], best))
    send, best = kernel_call(
        functools.partial(own_stage, per, 1, cuts, bits, 1, 2),
        [stage_shape(len(late)), best_shape],
        [received, best] + late,
        "own_last",
    )
    others = [lax.ppermute(block, "blk", [(0, 1)]) for block in late]
    (out,) = kernel_call(
        functools.partial(cross_last, cuts),
        [jax.ShapeDtypeStruct((CLUS_DEV, rows), F32)],
        [received, send, best, ready] + others,
        "cross_last",
        [pltpu.VMEM((len(late) * per, width), BF), pltpu.VMEM((1, rows), F32)],
    )
    return out


def solution(mesh):
    placed = (P(("groups", "clus", "blk"), None), P(("groups", "clus", "blk"), None))
    return jax.shard_map(
        local, mesh=mesh, in_specs=placed, out_specs=P(("groups", "clus"), "blk"), check_vma=False
    )
```

```python
import functools

import jax
import jax.numpy as jnp
from jax import lax
from jax.experimental import pallas as pl
from jax.experimental.pallas import tpu as pltpu
from jax.sharding import PartitionSpec as P

CLUS_DEV = 2
LANES = 128
MARK = 2.0
BF = jnp.bfloat16
F32 = jnp.float32


def iota(shape, dim):
    return lax.broadcasted_iota(jnp.int32, shape, dim)


def matmul(a, b, contract):
    return lax.dot_general(a, b, (contract, ((), ())), preferred_element_type=F32)


def targets(ids, clusters, per_source):
    groups = ids.shape[1] // LANES
    parts = [ids[:, g * LANES : (g + 1) * LANES] for g in range(groups)]
    hot = jnp.concatenate(
        [(iota((clusters, LANES), 0) == part).astype(F32) for part in parts], axis=0
    )
    stacked = groups * clusters
    earlier = (iota((LANES, LANES), 0) < iota((LANES, LANES), 1)).astype(F32).astype(BF)
    within = matmul(hot.astype(BF), earlier, ((1,), (0,)))
    totals = jnp.broadcast_to(jnp.sum(hot, axis=1, keepdims=True), (stacked, LANES))
    a, b = iota((stacked, stacked), 0), iota((stacked, stacked), 1)
    chunks_before = ((a % clusters == b % clusters) & (b < a)).astype(F32).astype(BF)
    before = within + matmul(chunks_before, totals.astype(BF), ((1,), (0,)))
    picked = hot * before
    out = [
        jnp.sum(picked[g * clusters : (g + 1) * clusters], axis=0, keepdims=True).astype(jnp.int32)
        + parts[g] * per_source
        for g in range(groups)
    ]
    return jnp.concatenate(out, axis=1)


def pack_block(unit, tgt, dest, width):
    hit = (tgt - dest * width) == iota((width, tgt.shape[1]), 0)
    hot = hit.astype(F32)
    rows = matmul(hot.astype(BF), unit, ((1,), (0,)))
    empty = jnp.max(hot, axis=1, keepdims=True) < 0.5
    head = jnp.where(empty, F32(MARK), rows[:, :LANES])
    return head.astype(BF), rows[:, LANES:].astype(BF)


def store_blocks(unit, tgt, steps, width, outs):
    me = lax.axis_index("clus")
    for step, out in zip(steps, outs):
        head, tail = pack_block(unit, tgt, me ^ step, width)
        out[:, :LANES] = head
        out[:, LANES:] = tail


def pack_first(steps, clusters, per_source, emb, ids, unit, tgt, *outs):
    values = emb[...].astype(F32)
    scale = lax.rsqrt(jnp.sum(values * values, axis=1, keepdims=True) + 1e-6)
    unit[...] = (values * scale).astype(BF)
    tgt[...] = targets(ids[...], clusters, per_source)
    store_blocks(unit[...], tgt[...], steps, CLUS_DEV * per_source, outs)


def pack_rest(steps, per_source, unit, tgt, *outs):
    store_blocks(unit[...], tgt[...], steps, CLUS_DEV * per_source, outs)


VMEM = pl.BlockSpec(memory_space=pltpu.VMEM)


def kernel_call(kernel, shapes, inputs, name, scratch=()):
    return pl.pallas_call(
        kernel,
        out_shape=shapes,
        in_specs=[VMEM] * len(inputs),
        out_specs=[VMEM] * len(shapes),
        scratch_shapes=scratch,
        compiler_params=pltpu.CompilerParams(vmem_limit_bytes=20 * 2**20),
        cost_estimate=pl.CostEstimate(flops=1000, bytes_accessed=1000, transcendentals=0),
        name=name,
    )(*inputs)


def call_pack_first(emb, ids, steps, clusters, per_source):
    block = jax.ShapeDtypeStruct((CLUS_DEV * per_source, emb.shape[1]), BF)
    shapes = [jax.ShapeDtypeStruct(emb.shape, BF), jax.ShapeDtypeStruct(ids.shape, jnp.int32)]
    return kernel_call(
        functools.partial(pack_first, steps, clusters, per_source),
        shapes + [block] * len(steps),
        [emb, ids],
        "pack_first",
    )


def call_pack_rest(unit, tgt, steps, per_source):
    block = jax.ShapeDtypeStruct((CLUS_DEV * per_source, unit.shape[1]), BF)
    return kernel_call(
        functools.partial(pack_rest, steps, per_source),
        [block] * len(steps),
        [unit, tgt],
        "pack_rest",
    )


CHUNK = 256


def raise_best(best, keys, queries, triangular=False):
    rows = queries.shape[0]
    for start in range(0, rows, CHUNK):
        chunk = min(CHUNK, rows - start)
        count = start + chunk if triangular else keys.shape[0]
        sims = matmul(keys[:count, :], queries[start : start + chunk, :], ((1,), (1,)))
        filled = keys[:count, :LANES].astype(F32) < 1.5
        for first in range(0, chunk, LANES):
            allowed = filled
            if triangular:
                allowed = filled & (
                    iota((count, LANES), 0) < iota((count, LANES), 1) + (start + first)
                )
            part = jnp.where(allowed, sims[:, first : first + LANES], F32(-1.0))
            window = slice(start + first, start + first + LANES)
            best[:, window] = jnp.maximum(best[:, window], jnp.max(part, axis=0, keepdims=True))


def gather_group(blocks, cluster, out, me):
    per = blocks[0].shape[0] // CLUS_DEV
    for step, block in enumerate(blocks):
        place = (me & (len(blocks) - 1)) ^ step
        rows = pl.ds(pl.multiple_of(place * per, per), per)
        out[rows, :] = block[cluster * per : (cluster + 1) * per, :]


def score_pair(bests, groups, new, old, bit, me):
    later = (me & bit) == 0

    @pl.when(later)
    def _():
        raise_best(bests[new], groups[old], groups[new])

    @pl.when(jnp.logical_not(later))
    def _():
        raise_best(bests[old], groups[new], groups[old])


def own_stage(cuts, bits, held, first, *refs):
    stages, refs = refs[:held], refs[held:]
    blocks, (send, best) = list(refs[:-2]), refs[-2:]
    before = blocks.pop(0) if held else None
    per = blocks[0].shape[0] // CLUS_DEV
    me = lax.axis_index("clus")
    core = lax.axis_index("blk")
    spans = list(zip(cuts, cuts[1:]))
    base = spans[first][0]
    if held:
        best[:, :base] = before[:, :base]
    best[:, base:] = jnp.full((CLUS_DEV, best.shape[1] - base), -1.0, F32)
    for c in range(CLUS_DEV):
        rows = [best.at[c : c + 1, a:b] for a, b in spans]
        groups = []
        for stage in stages:
            start = spans[len(groups)][0]
            end = start + stage.shape[2]
            while len(groups) < first and spans[len(groups)][0] < end:
                a, b = spans[len(groups)]
                groups.append(stage.at[core, c, a - start : b - start])
        for i in range(first, len(spans)):
            a, b = spans[i]
            group = send.at[1, c, a - base : b - base]
            gather_group(blocks[(a - base) // per : (b - base) // per], c, group, me)
            groups.append(group)
            raise_best(rows[i], group, group, True)
            for j in range(i):
                score_pair(rows, groups, i, j, bits[j], me)
        send[0, c] = send[1, c]


def cross_stage(cuts, held, *refs):
    stages, before, best = refs[: held + 1], refs[held + 1], refs[held + 2]
    best[...] = before[...]

    @pl.when(lax.axis_index("blk") == 1)
    def _():
        new = stages[-1]
        for c in range(CLUS_DEV):
            base = 0
            for stage in stages:
                end = base + stage.shape[2]
                raise_best(best.at[c : c + 1, base:end], new.at[0, c], stage.at[1, c])
                base = end
            start = base - new.shape[2]
            for stage in stages[:-1]:
                raise_best(best.at[c : c + 1, start:base], stage.at[0, c], new.at[1, c])


def filled_queries(rows):
    ones = jnp.ones((8, LANES), BF)
    return matmul(ones, rows[:, :LANES], ((1,), (1,)))[:1] < 100.0


def gather_late(*refs):
    blocks, out = refs[:-1], refs[-1]
    for c in range(CLUS_DEV):
        gather_group(blocks, c, out.at[c], lax.axis_index("clus"))


def own_late(cuts, bits, held, *refs):
    stages, (cat, before, best) = refs[:held], refs[held:]
    me = lax.axis_index("clus")
    core = lax.axis_index("blk")
    spans = list(zip(cuts, cuts[1:]))
    last = len(spans) - 1
    start = spans[last][0]
    best[:, :start] = before[:, :start]
    best[:, start:] = jnp.full((CLUS_DEV, best.shape[1] - start), -1.0, F32)
    for c in range(CLUS_DEV):
        rows = [best.at[c : c + 1, a:b] for a, b in spans]
        groups = [stage.at[core, c] for stage in stages] + [cat.at[c]]
        raise_best(rows[last], groups[last], groups[last], True)
        for i in range(last):
            score_pair(rows, groups, last, i, bits[i], me)


def cross_late(cuts, per, held, *refs):
    stages, (cat, before, other, out, best) = refs[:held], refs[held:]
    me = lax.axis_index("clus")
    core = lax.axis_index("blk")
    spans = list(zip(cuts, cuts[1:]))
    best[...] = before[...]

    @pl.when(core == 1)
    def _():
        for c in range(CLUS_DEV):
            rows = [best.at[c : c + 1, a:b] for a, b in spans]
            for row, stage in zip(rows, stages):
                raise_best(row, other.at[c], stage.at[1, c])
                raise_best(rows[held], stage.at[0, c], cat.at[c])
            raise_best(rows[held], other.at[c], cat.at[c])

    for c in range(CLUS_DEV):
        groups = [stage.at[core, c] for stage in stages] + [cat.at[c]]
        for (a, b), group in zip(spans, groups):
            place = (me ^ (a // per)) & ~((b - a) // per - 1)
            at = pl.ds(pl.multiple_of(place * per, LANES), b - a)
            value = best[c : c + 1, a:b]
            out[c : c + 1, at] = jnp.where(filled_queries(group), value, F32(0.0))


def local(embeddings, cluster_ids):
    owners = lax.axis_size("clus")
    clusters = CLUS_DEV * owners
    rows, width = embeddings.shape
    per = 2 * rows // clusters
    bits = [owners // 2, owners // 4]
    bounds = [0, owners // 2, owners // 2 + owners // 4, owners]
    cuts = [x * per for x in bounds]
    near, far, late = [list(range(a, b)) for a, b in zip(bounds, bounds[1:])]
    best_shape = jax.ShapeDtypeStruct((CLUS_DEV, rows), F32)

    def to_owner(block, step):
        return lax.ppermute(block, "clus", [(i, i ^ step) for i in range(owners)])

    def stage_shape(sources):
        return jax.ShapeDtypeStruct((2, CLUS_DEV, sources * per, width), BF)

    def to_both(send):
        return lax.all_to_all(send, "blk", split_axis=0, concat_axis=0, tiled=True)

    arrived = {}
    lead = [near[-1], far[0]]
    unit, tgt, *packed = call_pack_first(embeddings, cluster_ids, lead, clusters, per)
    for steps in (near[1:-1] + far[1:] + [0], []):
        for step, block in zip(lead, packed):
            arrived[step] = to_owner(block, step) if step else block
        lead, packed = steps, call_pack_rest(unit, tgt, steps, per) if steps else []
    packed = call_pack_rest(unit, tgt, late, per)
    for part, gate in ((slice(0, len(late) // 2), near[-1]), (slice(len(late) // 2, None), far[0])):
        *held, arrived[gate] = lax.optimization_barrier((*packed[part], arrived[gate]))
        for step, block in zip(late[part], held):
            arrived[step] = to_owner(block, step)

    send, best = kernel_call(
        functools.partial(own_stage, cuts[:2], bits, 0, 0),
        [stage_shape(len(near)), best_shape],
        [arrived[s] for s in near],
        "own_near",
    )
    stages = [to_both(send)]
    (best,) = kernel_call(
        functools.partial(cross_stage, cuts, 0), [best_shape], stages + [best], "cross_near"
    )
    arrived[far[-1]], best = lax.optimization_barrier((arrived[far[-1]], best))
    send, best = kernel_call(
        functools.partial(own_stage, cuts[:3], bits, 1, 1),
        [stage_shape(len(far)), best_shape],
        stages + [best] + [arrived[s] for s in far],
        "own_far",
    )
    stages.append(to_both(send))
    (best,) = kernel_call(
        functools.partial(cross_stage, cuts, 1), [best_shape], stages + [best], "cross_far"
    )
    *new, best = lax.optimization_barrier((*[arrived[s] for s in late], best))
    cat_shape = jax.ShapeDtypeStruct((CLUS_DEV, len(late) * per, width), BF)
    (cat,) = kernel_call(gather_late, [cat_shape], new, "gather_late")
    other = lax.ppermute(cat, "blk", [(0, 1)])
    (best,) = kernel_call(
        functools.partial(own_late, cuts, bits, 2), [best_shape], stages + [cat, best], "own_late"
    )
    (out,) = kernel_call(
        functools.partial(cross_late, cuts, per, 2),
        [best_shape],
        stages + [cat, best, other],
        "cross_late",
        [pltpu.VMEM((CLUS_DEV, rows), F32)],
    )
    return out


def solution(mesh):
    placed = (P(("groups", "clus", "blk"), None), P(("groups", "clus", "blk"), None))
    return jax.shard_map(
        local, mesh=mesh, in_specs=placed, out_specs=P(("groups", "clus"), "blk"), check_vma=False
    )
```

```python
import functools

import jax
import jax.numpy as jnp
from jax import lax
from jax.experimental import pallas as pl
from jax.experimental.pallas import tpu as pltpu
from jax.sharding import PartitionSpec as P

CLUS_DEV = 2
LANES = 128
MARK = 2.0
UNFILLED = 8.0
BF = jnp.bfloat16
F32 = jnp.float32


def iota(shape, dim):
    return lax.broadcasted_iota(jnp.int32, shape, dim)


def matmul(a, b, contract):
    return lax.dot_general(a, b, (contract, ((), ())), preferred_element_type=F32)


def targets(ids, clusters, per_source):
    groups = ids.shape[1] // LANES
    parts = [ids[:, g * LANES : (g + 1) * LANES] for g in range(groups)]
    hot = jnp.concatenate(
        [(iota((clusters, LANES), 0) == part).astype(F32) for part in parts], axis=0
    )
    stacked = groups * clusters
    earlier = (iota((LANES, LANES), 0) < iota((LANES, LANES), 1)).astype(F32).astype(BF)
    within = matmul(hot.astype(BF), earlier, ((1,), (0,)))
    totals = jnp.broadcast_to(jnp.sum(hot, axis=1, keepdims=True), (stacked, LANES))
    a, b = iota((stacked, stacked), 0), iota((stacked, stacked), 1)
    chunks_before = ((a % clusters == b % clusters) & (b < a)).astype(F32).astype(BF)
    before = within + matmul(chunks_before, totals.astype(BF), ((1,), (0,)))
    picked = hot * before
    out = [
        jnp.sum(picked[g * clusters : (g + 1) * clusters], axis=0, keepdims=True).astype(jnp.int32)
        + parts[g] * per_source
        for g in range(groups)
    ]
    return jnp.concatenate(out, axis=1)


def pack_block(unit, tgt, dest, width):
    hit = (tgt - dest * width) == iota((width, tgt.shape[1]), 0)
    hot = hit.astype(F32)
    rows = matmul(hot.astype(BF), unit, ((1,), (0,)))
    empty = jnp.max(hot, axis=1, keepdims=True) < 0.5
    head = jnp.where(empty, F32(MARK), rows[:, :LANES])
    return head.astype(BF), rows[:, LANES:].astype(BF)


def store_blocks(unit, tgt, steps, width, outs):
    me = lax.axis_index("clus")
    for step, out in zip(steps, outs):
        head, tail = pack_block(unit, tgt, me ^ step, width)
        out[:, :LANES] = head
        out[:, LANES:] = tail


PIECES = 4


def pack_first(steps, clusters, per_source, emb, ids, unit, tgt, *refs):
    outs, (raw, raw_ids, sems, ids_sem) = refs[:-4], refs[-4:]
    size = emb.shape[0] // PIECES
    ids_copy = pltpu.make_async_copy(ids, raw_ids, ids_sem)
    ids_copy.start()
    windows = [pl.ds(piece * size, size) for piece in range(PIECES)]
    copies = [
        pltpu.make_async_copy(emb.at[window], raw.at[window], sems.at[piece])
        for piece, window in enumerate(windows)
    ]
    for copy in copies:
        copy.start()
    ids_copy.wait()
    tgt[...] = targets(raw_ids[...], clusters, per_source)
    for copy, window in zip(copies, windows):
        copy.wait()
        values = raw[window, :].astype(F32)
        scale = lax.rsqrt(jnp.sum(values * values, axis=1, keepdims=True) + 1e-6)
        unit[window, :] = (values * scale).astype(BF)
    store_blocks(unit[...], tgt[...], steps, CLUS_DEV * per_source, outs)


def pack_rest(steps, per_source, unit, tgt, *outs):
    store_blocks(unit[...], tgt[...], steps, CLUS_DEV * per_source, outs)


VMEM = pl.BlockSpec(memory_space=pltpu.VMEM)


def kernel_call(kernel, shapes, inputs, name, scratch=(), place=VMEM, grant=20 * 2**20):
    return pl.pallas_call(
        kernel,
        out_shape=shapes,
        in_specs=[place] * len(inputs),
        out_specs=[VMEM] * len(shapes),
        scratch_shapes=scratch,
        compiler_params=pltpu.CompilerParams(vmem_limit_bytes=grant),
        cost_estimate=pl.CostEstimate(flops=1000, bytes_accessed=1000, transcendentals=0),
        name=name,
    )(*inputs)


def call_pack_first(emb, ids, steps, clusters, per_source):
    block = jax.ShapeDtypeStruct((CLUS_DEV * per_source, emb.shape[1]), BF)
    shapes = [jax.ShapeDtypeStruct(emb.shape, BF), jax.ShapeDtypeStruct(ids.shape, jnp.int32)]
    return kernel_call(
        functools.partial(pack_first, steps, clusters, per_source),
        shapes + [block] * len(steps),
        [emb, ids],
        place=pl.BlockSpec(memory_space=pl.ANY),
        grant=50 * 2**20,
        name="pack_first",
        scratch=[
            pltpu.VMEM(emb.shape, BF),
            pltpu.VMEM(ids.shape, jnp.int32),
            pltpu.SemaphoreType.DMA((PIECES,)),
            pltpu.SemaphoreType.DMA,
        ],
    )


def call_pack_rest(unit, tgt, steps, per_source):
    block = jax.ShapeDtypeStruct((CLUS_DEV * per_source, unit.shape[1]), BF)
    return kernel_call(
        functools.partial(pack_rest, steps, per_source),
        [block] * len(steps),
        [unit, tgt],
        "pack_rest",
    )


CHUNK = 256


def raise_best(best, keys, queries, triangular=False):
    rows = queries.shape[0]
    for start in range(0, rows, CHUNK):
        chunk = min(CHUNK, rows - start)
        count = start + chunk if triangular else keys.shape[0]
        sims = matmul(keys[:count, :], queries[start : start + chunk, :], ((1,), (1,)))
        filled = keys[:count, :LANES].astype(F32) < 1.5
        for first in range(0, chunk, LANES):
            allowed = filled
            if triangular:
                allowed = filled & (
                    iota((count, LANES), 0) < iota((count, LANES), 1) + (start + first)
                )
            part = jnp.where(allowed, sims[:, first : first + LANES], F32(-1.0))
            window = slice(start + first, start + first + LANES)
            best[:, window] = jnp.maximum(best[:, window], jnp.max(part, axis=0, keepdims=True))


def gather_group(blocks, cluster, out, me):
    per = blocks[0].shape[0] // CLUS_DEV
    for step, block in enumerate(blocks):
        place = (me & (len(blocks) - 1)) ^ step
        rows = pl.ds(pl.multiple_of(place * per, per), per)
        out[rows, :] = block[cluster * per : (cluster + 1) * per, :]


def score_pair(bests, groups, new, old, bit, me):
    later = (me & bit) == 0

    @pl.when(later)
    def _():
        raise_best(bests[new], groups[old], groups[new])

    @pl.when(jnp.logical_not(later))
    def _():
        raise_best(bests[old], groups[new], groups[old])


def fresh_best(rows):
    ones = jnp.ones((8, LANES), BF)
    heads = matmul(ones, rows[:, :LANES], ((1,), (1,)))[:1]
    return jnp.where(heads < 100.0, F32(-1.0), F32(UNFILLED))


def own_stage(cuts, bits, held, first, *refs):
    stages, refs = refs[:held], refs[held:]
    blocks, (send, best) = list(refs[:-2]), refs[-2:]
    before = blocks.pop(0) if held else None
    per = blocks[0].shape[0] // CLUS_DEV
    me = lax.axis_index("clus")
    core = lax.axis_index("blk")
    spans = list(zip(cuts, cuts[1:]))
    base = spans[first][0]
    if held:
        best[:, :base] = before[:, :base]
    for c in range(CLUS_DEV):
        rows = [best.at[c : c + 1, a:b] for a, b in spans]
        groups = []
        for stage in stages:
            start = spans[len(groups)][0]
            end = start + stage.shape[2]
            while len(groups) < first and spans[len(groups)][0] < end:
                a, b = spans[len(groups)]
                groups.append(stage.at[core, c, a - start : b - start])
        for i in range(first, len(spans)):
            a, b = spans[i]
            group = send.at[1, c, a - base : b - base]
            gather_group(blocks[(a - base) // per : (b - base) // per], c, group, me)
            groups.append(group)
            rows[i][...] = fresh_best(group)
            raise_best(rows[i], group, group, True)
            for j in range(i):
                score_pair(rows, groups, i, j, bits[j], me)
        send[0, c] = send[1, c]


def cross_stage(cuts, held, *refs):
    stages, before, best = refs[: held + 1], refs[held + 1], refs[held + 2]
    best[...] = before[...]

    @pl.when(lax.axis_index("blk") == 1)
    def _():
        new = stages[-1]
        for c in range(CLUS_DEV):
            base = 0
            for stage in stages:
                end = base + stage.shape[2]
                raise_best(best.at[c : c + 1, base:end], new.at[0, c], stage.at[1, c])
                base = end
            start = base - new.shape[2]
            for stage in stages[:-1]:
                raise_best(best.at[c : c + 1, start:base], stage.at[0, c], new.at[1, c])


def gather_late(*refs):
    blocks, out = refs[:-1], refs[-1]
    for c in range(CLUS_DEV):
        gather_group(blocks, c, out.at[c], lax.axis_index("clus"))


def own_late(cuts, bits, held, *refs):
    stages, (cat, before, best) = refs[:held], refs[held:]
    me = lax.axis_index("clus")
    core = lax.axis_index("blk")
    spans = list(zip(cuts, cuts[1:]))
    last = len(spans) - 1
    start = spans[last][0]
    best[:, :start] = before[:, :start]
    for c in range(CLUS_DEV):
        rows = [best.at[c : c + 1, a:b] for a, b in spans]
        groups = [stage.at[core, c] for stage in stages] + [cat.at[c]]
        rows[last][...] = fresh_best(groups[last])
        raise_best(rows[last], groups[last], groups[last], True)
        for i in range(last):
            score_pair(rows, groups, last, i, bits[i], me)


def cross_late(cuts, per, held, *refs):
    stages, (cat, before, other, out, best) = refs[:held], refs[held:]
    me = lax.axis_index("clus")
    core = lax.axis_index("blk")
    spans = list(zip(cuts, cuts[1:]))
    best[...] = before[...]

    @pl.when(core == 1)
    def _():
        for c in range(CLUS_DEV):
            rows = [best.at[c : c + 1, a:b] for a, b in spans]
            for row, stage in zip(rows, stages):
                raise_best(row, other.at[c], stage.at[1, c])
                raise_best(rows[held], stage.at[0, c], cat.at[c])
            raise_best(rows[held], other.at[c], cat.at[c])

    for a, b in spans:
        place = (me ^ (a // per)) & ~((b - a) // per - 1)
        value = best[:, a:b]
        at = pl.ds(pl.multiple_of(place * per, LANES), b - a)
        out[:, at] = jnp.where(value > 0.5 * UNFILLED, F32(0.0), value)


def local(embeddings, cluster_ids):
    owners = lax.axis_size("clus")
    clusters = CLUS_DEV * owners
    rows, width = embeddings.shape
    per = 2 * rows // clusters
    bits = [owners // 2, owners // 4]
    bounds = [0, owners // 2, owners // 2 + owners // 4, owners]
    cuts = [x * per for x in bounds]
    near, far, late = [list(range(a, b)) for a, b in zip(bounds, bounds[1:])]
    best_shape = jax.ShapeDtypeStruct((CLUS_DEV, rows), F32)

    def to_owner(block, step):
        return lax.ppermute(block, "clus", [(i, i ^ step) for i in range(owners)])

    def stage_shape(sources):
        return jax.ShapeDtypeStruct((2, CLUS_DEV, sources * per, width), BF)

    def to_both(send):
        return lax.all_to_all(send, "blk", split_axis=0, concat_axis=0, tiled=True)

    arrived = {}
    lead = far[:1]
    unit, tgt, *packed = call_pack_first(embeddings, cluster_ids, lead, clusters, per)
    for steps in (near[1:] + far[1:] + [0], []):
        for step, block in zip(lead, packed):
            arrived[step] = to_owner(block, step) if step else block
        lead, packed = steps, call_pack_rest(unit, tgt, steps, per) if steps else []
    packed = call_pack_rest(unit, tgt, late, per)
    *held, arrived[far[0]] = lax.optimization_barrier((*packed, arrived[far[0]]))
    for step, block in zip(late, held):
        arrived[step] = to_owner(block, step)

    send, best = kernel_call(
        functools.partial(own_stage, cuts[:2], bits, 0, 0),
        [stage_shape(len(near)), best_shape],
        [arrived[s] for s in near],
        "own_near",
    )
    stages = [to_both(send)]
    (best,) = kernel_call(
        functools.partial(cross_stage, cuts, 0), [best_shape], stages + [best], "cross_near"
    )
    arrived[far[-1]], best = lax.optimization_barrier((arrived[far[-1]], best))
    send, best = kernel_call(
        functools.partial(own_stage, cuts[:3], bits, 1, 1),
        [stage_shape(len(far)), best_shape],
        stages + [best] + [arrived[s] for s in far],
        "own_far",
    )
    stages.append(to_both(send))
    (best,) = kernel_call(
        functools.partial(cross_stage, cuts, 1), [best_shape], stages + [best], "cross_far"
    )
    *new, best = lax.optimization_barrier((*[arrived[s] for s in late], best))
    cat_shape = jax.ShapeDtypeStruct((CLUS_DEV, len(late) * per, width), BF)
    (cat,) = kernel_call(gather_late, [cat_shape], new, "gather_late")
    other = lax.ppermute(cat, "blk", [(0, 1)])
    (best,) = kernel_call(
        functools.partial(own_late, cuts, bits, 2), [best_shape], stages + [cat, best], "own_late"
    )
    (out,) = kernel_call(
        functools.partial(cross_late, cuts, per, 2),
        [best_shape],
        stages + [cat, best, other],
        "cross_late",
        [pltpu.VMEM((CLUS_DEV, rows), F32)],
    )
    return out


def solution(mesh):
    placed = (P(("groups", "clus", "blk"), None), P(("groups", "clus", "blk"), None))
    return jax.shard_map(
        local, mesh=mesh, in_specs=placed, out_specs=P(("groups", "clus"), "blk"), check_vma=False
    )
```

```python
import functools

import jax
import jax.numpy as jnp
from jax import lax
from jax.experimental import pallas as pl
from jax.experimental.pallas import tpu as pltpu
from jax.sharding import PartitionSpec as P

CLUS_DEV = 2
LANES = 128
MARK = 2.0
UNFILLED = 8.0
BF = jnp.bfloat16
F32 = jnp.float32


def iota(shape, dim):
    return lax.broadcasted_iota(jnp.int32, shape, dim)


def matmul(a, b, contract):
    return lax.dot_general(a, b, (contract, ((), ())), preferred_element_type=F32)


def targets(ids, clusters, per_source):
    groups = ids.shape[1] // LANES
    parts = [ids[:, g * LANES : (g + 1) * LANES] for g in range(groups)]
    hot = jnp.concatenate(
        [(iota((clusters, LANES), 0) == part).astype(F32) for part in parts], axis=0
    )
    stacked = groups * clusters
    earlier = (iota((LANES, LANES), 0) < iota((LANES, LANES), 1)).astype(F32).astype(BF)
    within = matmul(hot.astype(BF), earlier, ((1,), (0,)))
    totals = jnp.broadcast_to(jnp.sum(hot, axis=1, keepdims=True), (stacked, LANES))
    a, b = iota((stacked, stacked), 0), iota((stacked, stacked), 1)
    chunks_before = ((a % clusters == b % clusters) & (b < a)).astype(F32).astype(BF)
    before = within + matmul(chunks_before, totals.astype(BF), ((1,), (0,)))
    picked = hot * before
    out = [
        jnp.sum(picked[g * clusters : (g + 1) * clusters], axis=0, keepdims=True).astype(jnp.int32)
        + parts[g] * per_source
        for g in range(groups)
    ]
    return jnp.concatenate(out, axis=1)


def pack_block(unit, tgt, dest, width):
    hit = (tgt - dest * width) == iota((width, tgt.shape[1]), 0)
    hot = hit.astype(F32)
    rows = matmul(hot.astype(BF), unit, ((1,), (0,)))
    empty = jnp.max(hot, axis=1, keepdims=True) < 0.5
    head = jnp.where(empty, F32(MARK), rows[:, :LANES])
    return head.astype(BF), rows[:, LANES:].astype(BF)


def store_blocks(unit, tgt, steps, width, outs):
    me = lax.axis_index("clus")
    for step, out in zip(steps, outs):
        head, tail = pack_block(unit, tgt, me ^ step, width)
        out[:, :LANES] = head
        out[:, LANES:] = tail


PIECES = 4


def pack_first(steps, clusters, per_source, emb, ids, unit, tgt, *refs):
    outs, (raw, raw_ids, sems, ids_sem) = refs[:-4], refs[-4:]
    size = emb.shape[0] // PIECES
    ids_copy = pltpu.make_async_copy(ids, raw_ids, ids_sem)
    ids_copy.start()
    windows = [pl.ds(piece * size, size) for piece in range(PIECES)]
    copies = [
        pltpu.make_async_copy(emb.at[window], raw.at[window], sems.at[piece])
        for piece, window in enumerate(windows)
    ]
    for copy in copies:
        copy.start()
    ids_copy.wait()
    tgt[...] = targets(raw_ids[...], clusters, per_source)
    for copy, window in zip(copies, windows):
        copy.wait()
        values = raw[window, :].astype(F32)
        scale = lax.rsqrt(jnp.sum(values * values, axis=1, keepdims=True) + 1e-6)
        unit[window, :] = (values * scale).astype(BF)
    store_blocks(unit[...], tgt[...], steps, CLUS_DEV * per_source, outs)


def pack_rest(steps, per_source, unit, tgt, *outs):
    store_blocks(unit[...], tgt[...], steps, CLUS_DEV * per_source, outs)


VMEM = pl.BlockSpec(memory_space=pltpu.VMEM)


def kernel_call(kernel, shapes, inputs, name, scratch=(), place=VMEM, grant=20 * 2**20):
    return pl.pallas_call(
        kernel,
        out_shape=shapes,
        in_specs=[place] * len(inputs),
        out_specs=[VMEM] * len(shapes),
        scratch_shapes=scratch,
        compiler_params=pltpu.CompilerParams(vmem_limit_bytes=grant),
        cost_estimate=pl.CostEstimate(flops=1000, bytes_accessed=1000, transcendentals=0),
        name=name,
    )(*inputs)


def call_pack_first(emb, ids, steps, clusters, per_source):
    block = jax.ShapeDtypeStruct((CLUS_DEV * per_source, emb.shape[1]), BF)
    shapes = [jax.ShapeDtypeStruct(emb.shape, BF), jax.ShapeDtypeStruct(ids.shape, jnp.int32)]
    return kernel_call(
        functools.partial(pack_first, steps, clusters, per_source),
        shapes + [block] * len(steps),
        [emb, ids],
        place=pl.BlockSpec(memory_space=pl.ANY),
        grant=50 * 2**20,
        name="pack_first",
        scratch=[
            pltpu.VMEM(emb.shape, BF),
            pltpu.VMEM(ids.shape, jnp.int32),
            pltpu.SemaphoreType.DMA((PIECES,)),
            pltpu.SemaphoreType.DMA,
        ],
    )


def call_pack_rest(unit, tgt, steps, per_source):
    block = jax.ShapeDtypeStruct((CLUS_DEV * per_source, unit.shape[1]), BF)
    return kernel_call(
        functools.partial(pack_rest, steps, per_source),
        [block] * len(steps),
        [unit, tgt],
        "pack_rest",
    )


CHUNK = 256


def raise_best(best, keys, queries, triangular=False):
    rows = queries.shape[0]
    for start in range(0, rows, CHUNK):
        chunk = min(CHUNK, rows - start)
        count = start + chunk if triangular else keys.shape[0]
        sims = matmul(keys[:count, :], queries[start : start + chunk, :], ((1,), (1,)))
        filled = keys[:count, :LANES].astype(F32) < 1.5
        for first in range(0, chunk, LANES):
            allowed = filled
            if triangular:
                allowed = filled & (
                    iota((count, LANES), 0) < iota((count, LANES), 1) + (start + first)
                )
            part = jnp.where(allowed, sims[:, first : first + LANES], F32(-1.0))
            window = slice(start + first, start + first + LANES)
            best[:, window] = jnp.maximum(best[:, window], jnp.max(part, axis=0, keepdims=True))


def gather_group(blocks, cluster, out, me):
    per = blocks[0].shape[0] // CLUS_DEV
    for step, block in enumerate(blocks):
        place = (me & (len(blocks) - 1)) ^ step
        rows = pl.ds(pl.multiple_of(place * per, per), per)
        out[rows, :] = block[cluster * per : (cluster + 1) * per, :]


def score_pair(bests, groups, new, old, bit, me):
    later = (me & bit) == 0

    @pl.when(later)
    def _():
        raise_best(bests[new], groups[old], groups[new])

    @pl.when(jnp.logical_not(later))
    def _():
        raise_best(bests[old], groups[new], groups[old])


def fresh_best(rows):
    ones = jnp.ones((8, LANES), BF)
    heads = matmul(ones, rows[:, :LANES], ((1,), (1,)))[:1]
    return jnp.where(heads < 100.0, F32(-1.0), F32(UNFILLED))


def own_stage(cuts, bits, held, first, *refs):
    stages, refs = refs[:held], refs[held:]
    blocks, (send, best) = list(refs[:-2]), refs[-2:]
    before = blocks.pop(0) if held else None
    blocks.reverse()
    per = blocks[0].shape[0] // CLUS_DEV
    me = lax.axis_index("clus")
    core = lax.axis_index("blk")
    spans = list(zip(cuts, cuts[1:]))
    base = spans[first][0]
    if held:
        best[:, :base] = before[:, :base]
    for c in range(CLUS_DEV):
        rows = [best.at[c : c + 1, a:b] for a, b in spans]
        groups = []
        for stage in stages:
            start = spans[len(groups)][0]
            end = start + stage.shape[2]
            while len(groups) < first and spans[len(groups)][0] < end:
                a, b = spans[len(groups)]
                groups.append(stage.at[core, c, a - start : b - start])
        for i in range(first, len(spans)):
            a, b = spans[i]
            group = send.at[1, c, a - base : b - base]
            gather_group(blocks[(a - base) // per : (b - base) // per], c, group, me)
            groups.append(group)
            rows[i][...] = fresh_best(group)
            raise_best(rows[i], group, group, True)
            for j in range(i):
                score_pair(rows, groups, i, j, bits[j], me)
        send[0, c] = send[1, c]


def cross_stage(cuts, held, *refs):
    stages, before, best = refs[: held + 1], refs[held + 1], refs[held + 2]
    best[...] = before[...]

    @pl.when(lax.axis_index("blk") == 1)
    def _():
        new = stages[-1]
        for c in range(CLUS_DEV):
            base = 0
            for stage in stages:
                end = base + stage.shape[2]
                raise_best(best.at[c : c + 1, base:end], new.at[0, c], stage.at[1, c])
                base = end
            start = base - new.shape[2]
            for stage in stages[:-1]:
                raise_best(best.at[c : c + 1, start:base], stage.at[0, c], new.at[1, c])


def gather_late(*refs):
    blocks, out = refs[:-1], refs[-1]
    for c in range(CLUS_DEV):
        gather_group(blocks, c, out.at[c], lax.axis_index("clus"))


def own_late(cuts, bits, held, *refs):
    stages, (cat, before, best) = refs[:held], refs[held:]
    me = lax.axis_index("clus")
    core = lax.axis_index("blk")
    spans = list(zip(cuts, cuts[1:]))
    last = len(spans) - 1
    start = spans[last][0]
    best[:, :start] = before[:, :start]
    for c in range(CLUS_DEV):
        rows = [best.at[c : c + 1, a:b] for a, b in spans]
        groups = [stage.at[core, c] for stage in stages] + [cat.at[c]]
        rows[last][...] = fresh_best(groups[last])
        raise_best(rows[last], groups[last], groups[last], True)
        for i in range(last):
            score_pair(rows, groups, last, i, bits[i], me)


def cross_late(cuts, per, held, *refs):
    stages, (cat, before, other, out, best) = refs[:held], refs[held:]
    me = lax.axis_index("clus")
    core = lax.axis_index("blk")
    spans = list(zip(cuts, cuts[1:]))
    best[...] = before[...]

    @pl.when(core == 1)
    def _():
        for c in range(CLUS_DEV):
            rows = [best.at[c : c + 1, a:b] for a, b in spans]
            for row, stage in zip(rows, stages):
                raise_best(row, other.at[c], stage.at[1, c])
                raise_best(rows[held], stage.at[0, c], cat.at[c])
            raise_best(rows[held], other.at[c], cat.at[c])

    for a, b in spans:
        place = (me ^ (a // per)) & ~((b - a) // per - 1)
        value = best[:, a:b]
        at = pl.ds(pl.multiple_of(place * per, LANES), b - a)
        out[:, at] = jnp.where(value > 0.5 * UNFILLED, F32(0.0), value)


def local(embeddings, cluster_ids):
    owners = lax.axis_size("clus")
    clusters = CLUS_DEV * owners
    rows, width = embeddings.shape
    per = 2 * rows // clusters
    bits = [owners // 2, owners // 4]
    bounds = [0, owners // 2, owners // 2 + owners // 4, owners]
    cuts = [x * per for x in bounds]
    near, far, late = [list(range(a, b)) for a, b in zip(bounds, bounds[1:])]
    best_shape = jax.ShapeDtypeStruct((CLUS_DEV, rows), F32)

    def to_owner(block, step):
        return lax.ppermute(block, "clus", [(i, i ^ step) for i in range(owners)])

    def stage_shape(sources):
        return jax.ShapeDtypeStruct((2, CLUS_DEV, sources * per, width), BF)

    def to_both(send):
        return lax.all_to_all(send, "blk", split_axis=0, concat_axis=0, tiled=True)

    arrived = {}
    lead = far[:1]
    unit, tgt, *packed = call_pack_first(embeddings, cluster_ids, lead, clusters, per)
    for steps in (near[1:] + far[1:] + [0], []):
        for step, block in zip(lead, packed):
            arrived[step] = to_owner(block, step) if step else block
        lead, packed = steps, call_pack_rest(unit, tgt, steps, per) if steps else []
    packed = call_pack_rest(unit, tgt, late, per)
    *held, arrived[far[0]] = lax.optimization_barrier((*packed, arrived[far[0]]))
    for step, block in zip(late, held):
        arrived[step] = to_owner(block, step)

    send, best = kernel_call(
        functools.partial(own_stage, cuts[:2], bits, 0, 0),
        [stage_shape(len(near)), best_shape],
        [arrived[s] for s in reversed(near)],
        "own_near",
    )
    stages = [to_both(send)]
    (best,) = kernel_call(
        functools.partial(cross_stage, cuts, 0), [best_shape], stages + [best], "cross_near"
    )
    arrived[far[-1]], best = lax.optimization_barrier((arrived[far[-1]], best))
    send, best = kernel_call(
        functools.partial(own_stage, cuts[:3], bits, 1, 1),
        [stage_shape(len(far)), best_shape],
        stages + [best] + [arrived[s] for s in reversed(far)],
        "own_far",
    )
    stages.append(to_both(send))
    (best,) = kernel_call(
        functools.partial(cross_stage, cuts, 1), [best_shape], stages + [best], "cross_far"
    )
    *new, best = lax.optimization_barrier((*[arrived[s] for s in late], best))
    cat_shape = jax.ShapeDtypeStruct((CLUS_DEV, len(late) * per, width), BF)
    (cat,) = kernel_call(gather_late, [cat_shape], new, "gather_late")
    other = lax.ppermute(cat, "blk", [(0, 1)])
    (best,) = kernel_call(
        functools.partial(own_late, cuts, bits, 2), [best_shape], stages + [cat, best], "own_late"
    )
    (out,) = kernel_call(
        functools.partial(cross_late, cuts, per, 2),
        [best_shape],
        stages + [cat, best, other],
        "cross_late",
        [pltpu.VMEM((CLUS_DEV, rows), F32)],
    )
    return out


def solution(mesh):
    placed = (P(("groups", "clus", "blk"), None), P(("groups", "clus", "blk"), None))
    return jax.shard_map(
        local, mesh=mesh, in_specs=placed, out_specs=P(("groups", "clus"), "blk"), check_vma=False
    )
```

```python
import functools

import jax
import jax.numpy as jnp
from jax import lax
from jax.experimental import pallas as pl
from jax.experimental.pallas import tpu as pltpu
from jax.sharding import PartitionSpec as P

CLUS_DEV = 2
LANES = 128
MARK = 2.0
UNFILLED = 8.0
BF = jnp.bfloat16
F32 = jnp.float32


def iota(shape, dim):
    return lax.broadcasted_iota(jnp.int32, shape, dim)


def matmul(a, b, contract):
    return lax.dot_general(a, b, (contract, ((), ())), preferred_element_type=F32)


def targets(ids, clusters, per_source):
    groups = ids.shape[1] // LANES
    parts = [ids[:, g * LANES : (g + 1) * LANES] for g in range(groups)]
    hot = jnp.concatenate(
        [(iota((clusters, LANES), 0) == part).astype(F32) for part in parts], axis=0
    )
    stacked = groups * clusters
    earlier = (iota((LANES, LANES), 0) < iota((LANES, LANES), 1)).astype(F32).astype(BF)
    within = matmul(hot.astype(BF), earlier, ((1,), (0,)))
    totals = jnp.broadcast_to(jnp.sum(hot, axis=1, keepdims=True), (stacked, LANES))
    a, b = iota((stacked, stacked), 0), iota((stacked, stacked), 1)
    chunks_before = ((a % clusters == b % clusters) & (b < a)).astype(F32).astype(BF)
    before = within + matmul(chunks_before, totals.astype(BF), ((1,), (0,)))
    picked = hot * before
    out = [
        jnp.sum(picked[g * clusters : (g + 1) * clusters], axis=0, keepdims=True).astype(jnp.int32)
        + parts[g] * per_source
        for g in range(groups)
    ]
    return jnp.concatenate(out, axis=1)


def pack_block(unit, tgt, dest, width):
    hit = (tgt - dest * width) == iota((width, tgt.shape[1]), 0)
    hot = hit.astype(F32)
    rows = matmul(hot.astype(BF), unit, ((1,), (0,)))
    empty = jnp.max(hot, axis=1, keepdims=True) < 0.5
    head = jnp.where(empty, F32(MARK), rows[:, :LANES])
    return head.astype(BF), rows[:, LANES:].astype(BF)


def store_blocks(unit, tgt, steps, width, outs):
    me = lax.axis_index("clus")
    for step, out in zip(steps, outs):
        head, tail = pack_block(unit, tgt, me ^ step, width)
        out[:, :LANES] = head
        out[:, LANES:] = tail


PIECES = 4


def pack_first(steps, clusters, per_source, emb, ids, unit, tgt, *refs):
    outs, (raw, raw_ids, sems, ids_sem) = refs[:-4], refs[-4:]
    size = emb.shape[0] // PIECES
    ids_copy = pltpu.make_async_copy(ids, raw_ids, ids_sem)
    ids_copy.start()
    windows = [pl.ds(piece * size, size) for piece in range(PIECES)]
    copies = [
        pltpu.make_async_copy(emb.at[window], raw.at[window], sems.at[piece])
        for piece, window in enumerate(windows)
    ]
    for copy in copies:
        copy.start()
    ids_copy.wait()
    tgt[...] = targets(raw_ids[...], clusters, per_source)
    for copy, window in zip(copies, windows):
        copy.wait()
        values = raw[window, :].astype(F32)
        scale = lax.rsqrt(jnp.sum(values * values, axis=1, keepdims=True) + 1e-6)
        unit[window, :] = (values * scale).astype(BF)
    store_blocks(unit[...], tgt[...], steps, CLUS_DEV * per_source, outs)


def pack_rest(steps, per_source, unit, tgt, *outs):
    store_blocks(unit[...], tgt[...], steps, CLUS_DEV * per_source, outs)


VMEM = pl.BlockSpec(memory_space=pltpu.VMEM)


def kernel_call(kernel, shapes, inputs, name, scratch=(), place=VMEM, grant=20 * 2**20):
    return pl.pallas_call(
        kernel,
        out_shape=shapes,
        in_specs=[place] * len(inputs),
        out_specs=[VMEM] * len(shapes),
        scratch_shapes=scratch,
        compiler_params=pltpu.CompilerParams(vmem_limit_bytes=grant),
        cost_estimate=pl.CostEstimate(flops=1000, bytes_accessed=1000, transcendentals=0),
        name=name,
    )(*inputs)


def call_pack_first(emb, ids, steps, clusters, per_source):
    block = jax.ShapeDtypeStruct((CLUS_DEV * per_source, emb.shape[1]), BF)
    shapes = [jax.ShapeDtypeStruct(emb.shape, BF), jax.ShapeDtypeStruct(ids.shape, jnp.int32)]
    return kernel_call(
        functools.partial(pack_first, steps, clusters, per_source),
        shapes + [block] * len(steps),
        [emb, ids],
        place=pl.BlockSpec(memory_space=pl.ANY),
        grant=50 * 2**20,
        name="pack_first",
        scratch=[
            pltpu.VMEM(emb.shape, BF),
            pltpu.VMEM(ids.shape, jnp.int32),
            pltpu.SemaphoreType.DMA((PIECES,)),
            pltpu.SemaphoreType.DMA,
        ],
    )


def call_pack_rest(unit, tgt, steps, per_source):
    block = jax.ShapeDtypeStruct((CLUS_DEV * per_source, unit.shape[1]), BF)
    return kernel_call(
        functools.partial(pack_rest, steps, per_source),
        [block] * len(steps),
        [unit, tgt],
        "pack_rest",
    )


CHUNK = 256


def raise_best(best, keys, queries, triangular=False):
    rows = queries.shape[0]
    for start in range(0, rows, CHUNK):
        chunk = min(CHUNK, rows - start)
        count = start + chunk if triangular else keys.shape[0]
        sims = matmul(keys[:count, :], queries[start : start + chunk, :], ((1,), (1,)))
        filled = keys[:count, :LANES].astype(F32) < 1.5
        for first in range(0, chunk, LANES):
            allowed = filled
            if triangular:
                allowed = filled & (
                    iota((count, LANES), 0) < iota((count, LANES), 1) + (start + first)
                )
            part = jnp.where(allowed, sims[:, first : first + LANES], F32(-1.0))
            window = slice(start + first, start + first + LANES)
            best[:, window] = jnp.maximum(best[:, window], jnp.max(part, axis=0, keepdims=True))


def gather_group(blocks, cluster, out, me):
    per = blocks[0].shape[0] // CLUS_DEV
    for step, block in enumerate(blocks):
        place = (me & (len(blocks) - 1)) ^ step
        rows = pl.ds(pl.multiple_of(place * per, per), per)
        out[rows, :] = block[cluster * per : (cluster + 1) * per, :]


def score_pair(bests, groups, new, old, bit, me):
    later = (me & bit) == 0

    @pl.when(later)
    def _():
        raise_best(bests[new], groups[old], groups[new])

    @pl.when(jnp.logical_not(later))
    def _():
        raise_best(bests[old], groups[new], groups[old])


def fresh_best(rows):
    ones = jnp.ones((8, LANES), BF)
    heads = matmul(ones, rows[:, :LANES], ((1,), (1,)))[:1]
    return jnp.where(heads < 100.0, F32(-1.0), F32(UNFILLED))


def own_stage(cuts, bits, held, first, *refs):
    stages, refs = refs[:held], refs[held:]
    blocks, (send, best) = list(refs[:-2]), refs[-2:]
    before = blocks.pop(0) if held else None
    blocks.reverse()
    per = blocks[0].shape[0] // CLUS_DEV
    me = lax.axis_index("clus")
    core = lax.axis_index("blk")
    spans = list(zip(cuts, cuts[1:]))
    base = spans[first][0]
    if held:
        best[:, :base] = before[:, :base]
    for c in range(CLUS_DEV):
        rows = [best.at[c : c + 1, a:b] for a, b in spans]
        groups = []
        for stage in stages:
            start = spans[len(groups)][0]
            end = start + stage.shape[2]
            while len(groups) < first and spans[len(groups)][0] < end:
                a, b = spans[len(groups)]
                groups.append(stage.at[core, c, a - start : b - start])
        for i in range(first, len(spans)):
            a, b = spans[i]
            group = send.at[1, c, a - base : b - base]
            gather_group(blocks[(a - base) // per : (b - base) // per], c, group, me)
            groups.append(group)
            rows[i][...] = fresh_best(group)
            raise_best(rows[i], group, group, True)
            for j in range(i):
                score_pair(rows, groups, i, j, bits[j], me)
        send[0, c] = send[1, c]


def cross_stage(cuts, held, *refs):
    stages, before, best = refs[: held + 1], refs[held + 1], refs[held + 2]
    best[...] = before[...]

    @pl.when(lax.axis_index("blk") == 1)
    def _():
        new = stages[-1]
        for c in range(CLUS_DEV):
            base = 0
            for stage in stages:
                end = base + stage.shape[2]
                raise_best(best.at[c : c + 1, base:end], new.at[0, c], stage.at[1, c])
                base = end
            start = base - new.shape[2]
            for stage in stages[:-1]:
                raise_best(best.at[c : c + 1, start:base], stage.at[0, c], new.at[1, c])


def gather_late(*refs):
    blocks, out = refs[:-1], refs[-1]
    for c in range(CLUS_DEV):
        gather_group(blocks, c, out.at[c], lax.axis_index("clus"))


def own_late(cuts, bits, held, *refs):
    stages, (cat, before, best) = refs[:held], refs[held:]
    me = lax.axis_index("clus")
    core = lax.axis_index("blk")
    spans = list(zip(cuts, cuts[1:]))
    last = len(spans) - 1
    start = spans[last][0]
    best[:, :start] = before[:, :start]
    for c in range(CLUS_DEV):
        rows = [best.at[c : c + 1, a:b] for a, b in spans]
        groups = [stages[0].at[core, c, a:b] for a, b in spans[:-1]] + [cat.at[c]]
        rows[last][...] = fresh_best(groups[last])
        raise_best(rows[last], groups[last], groups[last], True)
        for i in range(last):
            score_pair(rows, groups, last, i, bits[i], me)


def cross_late(cuts, per, held, *refs):
    stages, (cat, before, other, out, best) = refs[:held], refs[held:]
    me = lax.axis_index("clus")
    core = lax.axis_index("blk")
    spans = list(zip(cuts, cuts[1:]))
    best[...] = before[...]

    @pl.when(core == 1)
    def _():
        start = spans[-1][0]
        for c in range(CLUS_DEV):
            fresh = best.at[c : c + 1, start:]
            raise_best(best.at[c : c + 1, :start], other.at[c], stages[0].at[1, c])
            raise_best(fresh, stages[0].at[0, c], cat.at[c])
            raise_best(fresh, other.at[c], cat.at[c])

    for a, b in spans:
        place = (me ^ (a // per)) & ~((b - a) // per - 1)
        value = best[:, a:b]
        at = pl.ds(pl.multiple_of(place * per, LANES), b - a)
        out[:, at] = jnp.where(value > 0.5 * UNFILLED, F32(0.0), value)


def local(embeddings, cluster_ids):
    owners = lax.axis_size("clus")
    clusters = CLUS_DEV * owners
    rows, width = embeddings.shape
    per = 2 * rows // clusters
    bits = [owners // 2, owners // 4]
    bounds = [0, owners // 2, owners // 2 + owners // 4, owners]
    cuts = [x * per for x in bounds]
    near, far, late = [list(range(a, b)) for a, b in zip(bounds, bounds[1:])]
    best_shape = jax.ShapeDtypeStruct((CLUS_DEV, rows), F32)

    def to_owner(block, step):
        return lax.ppermute(block, "clus", [(i, i ^ step) for i in range(owners)])

    def stage_shape(sources):
        return jax.ShapeDtypeStruct((2, CLUS_DEV, sources * per, width), BF)

    def to_both(send):
        return lax.all_to_all(send, "blk", split_axis=0, concat_axis=0, tiled=True)

    arrived = {}
    lead = far[:1]
    unit, tgt, *packed = call_pack_first(embeddings, cluster_ids, lead, clusters, per)
    for steps in (near[1:] + far[1:] + [0], []):
        for step, block in zip(lead, packed):
            arrived[step] = to_owner(block, step) if step else block
        lead, packed = steps, call_pack_rest(unit, tgt, steps, per) if steps else []
    packed = call_pack_rest(unit, tgt, late, per)
    *held, arrived[far[0]] = lax.optimization_barrier((*packed, arrived[far[0]]))
    for step, block in zip(late, held):
        arrived[step] = to_owner(block, step)

    early = near + far
    send, best = kernel_call(
        functools.partial(own_stage, cuts[:3], bits, 0, 0),
        [stage_shape(len(early)), best_shape],
        [arrived[s] for s in reversed(early)],
        "own_early",
    )
    stages = [to_both(send)]
    (best,) = kernel_call(
        functools.partial(cross_stage, cuts, 0), [best_shape], stages + [best], "cross_early"
    )
    *new, best = lax.optimization_barrier((*[arrived[s] for s in late], best))
    cat_shape = jax.ShapeDtypeStruct((CLUS_DEV, len(late) * per, width), BF)
    (cat,) = kernel_call(gather_late, [cat_shape], new, "gather_late")
    other = lax.ppermute(cat, "blk", [(0, 1)])
    (best,) = kernel_call(
        functools.partial(own_late, cuts, bits, 1), [best_shape], stages + [cat, best], "own_late"
    )
    (out,) = kernel_call(
        functools.partial(cross_late, cuts, per, 1),
        [best_shape],
        stages + [cat, best, other],
        "cross_late",
        [pltpu.VMEM((CLUS_DEV, rows), F32)],
    )
    return out


def solution(mesh):
    placed = (P(("groups", "clus", "blk"), None), P(("groups", "clus", "blk"), None))
    return jax.shard_map(
        local, mesh=mesh, in_specs=placed, out_specs=P(("groups", "clus"), "blk"), check_vma=False
    )
```

```python
import functools

import jax
import jax.numpy as jnp
from jax import lax
from jax.experimental import pallas as pl
from jax.experimental.pallas import tpu as pltpu
from jax.sharding import PartitionSpec as P

CLUS_DEV = 2
LANES = 128
MARK = 2.0
UNFILLED = 8.0
BF = jnp.bfloat16
F32 = jnp.float32


def iota(shape, dim):
    return lax.broadcasted_iota(jnp.int32, shape, dim)


def matmul(a, b, contract):
    return lax.dot_general(a, b, (contract, ((), ())), preferred_element_type=F32)


def targets(ids, clusters, per_source):
    groups = ids.shape[1] // LANES
    parts = [ids[:, g * LANES : (g + 1) * LANES] for g in range(groups)]
    hot = jnp.concatenate(
        [(iota((clusters, LANES), 0) == part).astype(F32) for part in parts], axis=0
    )
    stacked = groups * clusters
    earlier = (iota((LANES, LANES), 0) < iota((LANES, LANES), 1)).astype(F32).astype(BF)
    within = matmul(hot.astype(BF), earlier, ((1,), (0,)))
    totals = jnp.broadcast_to(jnp.sum(hot, axis=1, keepdims=True), (stacked, LANES))
    a, b = iota((stacked, stacked), 0), iota((stacked, stacked), 1)
    chunks_before = ((a % clusters == b % clusters) & (b < a)).astype(F32).astype(BF)
    before = within + matmul(chunks_before, totals.astype(BF), ((1,), (0,)))
    picked = hot * before
    out = [
        jnp.sum(picked[g * clusters : (g + 1) * clusters], axis=0, keepdims=True).astype(jnp.int32)
        + parts[g] * per_source
        for g in range(groups)
    ]
    return jnp.concatenate(out, axis=1)


def pack_block(unit, tgt, dest, width):
    hit = (tgt - dest * width) == iota((width, tgt.shape[1]), 0)
    hot = hit.astype(F32)
    rows = matmul(hot.astype(BF), unit, ((1,), (0,)))
    empty = jnp.max(hot, axis=1, keepdims=True) < 0.5
    head = jnp.where(empty, F32(MARK), rows[:, :LANES])
    return head.astype(BF), rows[:, LANES:].astype(BF)


def store_blocks(unit, tgt, steps, width, outs):
    me = lax.axis_index("clus")
    for step, out in zip(steps, outs):
        head, tail = pack_block(unit, tgt, me ^ step, width)
        out[:, :LANES] = head
        out[:, LANES:] = tail


PIECES = 4


def pack_first(steps, clusters, per_source, emb, ids, unit, tgt, *refs):
    outs, (raw, raw_ids, sems, ids_sem) = refs[:-4], refs[-4:]
    size = emb.shape[0] // PIECES
    ids_copy = pltpu.make_async_copy(ids, raw_ids, ids_sem)
    ids_copy.start()
    windows = [pl.ds(piece * size, size) for piece in range(PIECES)]
    copies = [
        pltpu.make_async_copy(emb.at[window], raw.at[window], sems.at[piece])
        for piece, window in enumerate(windows)
    ]
    for copy in copies:
        copy.start()
    ids_copy.wait()
    tgt[...] = targets(raw_ids[...], clusters, per_source)
    for copy, window in zip(copies, windows):
        copy.wait()
        values = raw[window, :].astype(F32)
        scale = lax.rsqrt(jnp.sum(values * values, axis=1, keepdims=True) + 1e-6)
        unit[window, :] = (values * scale).astype(BF)
    store_blocks(unit[...], tgt[...], steps, CLUS_DEV * per_source, outs)


def pack_rest(steps, per_source, unit, tgt, *outs):
    store_blocks(unit[...], tgt[...], steps, CLUS_DEV * per_source, outs)


VMEM = pl.BlockSpec(memory_space=pltpu.VMEM)


def kernel_call(kernel, shapes, inputs, name, scratch=(), place=VMEM, grant=20 * 2**20):
    return pl.pallas_call(
        kernel,
        out_shape=shapes,
        in_specs=[place] * len(inputs),
        out_specs=[VMEM] * len(shapes),
        scratch_shapes=scratch,
        compiler_params=pltpu.CompilerParams(vmem_limit_bytes=grant),
        cost_estimate=pl.CostEstimate(flops=1000, bytes_accessed=1000, transcendentals=0),
        name=name,
    )(*inputs)


def call_pack_first(emb, ids, steps, clusters, per_source):
    block = jax.ShapeDtypeStruct((CLUS_DEV * per_source, emb.shape[1]), BF)
    shapes = [jax.ShapeDtypeStruct(emb.shape, BF), jax.ShapeDtypeStruct(ids.shape, jnp.int32)]
    return kernel_call(
        functools.partial(pack_first, steps, clusters, per_source),
        shapes + [block] * len(steps),
        [emb, ids],
        place=pl.BlockSpec(memory_space=pl.ANY),
        grant=50 * 2**20,
        name="pack_first",
        scratch=[
            pltpu.VMEM(emb.shape, BF),
            pltpu.VMEM(ids.shape, jnp.int32),
            pltpu.SemaphoreType.DMA((PIECES,)),
            pltpu.SemaphoreType.DMA,
        ],
    )


def call_pack_rest(unit, tgt, steps, per_source):
    block = jax.ShapeDtypeStruct((CLUS_DEV * per_source, unit.shape[1]), BF)
    return kernel_call(
        functools.partial(pack_rest, steps, per_source),
        [block] * len(steps),
        [unit, tgt],
        "pack_rest",
    )


CHUNK = 256


def raise_best(best, keys, queries, triangular=False):
    rows = queries.shape[0]
    for start in range(0, rows, CHUNK):
        chunk = min(CHUNK, rows - start)
        count = start + chunk if triangular else keys.shape[0]
        sims = matmul(keys[:count, :], queries[start : start + chunk, :], ((1,), (1,)))
        filled = keys[:count, :LANES].astype(F32) < 1.5
        for first in range(0, chunk, LANES):
            allowed = filled
            if triangular:
                allowed = filled & (
                    iota((count, LANES), 0) < iota((count, LANES), 1) + (start + first)
                )
            part = jnp.where(allowed, sims[:, first : first + LANES], F32(-1.0))
            window = slice(start + first, start + first + LANES)
            best[:, window] = jnp.maximum(best[:, window], jnp.max(part, axis=0, keepdims=True))


def gather_group(blocks, cluster, out, me):
    per = blocks[0].shape[0] // CLUS_DEV
    for step, block in enumerate(blocks):
        place = (me & (len(blocks) - 1)) ^ step
        rows = pl.ds(pl.multiple_of(place * per, per), per)
        out[rows, :] = block[cluster * per : (cluster + 1) * per, :]


def score_pair(bests, groups, new, old, bit, me):
    later = (me & bit) == 0

    @pl.when(later)
    def _():
        raise_best(bests[new], groups[old], groups[new])

    @pl.when(jnp.logical_not(later))
    def _():
        raise_best(bests[old], groups[new], groups[old])


def fresh_best(rows):
    ones = jnp.ones((8, LANES), BF)
    heads = matmul(ones, rows[:, :LANES], ((1,), (1,)))[:1]
    return jnp.where(heads < 100.0, F32(-1.0), F32(UNFILLED))


def own_stage(cuts, bits, held, first, *refs):
    stages, refs = refs[:held], refs[held:]
    blocks, (send, best) = list(refs[:-2]), refs[-2:]
    before = blocks.pop(0) if held else None
    blocks.reverse()
    per = blocks[0].shape[0] // CLUS_DEV
    me = lax.axis_index("clus")
    core = lax.axis_index("blk")
    spans = list(zip(cuts, cuts[1:]))
    base = spans[first][0]
    if held:
        best[:, :base] = before[:, :base]
    for c in range(CLUS_DEV):
        rows = [best.at[c : c + 1, a:b] for a, b in spans]
        groups = []
        for stage in stages:
            start = spans[len(groups)][0]
            end = start + stage.shape[2]
            while len(groups) < first and spans[len(groups)][0] < end:
                a, b = spans[len(groups)]
                groups.append(stage.at[core, c, a - start : b - start])
        for i in range(first, len(spans)):
            a, b = spans[i]
            group = send.at[1, c, a - base : b - base]
            gather_group(blocks[(a - base) // per : (b - base) // per], c, group, me)
            groups.append(group)
            rows[i][...] = fresh_best(group)
            raise_best(rows[i], group, group, True)
            for j in range(i):
                score_pair(rows, groups, i, j, bits[j], me)
        send[0, c] = send[1, c]


def cross_stage(cuts, held, *refs):
    stages, before, best = refs[: held + 1], refs[held + 1], refs[held + 2]
    best[...] = before[...]

    @pl.when(lax.axis_index("blk") == 1)
    def _():
        new = stages[-1]
        for c in range(CLUS_DEV):
            base = 0
            for stage in stages:
                end = base + stage.shape[2]
                raise_best(best.at[c : c + 1, base:end], new.at[0, c], stage.at[1, c])
                base = end
            start = base - new.shape[2]
            for stage in stages[:-1]:
                raise_best(best.at[c : c + 1, start:base], stage.at[0, c], new.at[1, c])


def gather_late(*refs):
    blocks, out = refs[:-1], refs[-1]
    for c in range(CLUS_DEV):
        gather_group(blocks, c, out.at[c], lax.axis_index("clus"))


def own_late(cuts, bits, held, *refs):
    stages, (cat, before, best) = refs[:held], refs[held:]
    me = lax.axis_index("clus")
    core = lax.axis_index("blk")
    spans = list(zip(cuts, cuts[1:]))
    last = len(spans) - 1
    start = spans[last][0]
    best[:, :start] = before[:, :start]
    for c in range(CLUS_DEV):
        rows = [best.at[c : c + 1, a:b] for a, b in spans]
        groups = [stages[0].at[core, c, a:b] for a, b in spans[:-1]] + [cat.at[c]]
        rows[last][...] = fresh_best(groups[last])
        raise_best(rows[last], groups[last], groups[last], True)
        for i in range(last):
            score_pair(rows, groups, last, i, bits[i], me)

    @pl.when(core == 1)
    def _():
        for c in range(CLUS_DEV):
            raise_best(best.at[c : c + 1, start:], stages[0].at[0, c], cat.at[c])


def cross_late(cuts, per, held, *refs):
    stages, (cat, before, other, out, best) = refs[:held], refs[held:]
    me = lax.axis_index("clus")
    core = lax.axis_index("blk")
    spans = list(zip(cuts, cuts[1:]))
    best[...] = before[...]

    @pl.when(core == 1)
    def _():
        start = spans[-1][0]
        for c in range(CLUS_DEV):
            fresh = best.at[c : c + 1, start:]
            raise_best(best.at[c : c + 1, :start], other.at[c], stages[0].at[1, c])
            raise_best(fresh, other.at[c], cat.at[c])

    for a, b in spans:
        place = (me ^ (a // per)) & ~((b - a) // per - 1)
        value = best[:, a:b]
        at = pl.ds(pl.multiple_of(place * per, LANES), b - a)
        out[:, at] = jnp.where(value > 0.5 * UNFILLED, F32(0.0), value)


def local(embeddings, cluster_ids):
    owners = lax.axis_size("clus")
    clusters = CLUS_DEV * owners
    rows, width = embeddings.shape
    per = 2 * rows // clusters
    bits = [owners // 2, owners // 4]
    bounds = [0, owners // 2, owners // 2 + owners // 4, owners]
    cuts = [x * per for x in bounds]
    near, far, late = [list(range(a, b)) for a, b in zip(bounds, bounds[1:])]
    best_shape = jax.ShapeDtypeStruct((CLUS_DEV, rows), F32)

    def to_owner(block, step):
        return lax.ppermute(block, "clus", [(i, i ^ step) for i in range(owners)])

    def stage_shape(sources):
        return jax.ShapeDtypeStruct((2, CLUS_DEV, sources * per, width), BF)

    def to_both(send):
        return lax.all_to_all(send, "blk", split_axis=0, concat_axis=0, tiled=True)

    arrived = {}
    lead = far[:1]
    unit, tgt, *packed = call_pack_first(embeddings, cluster_ids, lead, clusters, per)
    for steps in (near[1:] + far[1:] + [0], []):
        for step, block in zip(lead, packed):
            arrived[step] = to_owner(block, step) if step else block
        lead, packed = steps, call_pack_rest(unit, tgt, steps, per) if steps else []
    packed = call_pack_rest(unit, tgt, late, per)
    *held, arrived[far[0]] = lax.optimization_barrier((*packed, arrived[far[0]]))
    for step, block in zip(late, held):
        arrived[step] = to_owner(block, step)

    early = near + far
    send, best = kernel_call(
        functools.partial(own_stage, cuts[:3], bits, 0, 0),
        [stage_shape(len(early)), best_shape],
        [arrived[s] for s in reversed(early)],
        "own_early",
    )
    stages = [to_both(send)]
    (best,) = kernel_call(
        functools.partial(cross_stage, cuts, 0), [best_shape], stages + [best], "cross_early"
    )
    *new, best = lax.optimization_barrier((*[arrived[s] for s in late], best))
    cat_shape = jax.ShapeDtypeStruct((CLUS_DEV, len(late) * per, width), BF)
    (cat,) = kernel_call(gather_late, [cat_shape], new, "gather_late")
    other = lax.ppermute(cat, "blk", [(0, 1)])
    (best,) = kernel_call(
        functools.partial(own_late, cuts, bits, 1), [best_shape], stages + [cat, best], "own_late"
    )
    (out,) = kernel_call(
        functools.partial(cross_late, cuts, per, 1),
        [best_shape],
        stages + [cat, best, other],
        "cross_late",
        [pltpu.VMEM((CLUS_DEV, rows), F32)],
    )
    return out


def solution(mesh):
    placed = (P(("groups", "clus", "blk"), None), P(("groups", "clus", "blk"), None))
    return jax.shard_map(
        local, mesh=mesh, in_specs=placed, out_specs=P(("groups", "clus"), "blk"), check_vma=False
    )
```

```python
import functools

import jax
import jax.numpy as jnp
from jax import lax
from jax.experimental import pallas as pl
from jax.experimental.pallas import tpu as pltpu
from jax.sharding import PartitionSpec as P

CLUS_DEV = 2
LANES = 128
MARK = 2.0
UNFILLED = 8.0
BF = jnp.bfloat16
F32 = jnp.float32


def iota(shape, dim):
    return lax.broadcasted_iota(jnp.int32, shape, dim)


def matmul(a, b, contract):
    return lax.dot_general(a, b, (contract, ((), ())), preferred_element_type=F32)


def targets(ids, clusters, per_source):
    groups = ids.shape[1] // LANES
    parts = [ids[:, g * LANES : (g + 1) * LANES] for g in range(groups)]
    hot = jnp.concatenate(
        [(iota((clusters, LANES), 0) == part).astype(F32) for part in parts], axis=0
    )
    stacked = groups * clusters
    earlier = (iota((LANES, LANES), 0) < iota((LANES, LANES), 1)).astype(F32).astype(BF)
    within = matmul(hot.astype(BF), earlier, ((1,), (0,)))
    totals = jnp.broadcast_to(jnp.sum(hot, axis=1, keepdims=True), (stacked, LANES))
    a, b = iota((stacked, stacked), 0), iota((stacked, stacked), 1)
    chunks_before = ((a % clusters == b % clusters) & (b < a)).astype(F32).astype(BF)
    before = within + matmul(chunks_before, totals.astype(BF), ((1,), (0,)))
    picked = hot * before
    out = [
        jnp.sum(picked[g * clusters : (g + 1) * clusters], axis=0, keepdims=True).astype(jnp.int32)
        + parts[g] * per_source
        for g in range(groups)
    ]
    return jnp.concatenate(out, axis=1)


def pack_block(unit, tgt, dest, width):
    hit = (tgt - dest * width) == iota((width, tgt.shape[1]), 0)
    hot = hit.astype(F32)
    rows = matmul(hot.astype(BF), unit, ((1,), (0,)))
    empty = jnp.max(hot, axis=1, keepdims=True) < 0.5
    head = jnp.where(empty, F32(MARK), rows[:, :LANES])
    return head.astype(BF), rows[:, LANES:].astype(BF)


def store_blocks(unit, tgt, steps, width, outs):
    me = lax.axis_index("clus")
    for step, out in zip(steps, outs):
        head, tail = pack_block(unit, tgt, me ^ step, width)
        out[:, :LANES] = head
        out[:, LANES:] = tail


PIECES = 4


def pack_first(steps, clusters, per_source, emb, ids, unit, tgt, *refs):
    outs, (raw, raw_ids, sems, ids_sem) = refs[:-4], refs[-4:]
    size = emb.shape[0] // PIECES
    ids_copy = pltpu.make_async_copy(ids, raw_ids, ids_sem)
    ids_copy.start()
    windows = [pl.ds(piece * size, size) for piece in range(PIECES)]
    copies = [
        pltpu.make_async_copy(emb.at[window], raw.at[window], sems.at[piece])
        for piece, window in enumerate(windows)
    ]
    for copy in copies:
        copy.start()
    ids_copy.wait()
    tgt[...] = targets(raw_ids[...], clusters, per_source)
    for copy, window in zip(copies, windows):
        copy.wait()
        values = raw[window, :].astype(F32)
        scale = lax.rsqrt(jnp.sum(values * values, axis=1, keepdims=True) + 1e-6)
        unit[window, :] = (values * scale).astype(BF)
    store_blocks(unit[...], tgt[...], steps, CLUS_DEV * per_source, outs)


def pack_rest(steps, per_source, unit, tgt, *outs):
    store_blocks(unit[...], tgt[...], steps, CLUS_DEV * per_source, outs)


VMEM = pl.BlockSpec(memory_space=pltpu.VMEM)


def kernel_call(kernel, shapes, inputs, name, scratch=(), place=VMEM, grant=20 * 2**20):
    return pl.pallas_call(
        kernel,
        out_shape=shapes,
        in_specs=[place] * len(inputs),
        out_specs=[VMEM] * len(shapes),
        scratch_shapes=scratch,
        compiler_params=pltpu.CompilerParams(vmem_limit_bytes=grant),
        cost_estimate=pl.CostEstimate(flops=1000, bytes_accessed=1000, transcendentals=0),
        name=name,
    )(*inputs)


def call_pack_first(emb, ids, steps, clusters, per_source):
    block = jax.ShapeDtypeStruct((CLUS_DEV * per_source, emb.shape[1]), BF)
    shapes = [jax.ShapeDtypeStruct(emb.shape, BF), jax.ShapeDtypeStruct(ids.shape, jnp.int32)]
    return kernel_call(
        functools.partial(pack_first, steps, clusters, per_source),
        shapes + [block] * len(steps),
        [emb, ids],
        place=pl.BlockSpec(memory_space=pl.ANY),
        grant=50 * 2**20,
        name="pack_first",
        scratch=[
            pltpu.VMEM(emb.shape, BF),
            pltpu.VMEM(ids.shape, jnp.int32),
            pltpu.SemaphoreType.DMA((PIECES,)),
            pltpu.SemaphoreType.DMA,
        ],
    )


def call_pack_rest(unit, tgt, steps, per_source):
    block = jax.ShapeDtypeStruct((CLUS_DEV * per_source, unit.shape[1]), BF)
    return kernel_call(
        functools.partial(pack_rest, steps, per_source),
        [block] * len(steps),
        [unit, tgt],
        "pack_rest",
    )


CHUNK = 256


def raise_best(best, keys, queries, triangular=False):
    rows = queries.shape[0]
    chunk = min(CHUNK, rows) if triangular else rows
    for start in range(0, rows, chunk):
        count = start + chunk if triangular else keys.shape[0]
        sims = matmul(keys[:count, :], queries[start : start + chunk, :], ((1,), (1,)))
        filled = keys[:count, :LANES].astype(F32) < 1.5
        parts = []
        for first in range(0, chunk, LANES):
            allowed = filled
            if triangular:
                allowed = filled & (
                    iota((count, LANES), 0) < iota((count, LANES), 1) + (start + first)
                )
            part = jnp.where(allowed, sims[:, first : first + LANES], F32(-1.0))
            parts.append(jnp.max(part, axis=0, keepdims=True))
        window = slice(start, start + chunk)
        best[:, window] = jnp.maximum(best[:, window], jnp.concatenate(parts, axis=1))


def gather_group(blocks, cluster, out, me):
    per = blocks[0].shape[0] // CLUS_DEV
    for step, block in enumerate(blocks):
        place = (me & (len(blocks) - 1)) ^ step
        rows = pl.ds(pl.multiple_of(place * per, per), per)
        out[rows, :] = block[cluster * per : (cluster + 1) * per, :]


def score_pairs(bests, groups, new, old, bit, me):
    later = (me & bit) == 0

    @pl.when(later)
    def _():
        for best, group in zip(bests, groups):
            raise_best(best[new], group[old], group[new])

    @pl.when(jnp.logical_not(later))
    def _():
        for best, group in zip(bests, groups):
            raise_best(best[old], group[new], group[old])


def fresh_best(rows):
    ones = jnp.ones((8, LANES), BF)
    heads = matmul(ones, rows[:, :LANES], ((1,), (1,)))[:1]
    return jnp.where(heads < 100.0, F32(-1.0), F32(UNFILLED))


def own_early(cuts, bits, *refs):
    blocks, (send, best) = list(reversed(refs[:-2])), refs[-2:]
    per = blocks[0].shape[0] // CLUS_DEV
    me = lax.axis_index("clus")
    spans = list(zip(cuts, cuts[1:]))
    bests = [[best.at[c : c + 1, a:b] for a, b in spans] for c in range(CLUS_DEV)]
    groups = [[send.at[1, c, a:b] for a, b in spans] for c in range(CLUS_DEV)]
    for c in range(CLUS_DEV):
        for i, (a, b) in enumerate(spans):
            gather_group(blocks[a // per : b // per], c, groups[c][i], me)
            bests[c][i][...] = fresh_best(groups[c][i])
            raise_best(bests[c][i], groups[c][i], groups[c][i], True)
        send[0, c] = send[1, c]
    score_pairs(bests, groups, 1, 0, bits[0], me)


def cross_early(received, before, best):
    best[...] = before[...]

    @pl.when(lax.axis_index("blk") == 1)
    def _():
        for c in range(CLUS_DEV):
            raise_best(best.at[c : c + 1, : received.shape[2]], received.at[0, c], received.at[1, c])


def gather_late(*refs):
    blocks, out = refs[:-1], refs[-1]
    for c in range(CLUS_DEV):
        gather_group(blocks, c, out.at[c], lax.axis_index("clus"))


def own_late(cuts, bits, received, cat, before, best):
    me = lax.axis_index("clus")
    core = lax.axis_index("blk")
    spans = list(zip(cuts, cuts[1:]))
    last = len(spans) - 1
    start = spans[last][0]
    best[:, :start] = before[:, :start]
    bests = [[best.at[c : c + 1, a:b] for a, b in spans] for c in range(CLUS_DEV)]
    groups = [
        [received.at[core, c, a:b] for a, b in spans[:-1]] + [cat.at[c]] for c in range(CLUS_DEV)
    ]
    for c in range(CLUS_DEV):
        bests[c][last][...] = fresh_best(cat.at[c])
        raise_best(bests[c][last], cat.at[c], cat.at[c], True)
    for i in range(last):
        score_pairs(bests, groups, last, i, bits[i], me)

    @pl.when(core == 1)
    def _():
        for c in range(CLUS_DEV):
            raise_best(bests[c][last], received.at[0, c], cat.at[c])


def cross_late(cuts, per, received, cat, before, other, out, best):
    me = lax.axis_index("clus")
    core = lax.axis_index("blk")
    spans = list(zip(cuts, cuts[1:]))
    best[...] = before[...]

    @pl.when(core == 1)
    def _():
        start = spans[-1][0]
        for c in range(CLUS_DEV):
            fresh = best.at[c : c + 1, start:]
            raise_best(best.at[c : c + 1, :start], other.at[c], received.at[1, c])
            raise_best(fresh, other.at[c], cat.at[c])

    for a, b in spans:
        place = (me ^ (a // per)) & ~((b - a) // per - 1)
        value = best[:, a:b]
        at = pl.ds(pl.multiple_of(place * per, LANES), b - a)
        out[:, at] = jnp.where(value > 0.5 * UNFILLED, F32(0.0), value)


def local(embeddings, cluster_ids):
    owners = lax.axis_size("clus")
    clusters = CLUS_DEV * owners
    rows, width = embeddings.shape
    per = 2 * rows // clusters
    bits = [owners // 2, owners // 4]
    bounds = [0, owners // 2, owners // 2 + owners // 4, owners]
    cuts = [x * per for x in bounds]
    near, far, late = [list(range(a, b)) for a, b in zip(bounds, bounds[1:])]
    best_shape = jax.ShapeDtypeStruct((CLUS_DEV, rows), F32)

    def to_owner(block, step):
        return lax.ppermute(block, "clus", [(i, i ^ step) for i in range(owners)])

    def stage_shape(sources):
        return jax.ShapeDtypeStruct((2, CLUS_DEV, sources * per, width), BF)

    def to_both(send):
        return lax.all_to_all(send, "blk", split_axis=0, concat_axis=0, tiled=True)

    arrived = {}
    lead = far[:1]
    unit, tgt, *packed = call_pack_first(embeddings, cluster_ids, lead, clusters, per)
    for steps in (near[1:] + far[1:] + [0], []):
        for step, block in zip(lead, packed):
            arrived[step] = to_owner(block, step) if step else block
        lead, packed = steps, call_pack_rest(unit, tgt, steps, per) if steps else []
    packed = call_pack_rest(unit, tgt, late, per)
    *held, arrived[far[0]] = lax.optimization_barrier((*packed, arrived[far[0]]))
    for step, block in zip(late, held):
        arrived[step] = to_owner(block, step)

    early = near + far
    send, best = kernel_call(
        functools.partial(own_early, cuts[:3], bits),
        [stage_shape(len(early)), best_shape],
        [arrived[s] for s in reversed(early)],
        "own_early",
    )
    received = to_both(send)
    (best,) = kernel_call(cross_early, [best_shape], [received, best], "cross_early")
    *new, best = lax.optimization_barrier((*[arrived[s] for s in late], best))
    cat_shape = jax.ShapeDtypeStruct((CLUS_DEV, len(late) * per, width), BF)
    (cat,) = kernel_call(gather_late, [cat_shape], new, "gather_late")
    other = lax.ppermute(cat, "blk", [(0, 1)])
    (best,) = kernel_call(
        functools.partial(own_late, cuts, bits), [best_shape], [received, cat, best], "own_late"
    )
    (out,) = kernel_call(
        functools.partial(cross_late, cuts, per),
        [best_shape],
        [received, cat, best, other],
        "cross_late",
        [pltpu.VMEM((CLUS_DEV, rows), F32)],
    )
    return out


def solution(mesh):
    placed = (P(("groups", "clus", "blk"), None), P(("groups", "clus", "blk"), None))
    return jax.shard_map(
        local, mesh=mesh, in_specs=placed, out_specs=P(("groups", "clus"), "blk"), check_vma=False
    )
```

```python
import functools

import jax
import jax.numpy as jnp
from jax import lax
from jax.experimental import pallas as pl
from jax.experimental.pallas import tpu as pltpu
from jax.sharding import PartitionSpec as P

CLUS_DEV = 2
LANES = 128
MARK = 2.0
UNFILLED = 8.0
BF = jnp.bfloat16
F32 = jnp.float32


def iota(shape, dim):
    return lax.broadcasted_iota(jnp.int32, shape, dim)


def matmul(a, b, contract):
    return lax.dot_general(a, b, (contract, ((), ())), preferred_element_type=F32)


def targets(ids, clusters, per_source):
    groups = ids.shape[1] // LANES
    parts = [ids[:, g * LANES : (g + 1) * LANES] for g in range(groups)]
    hot = jnp.concatenate(
        [(iota((clusters, LANES), 0) == part).astype(F32) for part in parts], axis=0
    )
    stacked = groups * clusters
    earlier = (iota((LANES, LANES), 0) < iota((LANES, LANES), 1)).astype(F32).astype(BF)
    within = matmul(hot.astype(BF), earlier, ((1,), (0,)))
    totals = jnp.broadcast_to(jnp.sum(hot, axis=1, keepdims=True), (stacked, LANES))
    a, b = iota((stacked, stacked), 0), iota((stacked, stacked), 1)
    chunks_before = ((a % clusters == b % clusters) & (b < a)).astype(F32).astype(BF)
    before = within + matmul(chunks_before, totals.astype(BF), ((1,), (0,)))
    picked = hot * before
    out = [
        jnp.sum(picked[g * clusters : (g + 1) * clusters], axis=0, keepdims=True).astype(jnp.int32)
        + parts[g] * per_source
        for g in range(groups)
    ]
    return jnp.concatenate(out, axis=1)


def pack_block(unit, tgt, dest, width):
    hit = (tgt - dest * width) == iota((width, tgt.shape[1]), 0)
    hot = hit.astype(F32)
    rows = matmul(hot.astype(BF), unit, ((1,), (0,)))
    empty = jnp.max(hot, axis=1, keepdims=True) < 0.5
    head = jnp.where(empty, F32(MARK), rows[:, :LANES])
    return head.astype(BF), rows[:, LANES:].astype(BF)


def store_blocks(unit, tgt, steps, width, outs):
    me = lax.axis_index("clus")
    for step, out in zip(steps, outs):
        head, tail = pack_block(unit, tgt, me ^ step, width)
        out[:, :LANES] = head
        out[:, LANES:] = tail


PIECES = 4


def pack_first(steps, clusters, per_source, emb, ids, tgt, *refs):
    outs, (unit, raw, raw_ids, sems, ids_sem) = refs[:-5], refs[-5:]
    size = emb.shape[0] // PIECES
    ids_copy = pltpu.make_async_copy(ids, raw_ids, ids_sem)
    ids_copy.start()
    windows = [pl.ds(piece * size, size) for piece in range(PIECES)]
    copies = [
        pltpu.make_async_copy(emb.at[window], raw.at[window], sems.at[piece])
        for piece, window in enumerate(windows)
    ]
    for copy in copies:
        copy.start()
    ids_copy.wait()
    tgt[...] = targets(raw_ids[...], clusters, per_source)
    for copy, window in zip(copies, windows):
        copy.wait()
        values = raw[window, :].astype(F32)
        scale = lax.rsqrt(jnp.sum(values * values, axis=1, keepdims=True) + 1e-6)
        unit[window, :] = (values * scale).astype(BF)
    store_blocks(unit[...], tgt[...], steps, CLUS_DEV * per_source, outs)


def pack_second(steps, per_source, emb, tgt, unit, *outs):
    values = emb[...].astype(F32)
    scale = lax.rsqrt(jnp.sum(values * values, axis=1, keepdims=True) + 1e-6)
    unit[...] = (values * scale).astype(BF)
    store_blocks(unit[...], tgt[...], steps, CLUS_DEV * per_source, outs)


def pack_rest(steps, per_source, unit, tgt, *outs):
    store_blocks(unit[...], tgt[...], steps, CLUS_DEV * per_source, outs)


VMEM = pl.BlockSpec(memory_space=pltpu.VMEM)


def kernel_call(kernel, shapes, inputs, name, scratch=(), place=VMEM, grant=20 * 2**20):
    return pl.pallas_call(
        kernel,
        out_shape=shapes,
        in_specs=[place] * len(inputs),
        out_specs=[VMEM] * len(shapes),
        scratch_shapes=scratch,
        compiler_params=pltpu.CompilerParams(vmem_limit_bytes=grant),
        cost_estimate=pl.CostEstimate(flops=1000, bytes_accessed=1000, transcendentals=0),
        name=name,
    )(*inputs)


def call_pack_first(emb, ids, steps, clusters, per_source):
    block = jax.ShapeDtypeStruct((CLUS_DEV * per_source, emb.shape[1]), BF)
    shapes = [jax.ShapeDtypeStruct(ids.shape, jnp.int32)]
    return kernel_call(
        functools.partial(pack_first, steps, clusters, per_source),
        shapes + [block] * len(steps),
        [emb, ids],
        place=pl.BlockSpec(memory_space=pl.ANY),
        grant=54 * 2**20,
        name="pack_first",
        scratch=[
            pltpu.VMEM(emb.shape, BF),
            pltpu.VMEM(emb.shape, BF),
            pltpu.VMEM(ids.shape, jnp.int32),
            pltpu.SemaphoreType.DMA((PIECES,)),
            pltpu.SemaphoreType.DMA,
        ],
    )


def call_pack_rest(unit, tgt, steps, per_source):
    block = jax.ShapeDtypeStruct((CLUS_DEV * per_source, unit.shape[1]), BF)
    return kernel_call(
        functools.partial(pack_rest, steps, per_source),
        [block] * len(steps),
        [unit, tgt],
        "pack_rest",
    )


CHUNK = 256


def raise_best(best, keys, queries, triangular=False):
    rows = queries.shape[0]
    chunk = min(CHUNK, rows) if triangular else rows
    for start in range(0, rows, chunk):
        count = start + chunk if triangular else keys.shape[0]
        sims = matmul(keys[:count, :], queries[start : start + chunk, :], ((1,), (1,)))
        filled = keys[:count, :LANES].astype(F32) < 1.5
        parts = []
        for first in range(0, chunk, LANES):
            allowed = filled
            if triangular:
                allowed = filled & (
                    iota((count, LANES), 0) < iota((count, LANES), 1) + (start + first)
                )
            part = jnp.where(allowed, sims[:, first : first + LANES], F32(-1.0))
            parts.append(jnp.max(part, axis=0, keepdims=True))
        window = slice(start, start + chunk)
        best[:, window] = jnp.maximum(best[:, window], jnp.concatenate(parts, axis=1))


def gather_group(blocks, cluster, out, me):
    per = blocks[0].shape[0] // CLUS_DEV
    for step, block in enumerate(blocks):
        place = (me & (len(blocks) - 1)) ^ step
        rows = pl.ds(pl.multiple_of(place * per, per), per)
        out[rows, :] = block[cluster * per : (cluster + 1) * per, :]


def score_pairs(bests, groups, new, old, bit, me):
    later = (me & bit) == 0

    @pl.when(later)
    def _():
        for best, group in zip(bests, groups):
            raise_best(best[new], group[old], group[new])

    @pl.when(jnp.logical_not(later))
    def _():
        for best, group in zip(bests, groups):
            raise_best(best[old], group[new], group[old])


def fresh_best(rows):
    ones = jnp.ones((8, LANES), BF)
    heads = matmul(ones, rows[:, :LANES], ((1,), (1,)))[:1]
    return jnp.where(heads < 100.0, F32(-1.0), F32(UNFILLED))


def own_early(cuts, bits, *refs):
    blocks, (send, best) = list(reversed(refs[:-2])), refs[-2:]
    per = blocks[0].shape[0] // CLUS_DEV
    me = lax.axis_index("clus")
    spans = list(zip(cuts, cuts[1:]))
    bests = [[best.at[c : c + 1, a:b] for a, b in spans] for c in range(CLUS_DEV)]
    groups = [[send.at[1, c, a:b] for a, b in spans] for c in range(CLUS_DEV)]
    for c in range(CLUS_DEV):
        for i, (a, b) in enumerate(spans):
            gather_group(blocks[a // per : b // per], c, groups[c][i], me)
            bests[c][i][...] = fresh_best(groups[c][i])
            raise_best(bests[c][i], groups[c][i], groups[c][i], True)
        send[0, c] = send[1, c]
    score_pairs(bests, groups, 1, 0, bits[0], me)


def cross_early(received, before, best):
    best[...] = before[...]

    @pl.when(lax.axis_index("blk") == 1)
    def _():
        for c in range(CLUS_DEV):
            raise_best(best.at[c : c + 1, : received.shape[2]], received.at[0, c], received.at[1, c])


def gather_late(*refs):
    blocks, out = refs[:-1], refs[-1]
    for c in range(CLUS_DEV):
        gather_group(blocks, c, out.at[c], lax.axis_index("clus"))


def own_late(cuts, bits, received, *refs):
    cats, (before, best) = refs[:-2], refs[-2:]
    me = lax.axis_index("clus")
    core = lax.axis_index("blk")
    spans = list(zip(cuts, cuts[1:]))
    last = len(spans) - 1
    early = last - len(cats) + 1
    start = spans[last][0]
    best[:, :start] = before[:, :start]
    bests = [[best.at[c : c + 1, a:b] for a, b in spans] for c in range(CLUS_DEV)]
    groups = [
        [received.at[core, c, a:b] for a, b in spans[:early]]
        + [cat.at[c, : b - a] for cat, (a, b) in zip(cats, spans[early:])]
        for c in range(CLUS_DEV)
    ]
    for c in range(CLUS_DEV):
        bests[c][last][...] = fresh_best(groups[c][last])
        raise_best(bests[c][last], groups[c][last], groups[c][last], True)
    for i in range(last):
        score_pairs(bests, groups, last, i, bits[i], me)

    @pl.when(core == 1)
    def _():
        for c in range(CLUS_DEV):
            raise_best(bests[c][last], received.at[0, c], groups[c][last])


def cross_late(cuts, per, count, received, *refs):
    cats, (before, *others, out, best, keys, queries) = refs[:count], refs[count:]
    me = lax.axis_index("clus")
    spans = list(zip(cuts, cuts[1:]))
    start = received.shape[2]
    best[...] = before[...]

    @pl.when(lax.axis_index("blk") == 1)
    def _():
        for c in range(CLUS_DEV):
            for cat, other, (a, b) in zip(cats, others, spans[-count:]):
                keys[c, a - start : b - start, :] = other[c, : b - a, :]
                queries[c, a - start : b - start, :] = cat[c, : b - a, :]
            raise_best(best.at[c : c + 1, :start], keys.at[c], received.at[1, c])
            raise_best(best.at[c : c + 1, start:], keys.at[c], queries.at[c])

    for a, b in spans:
        place = (me ^ (a // per)) & ~((b - a) // per - 1)
        value = best[:, a:b]
        at = pl.ds(pl.multiple_of(place * per, LANES), b - a)
        out[:, at] = jnp.where(value > 0.5 * UNFILLED, F32(0.0), value)


def local(embeddings, cluster_ids):
    owners = lax.axis_size("clus")
    clusters = CLUS_DEV * owners
    rows, width = embeddings.shape
    per = 2 * rows // clusters
    bits = [owners // 2, owners // 4, owners // 8]
    bounds = [0, owners // 2, owners // 2 + owners // 4, owners - owners // 8, owners]
    cuts = [x * per for x in bounds]
    near, far, *lates = [list(range(a, b)) for a, b in zip(bounds, bounds[1:])]
    best_shape = jax.ShapeDtypeStruct((CLUS_DEV, rows), F32)

    def to_owner(block, step):
        return lax.ppermute(block, "clus", [(i, i ^ step) for i in range(owners)])

    def stage_shape(sources):
        return jax.ShapeDtypeStruct((2, CLUS_DEV, sources * per, width), BF)

    def to_both(send):
        return lax.all_to_all(send, "blk", split_axis=0, concat_axis=0, tiled=True)

    arrived = {}
    tgt, *packed = call_pack_first(embeddings, cluster_ids, far[:1], clusters, per)
    arrived[far[0]] = to_owner(packed[0], far[0])
    steps = near[1:] + far[1:] + [0]
    block = jax.ShapeDtypeStruct((CLUS_DEV * per, width), BF)
    unit, *packed = kernel_call(
        functools.partial(pack_second, steps, per),
        [jax.ShapeDtypeStruct(embeddings.shape, BF)] + [block] * len(steps),
        [embeddings, tgt],
        "pack_second",
    )
    for step, packed_block in zip(steps, packed):
        arrived[step] = to_owner(packed_block, step) if step else packed_block
    late = lates[0] + lates[1]
    packed = call_pack_rest(unit, tgt, late, per)
    *held, arrived[far[0]] = lax.optimization_barrier((*packed, arrived[far[0]]))
    for step, block in zip(late, held):
        arrived[step] = to_owner(block, step)

    early = near + far
    send, best = kernel_call(
        functools.partial(own_early, cuts[:3], bits),
        [stage_shape(len(early)), best_shape],
        [arrived[s] for s in reversed(early)],
        "own_early",
    )
    received = to_both(send)
    (best,) = kernel_call(cross_early, [best_shape], [received, best], "cross_early")
    cats, others = [], []
    for steps, spare in zip(lates, (1, 0)):
        *new, best = lax.optimization_barrier((*[arrived[s] for s in steps], best))
        count = len(steps) * per
        cat_shape = jax.ShapeDtypeStruct((CLUS_DEV, count + spare * count // 2, width), BF)
        cats += kernel_call(gather_late, [cat_shape], new, "gather_late")
        others.append(lax.ppermute(cats[-1], "blk", [(0, 1)]))
        (best,) = kernel_call(
            functools.partial(own_late, cuts[: 3 + len(cats)], bits),
            [best_shape],
            [received] + cats + [best],
            "own_late",
        )
    late_rows = (CLUS_DEV, len(late) * per, width)
    (out,) = kernel_call(
        functools.partial(cross_late, cuts, per, len(cats)),
        [best_shape],
        [received] + cats + [best] + others,
        "cross_late",
        [pltpu.VMEM((CLUS_DEV, rows), F32)] + [pltpu.VMEM(late_rows, BF)] * 2,
    )
    return out


def solution(mesh):
    placed = (P(("groups", "clus", "blk"), None), P(("groups", "clus", "blk"), None))
    return jax.shard_map(
        local, mesh=mesh, in_specs=placed, out_specs=P(("groups", "clus"), "blk"), check_vma=False
    )
```

```python
import functools

import jax
import jax.numpy as jnp
from jax import lax
from jax.experimental import pallas as pl
from jax.experimental.pallas import tpu as pltpu
from jax.sharding import PartitionSpec as P

CLUS_DEV = 2
LANES = 128
MARK = 2.0
UNFILLED = 8.0
BF = jnp.bfloat16
F32 = jnp.float32


def iota(shape, dim):
    return lax.broadcasted_iota(jnp.int32, shape, dim)


def matmul(a, b, contract):
    return lax.dot_general(a, b, (contract, ((), ())), preferred_element_type=F32)


def targets(ids, clusters, per_source):
    groups = ids.shape[1] // LANES
    parts = [ids[:, g * LANES : (g + 1) * LANES] for g in range(groups)]
    hot = jnp.concatenate(
        [(iota((clusters, LANES), 0) == part).astype(F32) for part in parts], axis=0
    )
    stacked = groups * clusters
    earlier = (iota((LANES, LANES), 0) < iota((LANES, LANES), 1)).astype(F32).astype(BF)
    within = matmul(hot.astype(BF), earlier, ((1,), (0,)))
    totals = jnp.broadcast_to(jnp.sum(hot, axis=1, keepdims=True), (stacked, LANES))
    a, b = iota((stacked, stacked), 0), iota((stacked, stacked), 1)
    chunks_before = ((a % clusters == b % clusters) & (b < a)).astype(F32).astype(BF)
    before = within + matmul(chunks_before, totals.astype(BF), ((1,), (0,)))
    picked = hot * before
    out = [
        jnp.sum(picked[g * clusters : (g + 1) * clusters], axis=0, keepdims=True).astype(jnp.int32)
        + parts[g] * per_source
        for g in range(groups)
    ]
    return jnp.concatenate(out, axis=1)


def pack_block(unit, tgt, dest, width):
    hit = (tgt - dest * width) == iota((width, tgt.shape[1]), 0)
    hot = hit.astype(F32)
    rows = matmul(hot.astype(BF), unit, ((1,), (0,)))
    empty = jnp.max(hot, axis=1, keepdims=True) < 0.5
    head = jnp.where(empty, F32(MARK), rows[:, :LANES])
    return head.astype(BF), rows[:, LANES:].astype(BF)


def store_blocks(unit, tgt, steps, width, outs):
    me = lax.axis_index("clus")
    for step, out in zip(steps, outs):
        head, tail = pack_block(unit, tgt, me ^ step, width)
        out[:, :LANES] = head
        out[:, LANES:] = tail


PIECES = 4


def pack_first(steps, clusters, per_source, emb, ids, unit, tgt, *refs):
    outs, (raw, sems) = refs[:-2], refs[-2:]
    size = emb.shape[0] // PIECES
    windows = [pl.ds(piece * size, size) for piece in range(PIECES)]
    copies = [
        pltpu.make_async_copy(emb.at[window], raw.at[window], sems.at[piece])
        for piece, window in enumerate(windows)
    ]
    for copy in copies:
        copy.start()
    tgt[...] = targets(ids[...], clusters, per_source)
    for copy, window in zip(copies, windows):
        copy.wait()
        values = raw[window, :].astype(F32)
        scale = lax.rsqrt(jnp.sum(values * values, axis=1, keepdims=True) + 1e-6)
        unit[window, :] = (values * scale).astype(BF)
    store_blocks(unit[...], tgt[...], steps, CLUS_DEV * per_source, outs)


def pack_rest(steps, per_source, unit, tgt, *outs):
    store_blocks(unit[...], tgt[...], steps, CLUS_DEV * per_source, outs)


VMEM = pl.BlockSpec(memory_space=pltpu.VMEM)


def kernel_call(kernel, shapes, inputs, name, scratch=(), places=None, grant=20 * 2**20):
    return pl.pallas_call(
        kernel,
        out_shape=shapes,
        in_specs=places or [VMEM] * len(inputs),
        out_specs=[VMEM] * len(shapes),
        scratch_shapes=scratch,
        compiler_params=pltpu.CompilerParams(vmem_limit_bytes=grant),
        cost_estimate=pl.CostEstimate(flops=1000, bytes_accessed=1000, transcendentals=0),
        name=name,
    )(*inputs)


def call_pack_first(emb, ids, steps, clusters, per_source):
    block = jax.ShapeDtypeStruct((CLUS_DEV * per_source, emb.shape[1]), BF)
    shapes = [jax.ShapeDtypeStruct(emb.shape, BF), jax.ShapeDtypeStruct(ids.shape, jnp.int32)]
    return kernel_call(
        functools.partial(pack_first, steps, clusters, per_source),
        shapes + [block] * len(steps),
        [emb, ids],
        places=[pl.BlockSpec(memory_space=pl.ANY), VMEM],
        grant=50 * 2**20,
        name="pack_first",
        scratch=[
            pltpu.VMEM(emb.shape, BF),
            pltpu.SemaphoreType.DMA((PIECES,)),
        ],
    )


def call_pack_rest(unit, tgt, steps, per_source):
    block = jax.ShapeDtypeStruct((CLUS_DEV * per_source, unit.shape[1]), BF)
    return kernel_call(
        functools.partial(pack_rest, steps, per_source),
        [block] * len(steps),
        [unit, tgt],
        "pack_rest",
    )


CHUNK = 256


def raise_best(best, keys, queries, triangular=False):
    rows = queries.shape[0]
    chunk = min(CHUNK, rows) if triangular else rows
    for start in range(0, rows, chunk):
        count = start + chunk if triangular else keys.shape[0]
        sims = matmul(keys[:count, :], queries[start : start + chunk, :], ((1,), (1,)))
        filled = keys[:count, :LANES].astype(F32) < 1.5
        parts = []
        for first in range(0, chunk, LANES):
            allowed = filled
            if triangular:
                allowed = filled & (
                    iota((count, LANES), 0) < iota((count, LANES), 1) + (start + first)
                )
            part = jnp.where(allowed, sims[:, first : first + LANES], F32(-1.0))
            parts.append(jnp.max(part, axis=0, keepdims=True))
        window = slice(start, start + chunk)
        best[:, window] = jnp.maximum(best[:, window], jnp.concatenate(parts, axis=1))


def gather_group(blocks, cluster, out, me):
    per = blocks[0].shape[0] // CLUS_DEV
    for step, block in enumerate(blocks):
        place = (me & (len(blocks) - 1)) ^ step
        rows = pl.ds(pl.multiple_of(place * per, per), per)
        out[rows, :] = block[cluster * per : (cluster + 1) * per, :]


def score_pairs(bests, groups, new, old, bit, me):
    later = (me & bit) == 0

    @pl.when(later)
    def _():
        for best, group in zip(bests, groups):
            raise_best(best[new], group[old], group[new])

    @pl.when(jnp.logical_not(later))
    def _():
        for best, group in zip(bests, groups):
            raise_best(best[old], group[new], group[old])


def fresh_best(rows):
    ones = jnp.ones((8, LANES), BF)
    heads = matmul(ones, rows[:, :LANES], ((1,), (1,)))[:1]
    return jnp.where(heads < 100.0, F32(-1.0), F32(UNFILLED))


def own_early(cuts, bits, *refs):
    blocks, (send, best) = list(reversed(refs[:-2])), refs[-2:]
    per = blocks[0].shape[0] // CLUS_DEV
    me = lax.axis_index("clus")
    spans = list(zip(cuts, cuts[1:]))
    bests = [[best.at[c : c + 1, a:b] for a, b in spans] for c in range(CLUS_DEV)]
    groups = [[send.at[1, c, a:b] for a, b in spans] for c in range(CLUS_DEV)]
    for c in range(CLUS_DEV):
        for i, (a, b) in enumerate(spans):
            gather_group(blocks[a // per : b // per], c, groups[c][i], me)
            bests[c][i][...] = fresh_best(groups[c][i])
            raise_best(bests[c][i], groups[c][i], groups[c][i], True)
        send[0, c] = send[1, c]
    score_pairs(bests, groups, 1, 0, bits[0], me)


def cross_early(received, before, best):
    best[...] = before[...]

    @pl.when(lax.axis_index("blk") == 1)
    def _():
        for c in range(CLUS_DEV):
            raise_best(best.at[c : c + 1, : received.shape[2]], received.at[0, c], received.at[1, c])


def gather_late(*refs):
    blocks, out = refs[:-1], refs[-1]
    for c in range(CLUS_DEV):
        gather_group(blocks, c, out.at[c], lax.axis_index("clus"))


def own_late(cuts, bits, received, cat, before, best):
    me = lax.axis_index("clus")
    core = lax.axis_index("blk")
    spans = list(zip(cuts, cuts[1:]))
    last = len(spans) - 1
    start = spans[last][0]
    best[:, :start] = before[:, :start]
    bests = [[best.at[c : c + 1, a:b] for a, b in spans] for c in range(CLUS_DEV)]
    groups = [
        [received.at[core, c, a:b] for a, b in spans[:-1]] + [cat.at[c]] for c in range(CLUS_DEV)
    ]
    for c in range(CLUS_DEV):
        bests[c][last][...] = fresh_best(cat.at[c])
        raise_best(bests[c][last], cat.at[c], cat.at[c], True)
    score_pairs(bests, groups, last, 0, bits[0], me)
    score_pairs(bests, groups, 1, last, bits[1], me)

    @pl.when(core == 1)
    def _():
        for c in range(CLUS_DEV):
            raise_best(bests[c][last], received.at[0, c], cat.at[c])


def cross_late(cuts, starts, per, received, cat, before, other, out, best):
    me = lax.axis_index("clus")
    core = lax.axis_index("blk")
    spans = list(zip(cuts, cuts[1:]))
    best[...] = before[...]

    @pl.when(core == 1)
    def _():
        start = spans[-1][0]
        for c in range(CLUS_DEV):
            fresh = best.at[c : c + 1, start:]
            raise_best(best.at[c : c + 1, :start], other.at[c], received.at[1, c])
            raise_best(fresh, other.at[c], cat.at[c])

    for (a, b), first in zip(spans, starts):
        place = (me ^ first) & ~((b - a) // per - 1)
        value = best[:, a:b]
        at = pl.ds(pl.multiple_of(place * per, LANES), b - a)
        out[:, at] = jnp.where(value > 0.5 * UNFILLED, F32(0.0), value)


def local(embeddings, cluster_ids):
    owners = lax.axis_size("clus")
    clusters = CLUS_DEV * owners
    rows, width = embeddings.shape
    per = 2 * rows // clusters
    bits = [owners // 2, owners // 4]
    half, rest = owners // 2, owners - owners // 4
    near, far, late = [list(range(*x)) for x in ((0, half), (rest, owners), (half, rest))]
    starts = [near[0], far[0], late[0]]
    cuts = [0, half * per, rest * per, rows]
    best_shape = jax.ShapeDtypeStruct((CLUS_DEV, rows), F32)

    def to_owner(block, step):
        return lax.ppermute(block, "clus", [(i, i ^ step) for i in range(owners)])

    def stage_shape(sources):
        return jax.ShapeDtypeStruct((2, CLUS_DEV, sources * per, width), BF)

    def to_both(send):
        return lax.all_to_all(send, "blk", split_axis=0, concat_axis=0, tiled=True)

    arrived = {}
    lead = far[:1]
    unit, tgt, *packed = call_pack_first(embeddings, cluster_ids, lead, clusters, per)
    for steps in (near[1:] + far[1:] + [0], []):
        for step, block in zip(lead, packed):
            arrived[step] = to_owner(block, step) if step else block
        lead, packed = steps, call_pack_rest(unit, tgt, steps, per) if steps else []
    packed = call_pack_rest(unit, tgt, late, per)
    *held, arrived[far[0]] = lax.optimization_barrier((*packed, arrived[far[0]]))
    for step, block in zip(late, held):
        arrived[step] = to_owner(block, step)

    early = near + far
    send, best = kernel_call(
        functools.partial(own_early, cuts[:3], bits),
        [stage_shape(len(early)), best_shape],
        [arrived[s] for s in reversed(early)],
        "own_early",
    )
    received = to_both(send)
    (best,) = kernel_call(cross_early, [best_shape], [received, best], "cross_early")
    *new, best = lax.optimization_barrier((*[arrived[s] for s in late], best))
    cat_shape = jax.ShapeDtypeStruct((CLUS_DEV, len(late) * per, width), BF)
    (cat,) = kernel_call(gather_late, [cat_shape], new, "gather_late")
    other = lax.ppermute(cat, "blk", [(0, 1)])
    (best,) = kernel_call(
        functools.partial(own_late, cuts, bits), [best_shape], [received, cat, best], "own_late"
    )
    (out,) = kernel_call(
        functools.partial(cross_late, cuts, starts, per),
        [best_shape],
        [received, cat, best, other],
        "cross_late",
        [pltpu.VMEM((CLUS_DEV, rows), F32)],
    )
    return out


def solution(mesh):
    placed = (P(("groups", "clus", "blk"), None), P(("groups", "clus", "blk"), None))
    return jax.shard_map(
        local, mesh=mesh, in_specs=placed, out_specs=P(("groups", "clus"), "blk"), check_vma=False
    )
```

```python
import functools

import jax
import jax.numpy as jnp
from jax import lax
from jax.experimental import pallas as pl
from jax.experimental.pallas import tpu as pltpu
from jax.sharding import PartitionSpec as P

CLUS_DEV = 2
LANES = 128
MARK = 2.0
UNFILLED = 8.0
BF = jnp.bfloat16
F32 = jnp.float32


def iota(shape, dim):
    return lax.broadcasted_iota(jnp.int32, shape, dim)


def matmul(a, b, contract):
    return lax.dot_general(a, b, (contract, ((), ())), preferred_element_type=F32)


def targets(ids, clusters, per_source):
    groups = ids.shape[1] // LANES
    parts = [ids[:, g * LANES : (g + 1) * LANES] for g in range(groups)]
    hot = jnp.concatenate(
        [(iota((clusters, LANES), 0) == part).astype(F32) for part in parts], axis=0
    )
    stacked = groups * clusters
    earlier = (iota((LANES, LANES), 0) < iota((LANES, LANES), 1)).astype(F32).astype(BF)
    within = matmul(hot.astype(BF), earlier, ((1,), (0,)))
    totals = jnp.broadcast_to(jnp.sum(hot, axis=1, keepdims=True), (stacked, LANES))
    a, b = iota((stacked, stacked), 0), iota((stacked, stacked), 1)
    chunks_before = ((a % clusters == b % clusters) & (b < a)).astype(F32).astype(BF)
    before = within + matmul(chunks_before, totals.astype(BF), ((1,), (0,)))
    picked = hot * before
    out = [
        jnp.sum(picked[g * clusters : (g + 1) * clusters], axis=0, keepdims=True).astype(jnp.int32)
        + parts[g] * per_source
        for g in range(groups)
    ]
    return jnp.concatenate(out, axis=1)


def pack_block(unit, tgt, dest, width):
    hit = (tgt - dest * width) == iota((width, tgt.shape[1]), 0)
    hot = hit.astype(F32)
    rows = matmul(hot.astype(BF), unit, ((1,), (0,)))
    empty = jnp.max(hot, axis=1, keepdims=True) < 0.5
    head = jnp.where(empty, F32(MARK), rows[:, :LANES])
    return head.astype(BF), rows[:, LANES:].astype(BF)


def store_blocks(unit, tgt, steps, width, outs):
    me = lax.axis_index("clus")
    for step, out in zip(steps, outs):
        head, tail = pack_block(unit, tgt, me ^ step, width)
        out[:, :LANES] = head
        out[:, LANES:] = tail


PIECES = 4


def pack_first(steps, clusters, per_source, emb, ids, unit, tgt, *refs):
    outs, (raw, sems) = refs[:-2], refs[-2:]
    size = emb.shape[0] // PIECES
    windows = [pl.ds(piece * size, size) for piece in range(PIECES)]
    copies = [
        pltpu.make_async_copy(emb.at[window], raw.at[window], sems.at[piece])
        for piece, window in enumerate(windows)
    ]
    for copy in copies:
        copy.start()
    tgt[...] = targets(ids[...], clusters, per_source)
    for copy, window in zip(copies, windows):
        copy.wait()
        values = raw[window, :].astype(F32)
        scale = lax.rsqrt(jnp.sum(values * values, axis=1, keepdims=True) + 1e-6)
        unit[window, :] = (values * scale).astype(BF)
    store_blocks(unit[...], tgt[...], steps, CLUS_DEV * per_source, outs)


def pack_rest(steps, per_source, unit, tgt, *outs):
    store_blocks(unit[...], tgt[...], steps, CLUS_DEV * per_source, outs)


VMEM = pl.BlockSpec(memory_space=pltpu.VMEM)


def kernel_call(kernel, shapes, inputs, name, scratch=(), places=None, grant=20 * 2**20):
    return pl.pallas_call(
        kernel,
        out_shape=shapes,
        in_specs=places or [VMEM] * len(inputs),
        out_specs=[VMEM] * len(shapes),
        scratch_shapes=scratch,
        compiler_params=pltpu.CompilerParams(vmem_limit_bytes=grant),
        cost_estimate=pl.CostEstimate(flops=1000, bytes_accessed=1000, transcendentals=0),
        name=name,
    )(*inputs)


def call_pack_first(emb, ids, steps, clusters, per_source):
    block = jax.ShapeDtypeStruct((CLUS_DEV * per_source, emb.shape[1]), BF)
    shapes = [jax.ShapeDtypeStruct(emb.shape, BF), jax.ShapeDtypeStruct(ids.shape, jnp.int32)]
    return kernel_call(
        functools.partial(pack_first, steps, clusters, per_source),
        shapes + [block] * len(steps),
        [emb, ids],
        places=[pl.BlockSpec(memory_space=pl.ANY), VMEM],
        grant=50 * 2**20,
        name="pack_first",
        scratch=[
            pltpu.VMEM(emb.shape, BF),
            pltpu.SemaphoreType.DMA((PIECES,)),
        ],
    )


def call_pack_rest(unit, tgt, steps, per_source):
    block = jax.ShapeDtypeStruct((CLUS_DEV * per_source, unit.shape[1]), BF)
    return kernel_call(
        functools.partial(pack_rest, steps, per_source),
        [block] * len(steps),
        [unit, tgt],
        "pack_rest",
    )


CHUNK = 256


def raise_best(best, keys, queries, triangular=False):
    rows = queries.shape[0]
    chunk = min(CHUNK, rows) if triangular else rows
    for start in range(0, rows, chunk):
        count = start + chunk if triangular else keys.shape[0]
        sims = matmul(keys[:count, :], queries[start : start + chunk, :], ((1,), (1,)))
        filled = keys[:count, :LANES].astype(F32) < 1.5
        parts = []
        for first in range(0, chunk, LANES):
            allowed = filled
            if triangular:
                allowed = filled & (
                    iota((count, LANES), 0) < iota((count, LANES), 1) + (start + first)
                )
            part = jnp.where(allowed, sims[:, first : first + LANES], F32(-1.0))
            parts.append(jnp.max(part, axis=0, keepdims=True))
        window = slice(start, start + chunk)
        best[:, window] = jnp.maximum(best[:, window], jnp.concatenate(parts, axis=1))


def gather_group(blocks, cluster, out, me):
    per = blocks[0].shape[0] // CLUS_DEV
    for step, block in enumerate(blocks):
        place = (me & (len(blocks) - 1)) ^ step
        rows = pl.ds(pl.multiple_of(place * per, per), per)
        out[rows, :] = block[cluster * per : (cluster + 1) * per, :]


def score_pairs(bests, groups, new, old, bit, me):
    later = (me & bit) == 0

    @pl.when(later)
    def _():
        for best, group in zip(bests, groups):
            raise_best(best[new], group[old], group[new])

    @pl.when(jnp.logical_not(later))
    def _():
        for best, group in zip(bests, groups):
            raise_best(best[old], group[new], group[old])


def fresh_best(rows):
    ones = jnp.ones((8, LANES), BF)
    heads = matmul(ones, rows[:, :LANES], ((1,), (1,)))[:1]
    return jnp.where(heads < 100.0, F32(-1.0), F32(UNFILLED))


def own_early(cuts, bits, *refs):
    blocks, (send, best) = refs[:-2], refs[-2:]
    per = blocks[0].shape[0] // CLUS_DEV
    near = cuts[1] // per
    blocks = blocks[near - 1 :: -1] + blocks[near:]
    me = lax.axis_index("clus")
    spans = list(zip(cuts, cuts[1:]))
    bests = [[best.at[c : c + 1, a:b] for a, b in spans] for c in range(CLUS_DEV)]
    groups = [[send.at[1, c, a:b] for a, b in spans] for c in range(CLUS_DEV)]
    for c in range(CLUS_DEV):
        for i, (a, b) in enumerate(spans):
            gather_group(blocks[a // per : b // per], c, groups[c][i], me)
            bests[c][i][...] = fresh_best(groups[c][i])
            raise_best(bests[c][i], groups[c][i], groups[c][i], True)
        send[0, c] = send[1, c]
    score_pairs(bests, groups, 1, 0, bits[0], me)


def cross_early(received, before, best):
    best[...] = before[...]

    @pl.when(lax.axis_index("blk") == 1)
    def _():
        for c in range(CLUS_DEV):
            raise_best(best.at[c : c + 1, : received.shape[2]], received.at[0, c], received.at[1, c])


def gather_late(*refs):
    blocks, out = refs[:-1], refs[-1]
    for c in range(CLUS_DEV):
        gather_group(blocks, c, out.at[c], lax.axis_index("clus"))


def own_late(cuts, bits, received, cat, before, best):
    me = lax.axis_index("clus")
    core = lax.axis_index("blk")
    spans = list(zip(cuts, cuts[1:]))
    last = len(spans) - 1
    start = spans[last][0]
    best[:, :start] = before[:, :start]
    bests = [[best.at[c : c + 1, a:b] for a, b in spans] for c in range(CLUS_DEV)]
    groups = [
        [received.at[core, c, a:b] for a, b in spans[:-1]] + [cat.at[c]] for c in range(CLUS_DEV)
    ]
    for c in range(CLUS_DEV):
        bests[c][last][...] = fresh_best(cat.at[c])
        raise_best(bests[c][last], cat.at[c], cat.at[c], True)
    score_pairs(bests, groups, last, 0, bits[0], me)
    score_pairs(bests, groups, 1, last, bits[1], me)

    @pl.when(core == 1)
    def _():
        for c in range(CLUS_DEV):
            raise_best(bests[c][last], received.at[0, c], cat.at[c])


def cross_late(cuts, starts, per, received, cat, before, other, out, best):
    me = lax.axis_index("clus")
    core = lax.axis_index("blk")
    spans = list(zip(cuts, cuts[1:]))
    best[...] = before[...]

    @pl.when(core == 1)
    def _():
        start = spans[-1][0]
        for c in range(CLUS_DEV):
            fresh = best.at[c : c + 1, start:]
            raise_best(best.at[c : c + 1, :start], other.at[c], received.at[1, c])
            raise_best(fresh, other.at[c], cat.at[c])

    for (a, b), first in zip(spans, starts):
        place = (me ^ first) & ~((b - a) // per - 1)
        value = best[:, a:b]
        at = pl.ds(pl.multiple_of(place * per, LANES), b - a)
        out[:, at] = jnp.where(value > 0.5 * UNFILLED, F32(0.0), value)


def local(embeddings, cluster_ids):
    owners = lax.axis_size("clus")
    clusters = CLUS_DEV * owners
    rows, width = embeddings.shape
    per = 2 * rows // clusters
    bits = [owners // 2, owners // 4]
    half, rest = owners // 2, owners - owners // 4
    near, far, late = [list(range(*x)) for x in ((0, half), (rest, owners), (half, rest))]
    starts = [near[0], far[0], late[0]]
    cuts = [0, half * per, rest * per, rows]
    best_shape = jax.ShapeDtypeStruct((CLUS_DEV, rows), F32)

    def to_owner(block, step):
        return lax.ppermute(block, "clus", [(i, i ^ step) for i in range(owners)])

    def stage_shape(sources):
        return jax.ShapeDtypeStruct((2, CLUS_DEV, sources * per, width), BF)

    def to_both(send):
        return lax.all_to_all(send, "blk", split_axis=0, concat_axis=0, tiled=True)

    arrived = {}
    lead = far[:1]
    unit, tgt, *packed = call_pack_first(embeddings, cluster_ids, lead, clusters, per)
    for steps in (near[1:] + far[1:] + [0], []):
        for step, block in zip(lead, packed):
            arrived[step] = to_owner(block, step) if step else block
        lead, packed = steps, call_pack_rest(unit, tgt, steps, per) if steps else []
    packed = call_pack_rest(unit, tgt, late, per)
    *held, arrived[far[0]] = lax.optimization_barrier((*packed, arrived[far[0]]))
    for step, block in zip(late, held):
        arrived[step] = to_owner(block, step)

    early = near + far
    send, best = kernel_call(
        functools.partial(own_early, cuts[:3], bits),
        [stage_shape(len(early)), best_shape],
        [arrived[s] for s in near[::-1] + far],
        "own_early",
    )
    received = to_both(send)
    (best,) = kernel_call(cross_early, [best_shape], [received, best], "cross_early")
    *new, best = lax.optimization_barrier((*[arrived[s] for s in late], best))
    cat_shape = jax.ShapeDtypeStruct((CLUS_DEV, len(late) * per, width), BF)
    (cat,) = kernel_call(gather_late, [cat_shape], new, "gather_late")
    other = lax.ppermute(cat, "blk", [(0, 1)])
    (best,) = kernel_call(
        functools.partial(own_late, cuts, bits), [best_shape], [received, cat, best], "own_late"
    )
    (out,) = kernel_call(
        functools.partial(cross_late, cuts, starts, per),
        [best_shape],
        [received, cat, best, other],
        "cross_late",
        [pltpu.VMEM((CLUS_DEV, rows), F32)],
    )
    return out


def solution(mesh):
    placed = (P(("groups", "clus", "blk"), None), P(("groups", "clus", "blk"), None))
    return jax.shard_map(
        local, mesh=mesh, in_specs=placed, out_specs=P(("groups", "clus"), "blk"), check_vma=False
    )
```

```python
import functools

import jax
import jax.numpy as jnp
from jax import lax
from jax.experimental import pallas as pl
from jax.experimental.pallas import tpu as pltpu
from jax.sharding import PartitionSpec as P

CLUS_DEV = 2
LANES = 128
MARK = 2.0
UNFILLED = 8.0
BF = jnp.bfloat16
F32 = jnp.float32


def iota(shape, dim):
    return lax.broadcasted_iota(jnp.int32, shape, dim)


def matmul(a, b, contract):
    return lax.dot_general(a, b, (contract, ((), ())), preferred_element_type=F32)


def targets(ids, clusters, per_source):
    groups = ids.shape[1] // LANES
    parts = [ids[:, g * LANES : (g + 1) * LANES] for g in range(groups)]
    hot = jnp.concatenate(
        [(iota((clusters, LANES), 0) == part).astype(F32) for part in parts], axis=0
    )
    stacked = groups * clusters
    earlier = (iota((LANES, LANES), 0) < iota((LANES, LANES), 1)).astype(F32).astype(BF)
    within = matmul(hot.astype(BF), earlier, ((1,), (0,)))
    totals = jnp.broadcast_to(jnp.sum(hot, axis=1, keepdims=True), (stacked, LANES))
    a, b = iota((stacked, stacked), 0), iota((stacked, stacked), 1)
    chunks_before = ((a % clusters == b % clusters) & (b < a)).astype(F32).astype(BF)
    before = within + matmul(chunks_before, totals.astype(BF), ((1,), (0,)))
    picked = hot * before
    out = [
        jnp.sum(picked[g * clusters : (g + 1) * clusters], axis=0, keepdims=True).astype(jnp.int32)
        + parts[g] * per_source
        for g in range(groups)
    ]
    return jnp.concatenate(out, axis=1)


def pack_block(unit, tgt, dest, width):
    hit = (tgt - dest * width) == iota((width, tgt.shape[1]), 0)
    hot = hit.astype(F32)
    rows = matmul(hot.astype(BF), unit, ((1,), (0,)))
    empty = jnp.max(hot, axis=1, keepdims=True) < 0.5
    head = jnp.where(empty, F32(MARK), rows[:, :LANES])
    return head.astype(BF), rows[:, LANES:].astype(BF)


def store_blocks(unit, tgt, steps, width, outs):
    me = lax.axis_index("clus")
    for step, out in zip(steps, outs):
        head, tail = pack_block(unit, tgt, me ^ step, width)
        out[:, :LANES] = head
        out[:, LANES:] = tail


PIECES = 4


def pack_first(steps, clusters, per_source, emb, ids, unit, tgt, *refs):
    outs, (raw, raw_ids, sems, ids_sem) = refs[:-4], refs[-4:]
    size = emb.shape[0] // PIECES
    ids_copy = pltpu.make_async_copy(ids, raw_ids, ids_sem)
    ids_copy.start()
    windows = [pl.ds(piece * size, size) for piece in range(PIECES)]
    copies = [
        pltpu.make_async_copy(emb.at[window], raw.at[window], sems.at[piece])
        for piece, window in enumerate(windows)
    ]
    for copy in copies:
        copy.start()
    ids_copy.wait()
    tgt[...] = targets(raw_ids[...], clusters, per_source)
    for copy, window in zip(copies, windows):
        copy.wait()
        values = raw[window, :].astype(F32)
        scale = lax.rsqrt(jnp.sum(values * values, axis=1, keepdims=True) + 1e-6)
        unit[window, :] = (values * scale).astype(BF)
    store_blocks(unit[...], tgt[...], steps, CLUS_DEV * per_source, outs)


def pack_rest(steps, per_source, unit, tgt, *outs):
    store_blocks(unit[...], tgt[...], steps, CLUS_DEV * per_source, outs)


VMEM = pl.BlockSpec(memory_space=pltpu.VMEM)


def kernel_call(kernel, shapes, inputs, name, scratch=(), place=VMEM, grant=20 * 2**20):
    return pl.pallas_call(
        kernel,
        out_shape=shapes,
        in_specs=[place] * len(inputs),
        out_specs=[VMEM] * len(shapes),
        scratch_shapes=scratch,
        compiler_params=pltpu.CompilerParams(vmem_limit_bytes=grant),
        cost_estimate=pl.CostEstimate(flops=1000, bytes_accessed=1000, transcendentals=0),
        name=name,
    )(*inputs)


def call_pack_first(emb, ids, steps, clusters, per_source):
    block = jax.ShapeDtypeStruct((CLUS_DEV * per_source, emb.shape[1]), BF)
    shapes = [jax.ShapeDtypeStruct(emb.shape, BF), jax.ShapeDtypeStruct(ids.shape, jnp.int32)]
    return kernel_call(
        functools.partial(pack_first, steps, clusters, per_source),
        shapes + [block] * len(steps),
        [emb, ids],
        place=pl.BlockSpec(memory_space=pl.ANY),
        grant=50 * 2**20,
        name="pack_first",
        scratch=[
            pltpu.VMEM(emb.shape, BF),
            pltpu.VMEM(ids.shape, jnp.int32),
            pltpu.SemaphoreType.DMA((PIECES,)),
            pltpu.SemaphoreType.DMA,
        ],
    )


def call_pack_rest(unit, tgt, steps, per_source):
    block = jax.ShapeDtypeStruct((CLUS_DEV * per_source, unit.shape[1]), BF)
    return kernel_call(
        functools.partial(pack_rest, steps, per_source),
        [block] * len(steps),
        [unit, tgt],
        "pack_rest",
    )


CHUNK = 256


def raise_best(best, keys, queries, triangular=False):
    rows = queries.shape[0]
    chunk = min(CHUNK, rows) if triangular else rows
    for start in range(0, rows, chunk):
        count = start + chunk if triangular else keys.shape[0]
        sims = matmul(keys[:count, :], queries[start : start + chunk, :], ((1,), (1,)))
        filled = keys[:count, :LANES].astype(F32) < 1.5
        parts = []
        for first in range(0, chunk, LANES):
            allowed = filled
            if triangular:
                allowed = filled & (
                    iota((count, LANES), 0) < iota((count, LANES), 1) + (start + first)
                )
            part = jnp.where(allowed, sims[:, first : first + LANES], F32(-1.0))
            parts.append(jnp.max(part, axis=0, keepdims=True))
        window = slice(start, start + chunk)
        best[:, window] = jnp.maximum(best[:, window], jnp.concatenate(parts, axis=1))


def gather_group(blocks, cluster, out, me):
    per = blocks[0].shape[0] // CLUS_DEV
    for step, block in enumerate(blocks):
        place = (me & (len(blocks) - 1)) ^ step
        rows = pl.ds(pl.multiple_of(place * per, per), per)
        out[rows, :] = block[cluster * per : (cluster + 1) * per, :]


def score_pairs(bests, groups, new, old, bit, me):
    later = (me & bit) == 0

    @pl.when(later)
    def _():
        for best, group in zip(bests, groups):
            raise_best(best[new], group[old], group[new])

    @pl.when(jnp.logical_not(later))
    def _():
        for best, group in zip(bests, groups):
            raise_best(best[old], group[new], group[old])


def fresh_best(rows):
    ones = jnp.ones((8, LANES), BF)
    heads = matmul(ones, rows[:, :LANES], ((1,), (1,)))[:1]
    return jnp.where(heads < 100.0, F32(-1.0), F32(UNFILLED))


def own_early(cuts, bits, *refs):
    blocks, (send, best) = refs[:-2], refs[-2:]
    per = blocks[0].shape[0] // CLUS_DEV
    me = lax.axis_index("clus")
    spans = list(zip(cuts, cuts[1:]))
    bests = [[best.at[c : c + 1, a:b] for a, b in spans] for c in range(CLUS_DEV)]
    groups = [[send.at[1, c, a:b] for a, b in spans] for c in range(CLUS_DEV)]
    for c in range(CLUS_DEV):
        for i, (a, b) in enumerate(spans):
            gather_group(blocks[a // per : b // per], c, groups[c][i], me)
            bests[c][i][...] = fresh_best(groups[c][i])
            raise_best(bests[c][i], groups[c][i], groups[c][i], True)
        send[0, c] = send[1, c]
    score_pairs(bests, groups, 1, 0, bits[0], me)


def cross_early(received, before, best):
    best[...] = before[...]

    @pl.when(lax.axis_index("blk") == 1)
    def _():
        for c in range(CLUS_DEV):
            raise_best(best.at[c : c + 1, : received.shape[2]], received.at[0, c], received.at[1, c])


def gather_late(*refs):
    blocks, out = refs[:-1], refs[-1]
    for c in range(CLUS_DEV):
        gather_group(blocks, c, out.at[c], lax.axis_index("clus"))


def own_late(cuts, bits, received, cat, before, best):
    me = lax.axis_index("clus")
    core = lax.axis_index("blk")
    spans = list(zip(cuts, cuts[1:]))
    last = len(spans) - 1
    start = spans[last][0]
    best[:, :start] = before[:, :start]
    bests = [[best.at[c : c + 1, a:b] for a, b in spans] for c in range(CLUS_DEV)]
    groups = [
        [received.at[core, c, a:b] for a, b in spans[:-1]] + [cat.at[c]] for c in range(CLUS_DEV)
    ]
    for c in range(CLUS_DEV):
        bests[c][last][...] = fresh_best(cat.at[c])
        raise_best(bests[c][last], cat.at[c], cat.at[c], True)
    for i in range(last):
        score_pairs(bests, groups, last, i, bits[i], me)

    @pl.when(core == 1)
    def _():
        for c in range(CLUS_DEV):
            raise_best(bests[c][last], received.at[0, c], cat.at[c])


def cross_late(cuts, per, received, cat, before, other, out, best):
    me = lax.axis_index("clus")
    core = lax.axis_index("blk")
    spans = list(zip(cuts, cuts[1:]))
    best[...] = before[...]

    @pl.when(core == 1)
    def _():
        start = spans[-1][0]
        for c in range(CLUS_DEV):
            fresh = best.at[c : c + 1, start:]
            raise_best(best.at[c : c + 1, :start], other.at[c], received.at[1, c])
            raise_best(fresh, other.at[c], cat.at[c])

    for a, b in spans:
        place = (me ^ (a // per)) & ~((b - a) // per - 1)
        value = best[:, a:b]
        at = pl.ds(pl.multiple_of(place * per, LANES), b - a)
        out[:, at] = jnp.where(value > 0.5 * UNFILLED, F32(0.0), value)


def local(embeddings, cluster_ids):
    owners = lax.axis_size("clus")
    clusters = CLUS_DEV * owners
    rows, width = embeddings.shape
    per = 2 * rows // clusters
    bits = [owners // 2, owners // 4]
    bounds = [0, owners // 2, owners // 2 + owners // 4, owners]
    cuts = [x * per for x in bounds]
    near, far, late = [list(range(a, b)) for a, b in zip(bounds, bounds[1:])]
    best_shape = jax.ShapeDtypeStruct((CLUS_DEV, rows), F32)

    def to_owner(block, step):
        return lax.ppermute(block, "clus", [(i, i ^ step) for i in range(owners)])

    def stage_shape(sources):
        return jax.ShapeDtypeStruct((2, CLUS_DEV, sources * per, width), BF)

    def to_both(send):
        return lax.all_to_all(send, "blk", split_axis=0, concat_axis=0, tiled=True)

    arrived = {}
    lead = [near[-1], far[0]]
    unit, tgt, *packed = call_pack_first(embeddings, cluster_ids, lead, clusters, per)
    for steps in (near[1:-1] + far[1:] + [0], []):
        for step, block in zip(lead, packed):
            arrived[step] = to_owner(block, step) if step else block
        lead, packed = steps, call_pack_rest(unit, tgt, steps, per) if steps else []
    packed = call_pack_rest(unit, tgt, late, per)
    *held, arrived[near[-1]], arrived[far[0]] = lax.optimization_barrier(
        (*packed, arrived[near[-1]], arrived[far[0]])
    )
    for step, block in zip(late, held):
        arrived[step] = to_owner(block, step)

    early = near + far
    send, best = kernel_call(
        functools.partial(own_early, cuts[:3], bits),
        [stage_shape(len(early)), best_shape],
        [arrived[s] for s in early],
        "own_early",
    )
    received = to_both(send)
    (best,) = kernel_call(cross_early, [best_shape], [received, best], "cross_early")
    *new, best = lax.optimization_barrier((*[arrived[s] for s in late], best))
    cat_shape = jax.ShapeDtypeStruct((CLUS_DEV, len(late) * per, width), BF)
    (cat,) = kernel_call(gather_late, [cat_shape], new, "gather_late")
    other = lax.ppermute(cat, "blk", [(0, 1)])
    (best,) = kernel_call(
        functools.partial(own_late, cuts, bits), [best_shape], [received, cat, best], "own_late"
    )
    (out,) = kernel_call(
        functools.partial(cross_late, cuts, per),
        [best_shape],
        [received, cat, best, other],
        "cross_late",
        [pltpu.VMEM((CLUS_DEV, rows), F32)],
    )
    return out


def solution(mesh):
    placed = (P(("groups", "clus", "blk"), None), P(("groups", "clus", "blk"), None))
    return jax.shard_map(
        local, mesh=mesh, in_specs=placed, out_specs=P(("groups", "clus"), "blk"), check_vma=False
    )
```

```python
import functools

import jax
import jax.numpy as jnp
from jax import lax
from jax.experimental import pallas as pl
from jax.experimental.pallas import tpu as pltpu
from jax.sharding import PartitionSpec as P

CLUS_DEV = 2
LANES = 128
MARK = 2.0
UNFILLED = 8.0
BF = jnp.bfloat16
F32 = jnp.float32


def iota(shape, dim):
    return lax.broadcasted_iota(jnp.int32, shape, dim)


def matmul(a, b, contract):
    return lax.dot_general(a, b, (contract, ((), ())), preferred_element_type=F32)


def targets(ids, clusters, per_source):
    groups = ids.shape[1] // LANES
    parts = [ids[:, g * LANES : (g + 1) * LANES] for g in range(groups)]
    hot = jnp.concatenate(
        [(iota((clusters, LANES), 0) == part).astype(F32) for part in parts], axis=0
    )
    stacked = groups * clusters
    earlier = (iota((LANES, LANES), 0) < iota((LANES, LANES), 1)).astype(F32).astype(BF)
    within = matmul(hot.astype(BF), earlier, ((1,), (0,)))
    totals = jnp.broadcast_to(jnp.sum(hot, axis=1, keepdims=True), (stacked, LANES))
    a, b = iota((stacked, stacked), 0), iota((stacked, stacked), 1)
    chunks_before = ((a % clusters == b % clusters) & (b < a)).astype(F32).astype(BF)
    before = within + matmul(chunks_before, totals.astype(BF), ((1,), (0,)))
    picked = hot * before
    out = [
        jnp.sum(picked[g * clusters : (g + 1) * clusters], axis=0, keepdims=True).astype(jnp.int32)
        + parts[g] * per_source
        for g in range(groups)
    ]
    return jnp.concatenate(out, axis=1)


def pack_block(unit, tgt, dest, width):
    hit = (tgt - dest * width) == iota((width, tgt.shape[1]), 0)
    hot = hit.astype(F32)
    rows = matmul(hot.astype(BF), unit, ((1,), (0,)))
    empty = jnp.max(hot, axis=1, keepdims=True) < 0.5
    head = jnp.where(empty, F32(MARK), rows[:, :LANES])
    return head.astype(BF), rows[:, LANES:].astype(BF)


def store_blocks(unit, tgt, steps, width, outs):
    me = lax.axis_index("clus")
    for step, out in zip(steps, outs):
        head, tail = pack_block(unit, tgt, me ^ step, width)
        out[:, :LANES] = head
        out[:, LANES:] = tail


PIECES = 4


def pack_first(steps, clusters, per_source, emb, ids, unit, tgt, *refs):
    outs, (raw, raw_ids, sems, ids_sem) = refs[:-4], refs[-4:]
    size = emb.shape[0] // PIECES
    ids_copy = pltpu.make_async_copy(ids, raw_ids, ids_sem)
    ids_copy.start()
    windows = [pl.ds(piece * size, size) for piece in range(PIECES)]
    copies = [
        pltpu.make_async_copy(emb.at[window], raw.at[window], sems.at[piece])
        for piece, window in enumerate(windows)
    ]
    for copy in copies:
        copy.start()
    ids_copy.wait()
    tgt[...] = targets(raw_ids[...], clusters, per_source)
    for copy, window in zip(copies, windows):
        copy.wait()
        values = raw[window, :].astype(F32)
        scale = lax.rsqrt(jnp.sum(values * values, axis=1, keepdims=True) + 1e-6)
        unit[window, :] = (values * scale).astype(BF)
    store_blocks(unit[...], tgt[...], steps, CLUS_DEV * per_source, outs)


def pack_rest(steps, per_source, unit, tgt, *outs):
    store_blocks(unit[...], tgt[...], steps, CLUS_DEV * per_source, outs)


VMEM = pl.BlockSpec(memory_space=pltpu.VMEM)


def kernel_call(kernel, shapes, inputs, name, scratch=(), place=VMEM, grant=20 * 2**20):
    return pl.pallas_call(
        kernel,
        out_shape=shapes,
        in_specs=[place] * len(inputs),
        out_specs=[VMEM] * len(shapes),
        scratch_shapes=scratch,
        compiler_params=pltpu.CompilerParams(vmem_limit_bytes=grant),
        cost_estimate=pl.CostEstimate(flops=1000, bytes_accessed=1000, transcendentals=0),
        name=name,
    )(*inputs)


def call_pack_first(emb, ids, steps, clusters, per_source):
    block = jax.ShapeDtypeStruct((CLUS_DEV * per_source, emb.shape[1]), BF)
    shapes = [jax.ShapeDtypeStruct(emb.shape, BF), jax.ShapeDtypeStruct(ids.shape, jnp.int32)]
    return kernel_call(
        functools.partial(pack_first, steps, clusters, per_source),
        shapes + [block] * len(steps),
        [emb, ids],
        place=pl.BlockSpec(memory_space=pl.ANY),
        grant=50 * 2**20,
        name="pack_first",
        scratch=[
            pltpu.VMEM(emb.shape, BF),
            pltpu.VMEM(ids.shape, jnp.int32),
            pltpu.SemaphoreType.DMA((PIECES,)),
            pltpu.SemaphoreType.DMA,
        ],
    )


def call_pack_rest(unit, tgt, steps, per_source):
    block = jax.ShapeDtypeStruct((CLUS_DEV * per_source, unit.shape[1]), BF)
    return kernel_call(
        functools.partial(pack_rest, steps, per_source),
        [block] * len(steps),
        [unit, tgt],
        "pack_rest",
    )


CHUNK = 256


def raise_best(best, keys, queries, triangular=False):
    rows = queries.shape[0]
    chunk = min(CHUNK, rows) if triangular else rows
    for start in range(0, rows, chunk):
        count = start + chunk if triangular else keys.shape[0]
        sims = matmul(keys[:count, :], queries[start : start + chunk, :], ((1,), (1,)))
        filled = keys[:count, :LANES].astype(F32) < 1.5
        parts = []
        for first in range(0, chunk, LANES):
            allowed = filled
            if triangular:
                allowed = filled & (
                    iota((count, LANES), 0) < iota((count, LANES), 1) + (start + first)
                )
            part = jnp.where(allowed, sims[:, first : first + LANES], F32(-1.0))
            parts.append(jnp.max(part, axis=0, keepdims=True))
        window = slice(start, start + chunk)
        best[:, window] = jnp.maximum(best[:, window], jnp.concatenate(parts, axis=1))


def gather_group(blocks, cluster, out, me):
    per = blocks[0].shape[0] // CLUS_DEV
    for step, block in enumerate(blocks):
        place = (me & (len(blocks) - 1)) ^ step
        rows = pl.ds(pl.multiple_of(place * per, per), per)
        out[rows, :] = block[cluster * per : (cluster + 1) * per, :]


def score_pairs(bests, groups, new, old, bit, me):
    later = (me & bit) == 0

    @pl.when(later)
    def _():
        for best, group in zip(bests, groups):
            raise_best(best[new], group[old], group[new])

    @pl.when(jnp.logical_not(later))
    def _():
        for best, group in zip(bests, groups):
            raise_best(best[old], group[new], group[old])


def fresh_best(rows):
    ones = jnp.ones((8, LANES), BF)
    heads = matmul(ones, rows[:, :LANES], ((1,), (1,)))[:1]
    return jnp.where(heads < 100.0, F32(-1.0), F32(UNFILLED))


def own_early(cuts, bits, *refs):
    blocks, (send, best) = list(reversed(refs[:-2])), refs[-2:]
    per = blocks[0].shape[0] // CLUS_DEV
    me = lax.axis_index("clus")
    spans = list(zip(cuts, cuts[1:]))
    bests = [[best.at[c : c + 1, a:b] for a, b in spans] for c in range(CLUS_DEV)]
    groups = [[send.at[1, c, a:b] for a, b in spans] for c in range(CLUS_DEV)]
    for c in range(CLUS_DEV):
        for i, (a, b) in enumerate(spans):
            gather_group(blocks[a // per : b // per], c, groups[c][i], me)
            bests[c][i][...] = fresh_best(groups[c][i])
            raise_best(bests[c][i], groups[c][i], groups[c][i], True)
        send[0, c] = send[1, c]
    score_pairs(bests, groups, 1, 0, bits[0], me)


def cross_early(received, before, best):
    best[...] = before[...]

    @pl.when(lax.axis_index("blk") == 1)
    def _():
        for c in range(CLUS_DEV):
            raise_best(best.at[c : c + 1, : received.shape[2]], received.at[0, c], received.at[1, c])


def gather_late(*refs):
    blocks, out = refs[:-1], refs[-1]
    for c in range(CLUS_DEV):
        gather_group(blocks, c, out.at[c], lax.axis_index("clus"))


def own_late(cuts, bits, received, first, second, before, cat, best):
    me = lax.axis_index("clus")
    size = second.shape[1]
    swapped = (me & (bits[-1] // 2)) != 0
    for half, swap in ((first, swapped), (second, jnp.logical_not(swapped))):
        rows = pl.ds(pl.multiple_of(jnp.where(swap, size, 0), size), size)
        for c in range(CLUS_DEV):
            cat[c, rows, :] = half[c, :size, :]
    core = lax.axis_index("blk")
    spans = list(zip(cuts, cuts[1:]))
    last = len(spans) - 1
    start = spans[last][0]
    best[:, :start] = before[:, :start]
    bests = [[best.at[c : c + 1, a:b] for a, b in spans] for c in range(CLUS_DEV)]
    groups = [
        [received.at[core, c, a:b] for a, b in spans[:-1]] + [cat.at[c]] for c in range(CLUS_DEV)
    ]
    for c in range(CLUS_DEV):
        bests[c][last][...] = fresh_best(cat.at[c])
        raise_best(bests[c][last], cat.at[c], cat.at[c], True)
    for i in range(last):
        score_pairs(bests, groups, last, i, bits[i], me)

    @pl.when(core == 1)
    def _():
        for c in range(CLUS_DEV):
            raise_best(bests[c][last], received.at[0, c], cat.at[c])


def cross_late(cuts, per, received, cat, before, first, second, out, best, keys):
    me = lax.axis_index("clus")
    core = lax.axis_index("blk")
    spans = list(zip(cuts, cuts[1:]))
    best[...] = before[...]

    @pl.when(core == 1)
    def _():
        start = spans[-1][0]
        size = second.shape[1]
        for c in range(CLUS_DEV):
            keys[c, :size, :] = first[c, :size, :]
            keys[c, size:, :] = second[c]
            fresh = best.at[c : c + 1, start:]
            raise_best(best.at[c : c + 1, :start], keys.at[c], received.at[1, c])
            raise_best(fresh, keys.at[c], cat.at[c])

    for a, b in spans:
        place = (me ^ (a // per)) & ~((b - a) // per - 1)
        value = best[:, a:b]
        at = pl.ds(pl.multiple_of(place * per, LANES), b - a)
        out[:, at] = jnp.where(value > 0.5 * UNFILLED, F32(0.0), value)


def local(embeddings, cluster_ids):
    owners = lax.axis_size("clus")
    clusters = CLUS_DEV * owners
    rows, width = embeddings.shape
    per = 2 * rows // clusters
    bits = [owners // 2, owners // 4]
    bounds = [0, owners // 2, owners // 2 + owners // 4, owners]
    cuts = [x * per for x in bounds]
    near, far, late = [list(range(a, b)) for a, b in zip(bounds, bounds[1:])]
    best_shape = jax.ShapeDtypeStruct((CLUS_DEV, rows), F32)

    def to_owner(block, step):
        return lax.ppermute(block, "clus", [(i, i ^ step) for i in range(owners)])

    def stage_shape(sources):
        return jax.ShapeDtypeStruct((2, CLUS_DEV, sources * per, width), BF)

    def to_both(send):
        return lax.all_to_all(send, "blk", split_axis=0, concat_axis=0, tiled=True)

    arrived = {}
    lead = far[:1]
    unit, tgt, *packed = call_pack_first(embeddings, cluster_ids, lead, clusters, per)
    for steps in (near[1:] + far[1:] + [0], []):
        for step, block in zip(lead, packed):
            arrived[step] = to_owner(block, step) if step else block
        lead, packed = steps, call_pack_rest(unit, tgt, steps, per) if steps else []
    packed = call_pack_rest(unit, tgt, late, per)
    *held, arrived[far[0]] = lax.optimization_barrier((*packed, arrived[far[0]]))
    for step, block in zip(late, held):
        arrived[step] = to_owner(block, step)

    early = near + far
    send, best = kernel_call(
        functools.partial(own_early, cuts[:3], bits),
        [stage_shape(len(early)), best_shape],
        [arrived[s] for s in reversed(early)],
        "own_early",
    )
    received = to_both(send)
    (best,) = kernel_call(cross_early, [best_shape], [received, best], "cross_early")
    count = len(late) // 2
    size = count * per
    count = len(late) // 2
    size = count * per
    halves, others = [], []
    for steps, spare in ((late[:count], size // 2), (late[count:], 0)):
        *new, best = lax.optimization_barrier((*[arrived[s] for s in steps], best))
        half_shape = jax.ShapeDtypeStruct((CLUS_DEV, size + spare, width), BF)
        (half,) = kernel_call(gather_late, [half_shape], new, "gather_late")
        others.append(lax.ppermute(half, "blk", [(0, 1)]))
        half, best = lax.optimization_barrier((half, best))
        halves.append(half)
    cat_shape = jax.ShapeDtypeStruct((CLUS_DEV, 2 * size, width), BF)
    cat, best = kernel_call(
        functools.partial(own_late, cuts, bits),
        [cat_shape, best_shape],
        [received] + halves + [best],
        "own_late",
    )
    (out,) = kernel_call(
        functools.partial(cross_late, cuts, per),
        [best_shape],
        [received, cat, best] + others,
        "cross_late",
        [pltpu.VMEM((CLUS_DEV, rows), F32), pltpu.VMEM(cat_shape.shape, BF)],
    )
    return out


def solution(mesh):
    placed = (P(("groups", "clus", "blk"), None), P(("groups", "clus", "blk"), None))
    return jax.shard_map(
        local, mesh=mesh, in_specs=placed, out_specs=P(("groups", "clus"), "blk"), check_vma=False
    )
```

```python
import functools

import jax
import jax.numpy as jnp
from jax import lax
from jax.experimental import pallas as pl
from jax.experimental.pallas import tpu as pltpu
from jax.sharding import PartitionSpec as P

CLUS_DEV = 2
LANES = 128
MARK = 2.0
UNFILLED = 8.0
BF = jnp.bfloat16
F32 = jnp.float32


def iota(shape, dim):
    return lax.broadcasted_iota(jnp.int32, shape, dim)


def matmul(a, b, contract):
    return lax.dot_general(a, b, (contract, ((), ())), preferred_element_type=F32)


def targets(ids, clusters, per_source):
    groups = ids.shape[1] // LANES
    parts = [ids[:, g * LANES : (g + 1) * LANES] for g in range(groups)]
    hot = jnp.concatenate(
        [(iota((clusters, LANES), 0) == part).astype(F32) for part in parts], axis=0
    )
    stacked = groups * clusters
    earlier = (iota((LANES, LANES), 0) < iota((LANES, LANES), 1)).astype(F32).astype(BF)
    within = matmul(hot.astype(BF), earlier, ((1,), (0,)))
    totals = jnp.broadcast_to(jnp.sum(hot, axis=1, keepdims=True), (stacked, LANES))
    a, b = iota((stacked, stacked), 0), iota((stacked, stacked), 1)
    chunks_before = ((a % clusters == b % clusters) & (b < a)).astype(F32).astype(BF)
    before = within + matmul(chunks_before, totals.astype(BF), ((1,), (0,)))
    picked = hot * before
    out = [
        jnp.sum(picked[g * clusters : (g + 1) * clusters], axis=0, keepdims=True).astype(jnp.int32)
        + parts[g] * per_source
        for g in range(groups)
    ]
    return jnp.concatenate(out, axis=1)


def pack_block(unit, tgt, dest, width):
    hit = (tgt - dest * width) == iota((width, tgt.shape[1]), 0)
    hot = hit.astype(F32)
    rows = matmul(hot.astype(BF), unit, ((1,), (0,)))
    empty = jnp.max(hot, axis=1, keepdims=True) < 0.5
    head = jnp.where(empty, F32(MARK), rows[:, :LANES])
    return head.astype(BF), rows[:, LANES:].astype(BF)


def store_blocks(unit, tgt, steps, width, outs):
    me = lax.axis_index("clus")
    for step, out in zip(steps, outs):
        head, tail = pack_block(unit, tgt, me ^ step, width)
        out[:, :LANES] = head
        out[:, LANES:] = tail


PIECES = 4


def pack_first(steps, clusters, per_source, emb, ids, unit, tgt, *refs):
    outs, (raw, raw_ids, sems, ids_sem) = refs[:-4], refs[-4:]
    size = emb.shape[0] // PIECES
    ids_copy = pltpu.make_async_copy(ids, raw_ids, ids_sem)
    ids_copy.start()
    windows = [pl.ds(piece * size, size) for piece in range(PIECES)]
    copies = [
        pltpu.make_async_copy(emb.at[window], raw.at[window], sems.at[piece])
        for piece, window in enumerate(windows)
    ]
    for copy in copies:
        copy.start()
    ids_copy.wait()
    tgt[...] = targets(raw_ids[...], clusters, per_source)
    for copy, window in zip(copies, windows):
        copy.wait()
        values = raw[window, :].astype(F32)
        scale = lax.rsqrt(jnp.sum(values * values, axis=1, keepdims=True) + 1e-6)
        unit[window, :] = (values * scale).astype(BF)
    store_blocks(unit[...], tgt[...], steps, CLUS_DEV * per_source, outs)


def pack_rest(steps, per_source, unit, tgt, *outs):
    store_blocks(unit[...], tgt[...], steps, CLUS_DEV * per_source, outs)


VMEM = pl.BlockSpec(memory_space=pltpu.VMEM)


def kernel_call(kernel, shapes, inputs, name, scratch=(), place=VMEM, grant=20 * 2**20):
    return pl.pallas_call(
        kernel,
        out_shape=shapes,
        in_specs=[place] * len(inputs),
        out_specs=[VMEM] * len(shapes),
        scratch_shapes=scratch,
        compiler_params=pltpu.CompilerParams(vmem_limit_bytes=grant),
        cost_estimate=pl.CostEstimate(flops=1000, bytes_accessed=1000, transcendentals=0),
        name=name,
    )(*inputs)


def call_pack_first(emb, ids, steps, clusters, per_source):
    block = jax.ShapeDtypeStruct((CLUS_DEV * per_source, emb.shape[1]), BF)
    shapes = [jax.ShapeDtypeStruct(emb.shape, BF), jax.ShapeDtypeStruct(ids.shape, jnp.int32)]
    return kernel_call(
        functools.partial(pack_first, steps, clusters, per_source),
        shapes + [block] * len(steps),
        [emb, ids],
        place=pl.BlockSpec(memory_space=pl.ANY),
        grant=50 * 2**20,
        name="pack_first",
        scratch=[
            pltpu.VMEM(emb.shape, BF),
            pltpu.VMEM(ids.shape, jnp.int32),
            pltpu.SemaphoreType.DMA((PIECES,)),
            pltpu.SemaphoreType.DMA,
        ],
    )


def call_pack_rest(unit, tgt, steps, per_source):
    block = jax.ShapeDtypeStruct((CLUS_DEV * per_source, unit.shape[1]), BF)
    return kernel_call(
        functools.partial(pack_rest, steps, per_source),
        [block] * len(steps),
        [unit, tgt],
        "pack_rest",
    )


CHUNK = 256


def raise_best(best, keys, queries, triangular=False):
    rows = queries.shape[0]
    chunk = min(CHUNK, rows) if triangular else rows
    for start in range(0, rows, chunk):
        count = start + chunk if triangular else keys.shape[0]
        sims = matmul(keys[:count, :], queries[start : start + chunk, :], ((1,), (1,)))
        filled = keys[:count, :LANES].astype(F32) < 1.5
        parts = []
        for first in range(0, chunk, LANES):
            allowed = filled
            if triangular:
                allowed = filled & (
                    iota((count, LANES), 0) < iota((count, LANES), 1) + (start + first)
                )
            part = jnp.where(allowed, sims[:, first : first + LANES], F32(-1.0))
            parts.append(jnp.max(part, axis=0, keepdims=True))
        window = slice(start, start + chunk)
        best[:, window] = jnp.maximum(best[:, window], jnp.concatenate(parts, axis=1))


def raise_wide(best, keys, queries, unfilled):
    sims = matmul(queries[...], keys[...], ((1,), (1,)))
    sims = jnp.where(unfilled > 1.0, F32(-1.0), sims)
    top = sims[:, :LANES]
    for first in range(LANES, sims.shape[1], LANES):
        top = jnp.maximum(top, sims[:, first : first + LANES])
    best[...] = jnp.maximum(best[...], jnp.max(top.T, axis=0, keepdims=True))


def gather_group(blocks, cluster, out, me):
    per = blocks[0].shape[0] // CLUS_DEV
    for step, block in enumerate(blocks):
        place = (me & (len(blocks) - 1)) ^ step
        rows = pl.ds(pl.multiple_of(place * per, per), per)
        out[rows, :] = block[cluster * per : (cluster + 1) * per, :]


def score_pairs(bests, groups, new, old, bit, me):
    later = (me & bit) == 0

    @pl.when(later)
    def _():
        for best, group in zip(bests, groups):
            raise_best(best[new], group[old], group[new])

    @pl.when(jnp.logical_not(later))
    def _():
        for best, group in zip(bests, groups):
            raise_best(best[old], group[new], group[old])


def fresh_best(rows):
    ones = jnp.ones((8, LANES), BF)
    heads = matmul(ones, rows[:, :LANES], ((1,), (1,)))[:1]
    return jnp.where(heads < 100.0, F32(-1.0), F32(UNFILLED))


def own_early(cuts, bits, *refs):
    blocks, (send, best) = list(reversed(refs[:-2])), refs[-2:]
    per = blocks[0].shape[0] // CLUS_DEV
    me = lax.axis_index("clus")
    spans = list(zip(cuts, cuts[1:]))
    bests = [[best.at[c : c + 1, a:b] for a, b in spans] for c in range(CLUS_DEV)]
    groups = [[send.at[1, c, a:b] for a, b in spans] for c in range(CLUS_DEV)]
    for c in range(CLUS_DEV):
        for i, (a, b) in enumerate(spans):
            gather_group(blocks[a // per : b // per], c, groups[c][i], me)
            bests[c][i][...] = fresh_best(groups[c][i])
            raise_best(bests[c][i], groups[c][i], groups[c][i], True)
        send[0, c] = send[1, c]
    score_pairs(bests, groups, 1, 0, bits[0], me)


def cross_early(received, before, best, unfilled):
    for c in range(CLUS_DEV):
        unfilled[c : c + 1, :] = fresh_best(received.at[0, c])
    best[...] = before[...]

    @pl.when(lax.axis_index("blk") == 1)
    def _():
        for c in range(CLUS_DEV):
            raise_best(best.at[c : c + 1, : received.shape[2]], received.at[0, c], received.at[1, c])


def gather_late(*refs):
    blocks, out = refs[:-1], refs[-1]
    for c in range(CLUS_DEV):
        gather_group(blocks, c, out.at[c], lax.axis_index("clus"))


def own_late(cuts, bits, received, first, second, before, unfilled, cat, best):
    me = lax.axis_index("clus")
    size = second.shape[1]
    swapped = (me & (bits[-1] // 2)) != 0
    for half, swap in ((first, swapped), (second, jnp.logical_not(swapped))):
        rows = pl.ds(pl.multiple_of(jnp.where(swap, size, 0), size), size)
        for c in range(CLUS_DEV):
            cat[c, rows, :] = half[c, :size, :]
    core = lax.axis_index("blk")
    spans = list(zip(cuts, cuts[1:]))
    last = len(spans) - 1
    start = spans[last][0]
    best[:, :start] = before[:, :start]
    bests = [[best.at[c : c + 1, a:b] for a, b in spans] for c in range(CLUS_DEV)]
    groups = [
        [received.at[core, c, a:b] for a, b in spans[:-1]] + [cat.at[c]] for c in range(CLUS_DEV)
    ]
    for c in range(CLUS_DEV):
        bests[c][last][...] = fresh_best(cat.at[c])
        raise_best(bests[c][last], cat.at[c], cat.at[c], True)
    for i in range(last):
        score_pairs(bests, groups, last, i, bits[i], me)

    @pl.when(core == 1)
    def _():
        for c in range(CLUS_DEV):
            raise_wide(bests[c][last], received.at[0, c], cat.at[c], unfilled[c : c + 1, :])


def cross_late(cuts, per, received, cat, before, first, second, out, best, keys):
    me = lax.axis_index("clus")
    core = lax.axis_index("blk")
    spans = list(zip(cuts, cuts[1:]))
    best[...] = before[...]

    @pl.when(core == 1)
    def _():
        start = spans[-1][0]
        size = second.shape[1]
        for c in range(CLUS_DEV):
            keys[c, :size, :] = first[c, :size, :]
            keys[c, size:, :] = second[c]
            fresh = best.at[c : c + 1, start:]
            raise_best(best.at[c : c + 1, :start], keys.at[c], received.at[1, c])
            raise_best(fresh, keys.at[c], cat.at[c])

    for a, b in spans:
        place = (me ^ (a // per)) & ~((b - a) // per - 1)
        value = best[:, a:b]
        at = pl.ds(pl.multiple_of(place * per, LANES), b - a)
        out[:, at] = jnp.where(value > 0.5 * UNFILLED, F32(0.0), value)


def local(embeddings, cluster_ids):
    owners = lax.axis_size("clus")
    clusters = CLUS_DEV * owners
    rows, width = embeddings.shape
    per = 2 * rows // clusters
    bits = [owners // 2, owners // 4]
    bounds = [0, owners // 2, owners // 2 + owners // 4, owners]
    cuts = [x * per for x in bounds]
    near, far, late = [list(range(a, b)) for a, b in zip(bounds, bounds[1:])]
    best_shape = jax.ShapeDtypeStruct((CLUS_DEV, rows), F32)

    def to_owner(block, step):
        return lax.ppermute(block, "clus", [(i, i ^ step) for i in range(owners)])

    def stage_shape(sources):
        return jax.ShapeDtypeStruct((2, CLUS_DEV, sources * per, width), BF)

    def to_both(send):
        return lax.all_to_all(send, "blk", split_axis=0, concat_axis=0, tiled=True)

    arrived = {}
    lead = far[:1]
    unit, tgt, *packed = call_pack_first(embeddings, cluster_ids, lead, clusters, per)
    for steps in (near[1:] + far[1:] + [0], []):
        for step, block in zip(lead, packed):
            arrived[step] = to_owner(block, step) if step else block
        lead, packed = steps, call_pack_rest(unit, tgt, steps, per) if steps else []
    packed = call_pack_rest(unit, tgt, late, per)
    *held, arrived[far[0]] = lax.optimization_barrier((*packed, arrived[far[0]]))
    for step, block in zip(late, held):
        arrived[step] = to_owner(block, step)

    early = near + far
    send, best = kernel_call(
        functools.partial(own_early, cuts[:3], bits),
        [stage_shape(len(early)), best_shape],
        [arrived[s] for s in reversed(early)],
        "own_early",
    )
    received = to_both(send)
    flags = jax.ShapeDtypeStruct((CLUS_DEV, cuts[2]), F32)
    best, unfilled = kernel_call(cross_early, [best_shape, flags], [received, best], "cross_early")
    count = len(late) // 2
    size = count * per
    count = len(late) // 2
    size = count * per
    halves, others = [], []
    for steps, spare in ((late[:count], size // 2), (late[count:], 0)):
        *new, best = lax.optimization_barrier((*[arrived[s] for s in steps], best))
        half_shape = jax.ShapeDtypeStruct((CLUS_DEV, size + spare, width), BF)
        (half,) = kernel_call(gather_late, [half_shape], new, "gather_late")
        others.append(lax.ppermute(half, "blk", [(0, 1)]))
        half, best = lax.optimization_barrier((half, best))
        halves.append(half)
    cat_shape = jax.ShapeDtypeStruct((CLUS_DEV, 2 * size, width), BF)
    cat, best = kernel_call(
        functools.partial(own_late, cuts, bits),
        [cat_shape, best_shape],
        [received] + halves + [best, unfilled],
        "own_late",
    )
    (out,) = kernel_call(
        functools.partial(cross_late, cuts, per),
        [best_shape],
        [received, cat, best] + others,
        "cross_late",
        [pltpu.VMEM((CLUS_DEV, rows), F32), pltpu.VMEM(cat_shape.shape, BF)],
    )
    return out


def solution(mesh):
    placed = (P(("groups", "clus", "blk"), None), P(("groups", "clus", "blk"), None))
    return jax.shard_map(
        local, mesh=mesh, in_specs=placed, out_specs=P(("groups", "clus"), "blk"), check_vma=False
    )
```

```python
import functools

import jax
import jax.numpy as jnp
from jax import lax
from jax.experimental import pallas as pl
from jax.experimental.pallas import tpu as pltpu
from jax.sharding import PartitionSpec as P

CLUS_DEV = 2
LANES = 128
MARK = 2.0
UNFILLED = 8.0
BF = jnp.bfloat16
F32 = jnp.float32


def iota(shape, dim):
    return lax.broadcasted_iota(jnp.int32, shape, dim)


def matmul(a, b, contract):
    return lax.dot_general(a, b, (contract, ((), ())), preferred_element_type=F32)


def targets(ids, clusters, per_source):
    groups = ids.shape[1] // LANES
    parts = [ids[:, g * LANES : (g + 1) * LANES] for g in range(groups)]
    hot = jnp.concatenate(
        [(iota((clusters, LANES), 0) == part).astype(F32) for part in parts], axis=0
    )
    stacked = groups * clusters
    earlier = (iota((LANES, LANES), 0) < iota((LANES, LANES), 1)).astype(F32).astype(BF)
    within = matmul(hot.astype(BF), earlier, ((1,), (0,)))
    totals = jnp.broadcast_to(jnp.sum(hot, axis=1, keepdims=True), (stacked, LANES))
    a, b = iota((stacked, stacked), 0), iota((stacked, stacked), 1)
    chunks_before = ((a % clusters == b % clusters) & (b < a)).astype(F32).astype(BF)
    before = within + matmul(chunks_before, totals.astype(BF), ((1,), (0,)))
    picked = hot * before
    out = [
        jnp.sum(picked[g * clusters : (g + 1) * clusters], axis=0, keepdims=True).astype(jnp.int32)
        + parts[g] * per_source
        for g in range(groups)
    ]
    return jnp.concatenate(out, axis=1)


def pack_block(unit, tgt, dest, width):
    hit = (tgt - dest * width) == iota((width, tgt.shape[1]), 0)
    hot = hit.astype(F32)
    rows = matmul(hot.astype(BF), unit, ((1,), (0,)))
    empty = jnp.max(hot, axis=1, keepdims=True) < 0.5
    head = jnp.where(empty, F32(MARK), rows[:, :LANES])
    return head.astype(BF), rows[:, LANES:].astype(BF)


def store_blocks(unit, tgt, steps, width, outs):
    me = lax.axis_index("clus")
    for step, out in zip(steps, outs):
        head, tail = pack_block(unit, tgt, me ^ step, width)
        out[:, :LANES] = head
        out[:, LANES:] = tail


PIECES = 8


def pack_first(steps, clusters, per_source, emb, ids, unit, tgt, *refs):
    outs, (raw, sems) = refs[:-2], refs[-2:]
    size = emb.shape[0] // PIECES
    windows = [pl.ds(piece * size, size) for piece in range(PIECES)]
    copies = [
        pltpu.make_async_copy(emb.at[window], raw.at[window], sems.at[piece])
        for piece, window in enumerate(windows)
    ]
    for copy in copies:
        copy.start()
    tgt[...] = targets(ids[...], clusters, per_source)
    for copy, window in zip(copies, windows):
        copy.wait()
        values = raw[window, :].astype(F32)
        scale = lax.rsqrt(jnp.sum(values * values, axis=1, keepdims=True) + 1e-6)
        unit[window, :] = (values * scale).astype(BF)
    store_blocks(unit[...], tgt[...], steps, CLUS_DEV * per_source, outs)


def pack_rest(steps, per_source, unit, tgt, *outs):
    store_blocks(unit[...], tgt[...], steps, CLUS_DEV * per_source, outs)


VMEM = pl.BlockSpec(memory_space=pltpu.VMEM)


def kernel_call(kernel, shapes, inputs, name, scratch=(), places=None, grant=20 * 2**20):
    return pl.pallas_call(
        kernel,
        out_shape=shapes,
        in_specs=places or [VMEM] * len(inputs),
        out_specs=[VMEM] * len(shapes),
        scratch_shapes=scratch,
        compiler_params=pltpu.CompilerParams(vmem_limit_bytes=grant),
        cost_estimate=pl.CostEstimate(flops=1000, bytes_accessed=1000, transcendentals=0),
        name=name,
    )(*inputs)


def call_pack_first(emb, ids, steps, clusters, per_source):
    block = jax.ShapeDtypeStruct((CLUS_DEV * per_source, emb.shape[1]), BF)
    shapes = [jax.ShapeDtypeStruct(emb.shape, BF), jax.ShapeDtypeStruct(ids.shape, jnp.int32)]
    return kernel_call(
        functools.partial(pack_first, steps, clusters, per_source),
        shapes + [block] * len(steps),
        [emb, ids],
        places=[pl.BlockSpec(memory_space=pl.ANY), VMEM],
        grant=50 * 2**20,
        name="pack_first",
        scratch=[
            pltpu.VMEM(emb.shape, BF),
            pltpu.SemaphoreType.DMA((PIECES,)),
        ],
    )


def call_pack_rest(unit, tgt, steps, per_source):
    block = jax.ShapeDtypeStruct((CLUS_DEV * per_source, unit.shape[1]), BF)
    return kernel_call(
        functools.partial(pack_rest, steps, per_source),
        [block] * len(steps),
        [unit, tgt],
        "pack_rest",
    )


CHUNK = 256


def raise_best(best, keys, queries, triangular=False):
    rows = queries.shape[0]
    chunk = min(CHUNK, rows) if triangular else rows
    for start in range(0, rows, chunk):
        count = start + chunk if triangular else keys.shape[0]
        sims = matmul(keys[:count, :], queries[start : start + chunk, :], ((1,), (1,)))
        filled = keys[:count, :LANES].astype(F32) < 1.5
        parts = []
        for first in range(0, chunk, LANES):
            allowed = filled
            if triangular:
                allowed = filled & (
                    iota((count, LANES), 0) < iota((count, LANES), 1) + (start + first)
                )
            part = jnp.where(allowed, sims[:, first : first + LANES], F32(-1.0))
            parts.append(jnp.max(part, axis=0, keepdims=True))
        window = slice(start, start + chunk)
        best[:, window] = jnp.maximum(best[:, window], jnp.concatenate(parts, axis=1))


def gather_group(blocks, cluster, out, me):
    per = blocks[0].shape[0] // CLUS_DEV
    for step, block in enumerate(blocks):
        place = (me & (len(blocks) - 1)) ^ step
        rows = pl.ds(pl.multiple_of(place * per, per), per)
        out[rows, :] = block[cluster * per : (cluster + 1) * per, :]


def score_pairs(bests, groups, new, old, bit, me):
    later = (me & bit) == 0

    @pl.when(later)
    def _():
        for best, group in zip(bests, groups):
            raise_best(best[new], group[old], group[new])

    @pl.when(jnp.logical_not(later))
    def _():
        for best, group in zip(bests, groups):
            raise_best(best[old], group[new], group[old])


def fresh_best(rows):
    ones = jnp.ones((8, LANES), BF)
    heads = matmul(ones, rows[:, :LANES], ((1,), (1,)))[:1]
    return jnp.where(heads < 100.0, F32(-1.0), F32(UNFILLED))


def own_early(cuts, bits, *refs):
    blocks, (send, best) = list(reversed(refs[:-2])), refs[-2:]
    per = blocks[0].shape[0] // CLUS_DEV
    me = lax.axis_index("clus")
    spans = list(zip(cuts, cuts[1:]))
    bests = [[best.at[c : c + 1, a:b] for a, b in spans] for c in range(CLUS_DEV)]
    groups = [[send.at[1, c, a:b] for a, b in spans] for c in range(CLUS_DEV)]
    for c in range(CLUS_DEV):
        for i, (a, b) in enumerate(spans):
            gather_group(blocks[a // per : b // per], c, groups[c][i], me)
            bests[c][i][...] = fresh_best(groups[c][i])
            raise_best(bests[c][i], groups[c][i], groups[c][i], True)
        send[0, c] = send[1, c]
    score_pairs(bests, groups, 1, 0, bits[0], me)


def cross_early(received, before, best):
    best[...] = before[...]

    @pl.when(lax.axis_index("blk") == 1)
    def _():
        for c in range(CLUS_DEV):
            raise_best(best.at[c : c + 1, : received.shape[2]], received.at[0, c], received.at[1, c])


def gather_late(*refs):
    blocks, out = refs[:-1], refs[-1]
    for c in range(CLUS_DEV):
        gather_group(blocks, c, out.at[c], lax.axis_index("clus"))


def own_late(cuts, bits, received, cat, before, best):
    me = lax.axis_index("clus")
    core = lax.axis_index("blk")
    spans = list(zip(cuts, cuts[1:]))
    last = len(spans) - 1
    start = spans[last][0]
    best[:, :start] = before[:, :start]
    bests = [[best.at[c : c + 1, a:b] for a, b in spans] for c in range(CLUS_DEV)]
    groups = [
        [received.at[core, c, a:b] for a, b in spans[:-1]] + [cat.at[c]] for c in range(CLUS_DEV)
    ]
    for c in range(CLUS_DEV):
        bests[c][last][...] = fresh_best(cat.at[c])
        raise_best(bests[c][last], cat.at[c], cat.at[c], True)
    for i in range(last):
        score_pairs(bests, groups, last, i, bits[i], me)

    @pl.when(core == 1)
    def _():
        for c in range(CLUS_DEV):
            raise_best(bests[c][last], received.at[0, c], cat.at[c])


def cross_late(cuts, per, received, cat, before, other, out, best):
    me = lax.axis_index("clus")
    core = lax.axis_index("blk")
    spans = list(zip(cuts, cuts[1:]))
    best[...] = before[...]

    @pl.when(core == 1)
    def _():
        start = spans[-1][0]
        for c in range(CLUS_DEV):
            fresh = best.at[c : c + 1, start:]
            raise_best(best.at[c : c + 1, :start], other.at[c], received.at[1, c])
            raise_best(fresh, other.at[c], cat.at[c])

    for a, b in spans:
        place = (me ^ (a // per)) & ~((b - a) // per - 1)
        value = best[:, a:b]
        at = pl.ds(pl.multiple_of(place * per, LANES), b - a)
        out[:, at] = jnp.where(value > 0.5 * UNFILLED, F32(0.0), value)


def local(embeddings, cluster_ids):
    owners = lax.axis_size("clus")
    clusters = CLUS_DEV * owners
    rows, width = embeddings.shape
    per = 2 * rows // clusters
    bits = [owners // 2, owners // 4]
    bounds = [0, owners // 2, owners // 2 + owners // 4, owners]
    cuts = [x * per for x in bounds]
    near, far, late = [list(range(a, b)) for a, b in zip(bounds, bounds[1:])]
    best_shape = jax.ShapeDtypeStruct((CLUS_DEV, rows), F32)

    def to_owner(block, step):
        return lax.ppermute(block, "clus", [(i, i ^ step) for i in range(owners)])

    def stage_shape(sources):
        return jax.ShapeDtypeStruct((2, CLUS_DEV, sources * per, width), BF)

    def to_both(send):
        return lax.all_to_all(send, "blk", split_axis=0, concat_axis=0, tiled=True)

    arrived = {}
    lead = far[:1]
    unit, tgt, *packed = call_pack_first(embeddings, cluster_ids, lead, clusters, per)
    for steps in (near[1:] + far[1:] + [0], []):
        for step, block in zip(lead, packed):
            arrived[step] = to_owner(block, step) if step else block
        lead, packed = steps, call_pack_rest(unit, tgt, steps, per) if steps else []
    packed = call_pack_rest(unit, tgt, late, per)
    *held, arrived[far[0]] = lax.optimization_barrier((*packed, arrived[far[0]]))
    for step, block in zip(late, held):
        arrived[step] = to_owner(block, step)

    early = near + far
    send, best = kernel_call(
        functools.partial(own_early, cuts[:3], bits),
        [stage_shape(len(early)), best_shape],
        [arrived[s] for s in reversed(early)],
        "own_early",
    )
    received = to_both(send)
    (best,) = kernel_call(cross_early, [best_shape], [received, best], "cross_early")
    *new, best = lax.optimization_barrier((*[arrived[s] for s in late], best))
    cat_shape = jax.ShapeDtypeStruct((CLUS_DEV, len(late) * per, width), BF)
    (cat,) = kernel_call(gather_late, [cat_shape], new, "gather_late")
    other = lax.ppermute(cat, "blk", [(0, 1)])
    (best,) = kernel_call(
        functools.partial(own_late, cuts, bits), [best_shape], [received, cat, best], "own_late"
    )
    (out,) = kernel_call(
        functools.partial(cross_late, cuts, per),
        [best_shape],
        [received, cat, best, other],
        "cross_late",
        [pltpu.VMEM((CLUS_DEV, rows), F32)],
    )
    return out


def solution(mesh):
    placed = (P(("groups", "clus", "blk"), None), P(("groups", "clus", "blk"), None))
    return jax.shard_map(
        local, mesh=mesh, in_specs=placed, out_specs=P(("groups", "clus"), "blk"), check_vma=False
    )
```
